32 devices in a mesh: batch: 4 (over x, core), seq: 8 (over z, y).
Axes of the slice: x: 2, y: 2, z: 4, core: 2. Of those that a mesh axis runs over, the one named last changes fastest.
Arguments:
- block_input: bfloat16 [8, 2048, 2048], P('batch', 'seq'), may hold values from -5.5 to 5.5, as said below
- weight: bfloat16 [2, 2048, 6144], P(None, ('batch', 'seq')), may hold values from -0.125 to 0.125
- vectors: float32 [2, 5, 2048], P(None, None, ('batch', 'seq')), may hold values from -1 to 13, as said below
- cotangent: bfloat16 [8, 2048, 2048], P('batch', 'seq'), may hold values from -5 to 5, as said below
Outputs:
- block_output: bfloat16 [8, 2048, 2048], P('batch', 'seq')
- input_grad: float32 [8, 2048, 2048], P('batch', 'seq')
- weight_grad: float32 [2, 2048, 6144], P(None, ('batch', 'seq'))
- vector_grad: float32 [2, 5, 2048], P(None, None, ('batch', 'seq'))
The draws below stay inside these ranges and needn't reach their ends.
Inputs may be any that keep to these rules, and one draw needn't show every extreme that they name: `block_input`: each sequence has a feature offset common to all its positions. `cotangent`: each sequence has a feature offset common to all its positions. `vectors`: gains near 1; vf, vr, br of order one; bf positive.
All inputs are finite; a program needn't handle non-finite values.
Results may differ from the reference program's by a relative error of at most 0.0044.
Values may be sent and summed in bfloat16 or wider, within the bound.
A program may use at most 256 MiB of HBM per device.

```python
import jax
import jax.numpy as jnp
from jax import lax

D = 2048
LAYERS = 2
LENGTH = 2048
SEQUENCES = 8


def offset_field(key, offset_scale, noise_clip):
    first, second = jax.random.split(key)
    offset = jnp.clip(jax.random.normal(first, (SEQUENCES, 1, D), jnp.float32) * offset_scale * 0.6, -offset_scale, offset_scale)
    noise = jnp.clip(jax.random.normal(second, (SEQUENCES, LENGTH, D), jnp.float32), -noise_clip, noise_clip)
    return offset + noise


def draw_block_input(key, part):
    key = jax.random.fold_in(key, 11)
    return offset_field(key, 1.5, 4.0).astype(jnp.bfloat16)


def draw_cotangent(key, part):
    key = jax.random.fold_in(key, 13)
    return offset_field(key, 1.0, 4.0).astype(jnp.bfloat16)


def draw_vectors(key, part):
    key = jax.random.fold_in(key, 17)
    keys = jax.random.split(key, 5)
    shape = (LAYERS, D)
    norm_scale = 1.0 + jax.random.uniform(keys[0], shape, jnp.float32, -0.25, 0.25)
    vforget = jax.random.uniform(keys[1], shape, jnp.float32, -0.5, 0.5)
    spread = jax.random.uniform(keys[2], shape, jnp.float32, 0.0, 1.0)
    low_end = jnp.log(30.0)
    high_end = jnp.log(2.0 * LENGTH)
    bforget = low_end + spread * (high_end - low_end)
    vreset = jax.random.uniform(keys[3], shape, jnp.float32, -1.0, 1.0)
    breset = jax.random.uniform(keys[4], shape, jnp.float32, -1.0, 1.0)
    return jnp.stack([norm_scale, vforget, bforget, vreset, breset], axis=1).astype(jnp.float32)


def steps_of(key, dims, pieces, least, high):
    loudness, own = 1.0, jax.random.fold_in(key, 6)
    for axis_at, parts in pieces:
        draws = jnp.exp(jax.random.uniform(jax.random.fold_in(own, axis_at), (parts,), jnp.float32, least / len(pieces), high / len(pieces)))
        loudness = loudness * jnp.repeat(draws, dims[axis_at] // parts).reshape([-1 if axis == axis_at else 1 for axis in range(len(dims))])
    return loudness


def centred(stream_key, extent, width, bound, shards=(), dtype=jnp.bfloat16):
    values = width * jax.random.normal(stream_key, extent, jnp.float32)
    if shards:
        values = values * steps_of(stream_key, extent, shards, -0.22, 0.18)
    return jnp.clip(values, -bound, bound).astype(dtype)


def setup_inputs(seed: int = 0) -> dict:
    seeds = jax.random.split(jax.random.key(seed), 5)
    block_input = draw_block_input(jax.random.fold_in(seeds[4], 71), 0)
    weight = centred(seeds[1], (LAYERS, D, 3 * D), D ** -0.5, 0.125, ((1, 32),))
    vectors = draw_vectors(jax.random.fold_in(seeds[4], 71), 0)
    cotangent = draw_cotangent(jax.random.fold_in(seeds[4], 71), 0)
    return {"block_input": block_input, "weight": weight, "vectors": vectors, "cotangent": cotangent}


@jax.custom_vjp
def low(v):
    return lax.optimization_barrier(v.astype(jnp.bfloat16)).astype(jnp.float32)

@jax.custom_vjp
def low_back(v):
    return v

def low_keep(v):
    return (low(v), None)

def low_pass(kept, grad):
    return (grad,)

def back_keep(v):
    return (v, None)

def back_low(kept, grad):
    return (low(grad),)
low.defvjp(low_keep, low_pass)
low_back.defvjp(back_keep, back_low)
epsilon = 1e-05

def one_layer(stream, matrix, vec):
    norm_scale, vforget, bforget, vreset, breset = (vec[0], vec[1], vec[2], vec[3], vec[4])
    hidden_width = stream.shape[-1]
    center = lax.optimization_barrier(jnp.mean(stream, axis=-1, keepdims=True))
    shifted_input = stream - center
    inverse_deviation = lax.rsqrt(lax.optimization_barrier(jnp.mean(shifted_input * shifted_input, axis=-1, keepdims=True)) + epsilon)
    normed_input = low(shifted_input * inverse_deviation * norm_scale)
    mixed = low_back(jnp.dot(normed_input, matrix, precision=lax.Precision.HIGHEST, preferred_element_type=jnp.float32))
    candidate_value = mixed[:, :hidden_width]
    forget_in = mixed[:, hidden_width:2 * hidden_width]
    reset_input = mixed[:, 2 * hidden_width:]
    forget_gate = jax.nn.sigmoid(forget_in + vforget * stream + bforget)

    def advance(cell, inputs):
        forget_t, cand_t, reset_t, row_t = inputs
        reset = jax.nn.sigmoid(reset_t + vreset * cell + breset)
        new_cell = forget_t * cell + (1.0 - forget_t) * cand_t
        return (new_cell, reset * new_cell + (1.0 - reset) * row_t)
    start = jnp.zeros((hidden_width,), jnp.float32)
    last, outputs = lax.scan(jax.checkpoint(advance), start, (forget_gate, candidate_value, reset_input, stream))
    return outputs

def forward(stream, weights, vectors):
    for layer in range(LAYERS):
        stream = one_layer(stream, weights[layer], vectors[layer])
    return stream

def reference(block_input, weight, vectors, cotangent):
    weights = weight.astype(jnp.float32)

    def per_sequence(totals, pair):
        seq_in, seq_cot = pair
        result, pull = jax.vjp(forward, seq_in.astype(jnp.float32), weights, vectors)
        grad_in, grad_w, grad_v = pull(seq_cot.astype(jnp.float32))
        return ((totals[0] + grad_w, totals[1] + grad_v), (result.astype(jnp.bfloat16), grad_in))
    start = (jnp.zeros(weights.shape, jnp.float32), jnp.zeros(vectors.shape, jnp.float32))
    totals, outs = lax.scan(per_sequence, start, (block_input, cotangent))
    return (outs[0], outs[1], totals[0], totals[1])
```

```python
import functools
import jax
import jax.numpy as jnp
from jax import lax
from jax.experimental import pallas as pl
from jax.experimental.pallas import tpu as pltpu
from jax.sharding import PartitionSpec as P

MESH = pl.DeviceIdType.MESH
F32, BF16 = jnp.float32, jnp.bfloat16
epsilon = 1e-05
F = 128
ANY = pl.BlockSpec(memory_space=pl.ANY)
VM = pl.BlockSpec(memory_space=pltpu.VMEM)


def remote(src, dst, ssem, rsem, dev):
    return pltpu.make_async_remote_copy(
        src_ref=src, dst_ref=dst, send_sem=ssem, recv_sem=rsem, device_id=dev, device_id_type=MESH
    )


def arrived(dst, rsem, dev):
    remote(dst, dst, rsem, rsem, dev).wait_recv()


def sent(src, ssem, dev):
    remote(src, src, ssem, ssem, dev).wait_send()


def sigmoid(v):
    return 1.0 / (1.0 + jnp.exp(jnp.minimum(-v, 80.0)))


def seq_rows(t, nseq, steps):
    return pl.ds(t, nseq, stride=steps)


def greet(b, s, nb, ns):
    barrier = pltpu.get_barrier_semaphore()
    for j in range(1, nb):
        pl.semaphore_signal(barrier, inc=1, device_id=(lax.rem(b + j, nb), s), device_id_type=MESH)
    for j in range(1, ns):
        pl.semaphore_signal(barrier, inc=1, device_id=(b, lax.rem(s + j, ns)), device_id_type=MESH)
    pl.semaphore_wait(barrier, nb - 1 + ns - 1)


class Dims:
    def __init__(self, nb, ns, x_shape, w_shape):
        self.nb, self.ns = nb, ns
        self.inner = 2 if ns == 8 else 8
        self.outer = ns // self.inner
        self.sb, self.steps, self.d = x_shape
        self.local = self.sb * self.steps
        self.nseq = self.sb * nb
        self.tok = self.local * nb
        self.q = self.d // nb
        self.nf = self.q // F
        self.layers, self.rows = w_shape[0], w_shape[1]


def layer_norm_rows(x, gain):
    mu = jnp.mean(x, axis=-1, keepdims=True)
    xc = x - mu
    rstd = lax.rsqrt(jnp.mean(xc * xc, axis=-1, keepdims=True) + epsilon)
    return mu, rstd, xc * rstd * gain


def forward_one(
    dm, x_in, w_in, vec_in, cot_in,
    normed_out, wq0_out, wq1_out, cot_out, x1g_out, x1_out, xo_out, f_out, c_out, r_out, cell_out, inc_out, vec_out,
    xg, normed, wq0, vecg, vecf, xo, fS, cS, rS, cellS, x1S, x1b, tot, incS, totS,
    pre_s, pre_r, z_s, z_r, y_s, y_r, vp_s, vp_r, vz_s, vz_r, vy_s, vy_r,
    xx_s, xx_r, xc_s, xc_r, xl_s, xl_r, cot_s, cot_r, t_s, t_r, h_s, h_r, hc_s, hc_r, hl_s, hl_r, loc,
):
    nb, ns, nf, inner, outer = dm.nb, dm.ns, dm.nf, dm.inner, dm.outer
    R = dm.rows
    b, s = lax.axis_index("batch"), lax.axis_index("seq")
    z, y = s // inner, lax.rem(s, inner)
    across, sib, diag = b ^ 2, b ^ 1, b ^ 3
    greet(b, s, nb, ns)
    batch_peers = [lax.rem(b + j, nb) for j in range(1, nb)]
    outer_peers = [lax.rem(z + j, outer) for j in range(1, outer)]
    inner_peers = [lax.rem(y + j, inner) for j in range(1, inner)]
    seq_peers = [lax.rem(s + j, ns) for j in range(1, ns)]
    wq = [wq0, wq1_out]

    def strip(l, fc, pos):
        return wq[l].at[fc, :, pl.ds(pl.multiple_of(pos * R, R), R)]

    def cell_strip(l, fc, bb, pos):
        return wq[l].at[fc, bb, pl.ds(pl.multiple_of(pos * R, R), R)]

    own = []

    def local_copy(src, dst, k):
        c = pltpu.make_async_copy(src, dst, loc.at[k])
        c.start()
        return c

    def pre_start(l, fc):
        for p in batch_peers:
            remote(w_in.at[l, p, fc], cell_strip(l, fc, b, s), pre_s.at[l, fc, p], pre_r.at[l, fc, b], (p, s)).start()

    vecg[b, s] = vec_in[...]
    for p in batch_peers:
        remote(vec_in, vecg.at[b, s], vp_s.at[p], vp_r.at[b], (p, s)).start()
    locals0 = [local_copy(x_in, xg.at[b], 0)]
    for l in range(2):
        for fc in range(nf):
            locals0.append(local_copy(w_in.at[l, b, fc], cell_strip(l, fc, b, s), 1 + l * nf + fc))
    for fc in range(nf):
        pre_start(0, fc)
    NX = 4
    XR = dm.local // NX
    remote(x_in, xg.at[b], xc_s, xc_r, (sib, s)).start()

    def x_send(k):
        rows = pl.ds(k * XR, XR)
        return remote(x_in.at[rows], xg.at[b, rows], xx_s.at[k], xx_r.at[k], (across, s))

    def x_relay(k):
        rows = pl.ds(k * XR, XR)
        return remote(xg.at[across, rows], xg.at[across, rows], xl_s.at[k], xl_r.at[k], (sib, s))

    for k in range(NX):
        x_send(k).start()
    for fc in range(nf):
        pre_start(1, fc)
    for p in batch_peers:
        cols = pl.ds(pl.multiple_of(p * dm.q, F), dm.q)
        remote(cot_in.at[:, cols], cot_out.at[b], cot_s.at[p], cot_r.at[b], (p, s)).start()
    locals0.append(local_copy(cot_in.at[:, pl.ds(pl.multiple_of(b * dm.q, F), dm.q)], cot_out.at[b], 1 + 2 * nf))

    for p in batch_peers:
        arrived(vecg.at[p, s], vp_r.at[p], (p, s))
    for p in outer_peers:
        remote(vecg.at[:, s], vecg.at[:, s], vz_s.at[p], vz_r.at[z], (b, p * inner + y)).start()
    for c in locals0:
        c.wait()

    def z_start(l, fc):
        for p in batch_peers:
            arrived(cell_strip(l, fc, p, s), pre_r.at[l, fc, p], (p, s))
        for p in outer_peers:
            remote(strip(l, fc, s), strip(l, fc, s), z_s.at[l, fc, p], z_r.at[l, fc, z], (b, p * inner + y)).start()
        for p in inner_peers:
            remote(strip(l, fc, s), strip(l, fc, s), y_s.at[l, fc, z, p], y_r.at[l, fc, z, y], (b, z * inner + p)).start()

    def z_forward(l, fc):
        for o in outer_peers:
            arrived(strip(l, fc, o * inner + y), z_r.at[l, fc, o], (b, o * inner + y))
            for p in inner_peers:
                remote(
                    strip(l, fc, o * inner + y), strip(l, fc, o * inner + y),
                    y_s.at[l, fc, o, p], y_r.at[l, fc, o, y], (b, z * inner + p),
                ).start()

    def y_wait(l, fc):
        for o in range(outer):
            for p in inner_peers:
                arrived(strip(l, fc, o * inner + p), y_r.at[l, fc, o, p], (b, z * inner + p))

    z_start(0, 0)
    for p in outer_peers:
        arrived(vecg.at[:, p * inner + y], vz_r.at[p], (b, p * inner + y))
    for o in range(outer):
        for p in inner_peers:
            at = vecg.at[:, o * inner + y]
            remote(at, at, vy_s.at[o, p], vy_r.at[o, y], (b, z * inner + p)).start()
    for fc in range(1, nf):
        z_start(0, fc)
    for o in range(outer):
        for p in inner_peers:
            arrived(vecg.at[:, o * inner + p], vy_r.at[o, p], (b, z * inner + p))
    per = F // R
    for k in range(dm.d // F):
        bb, s0 = (k * per) // ns, (k * per) % ns
        total = vecg[bb, s0]
        for j in range(1, per):
            total = total + vecg[bb, s0 + j]
        vecf[:, k * F : (k + 1) * F] = total
    vec_out[...] = vecf[...]

    TILE = 32

    def norm_block(bb):
        gain = vecf[0:1, :]

        def step(i, carry):
            rows = pl.ds(pl.multiple_of(i * TILE, TILE), TILE)
            x = xg[bb, rows, :].astype(F32)
            _, _, n = layer_norm_rows(x, gain)
            all_rows = pl.ds(pl.multiple_of(bb * dm.local + i * TILE, TILE), TILE)
            normed[all_rows, :] = n.astype(BF16)
            for fc in range(nf):
                cols = pl.ds(pl.multiple_of(b * dm.q + fc * F, F), F)
                xo[fc, all_rows, :] = xg[bb, rows, cols].astype(F32)
            return carry

        lax.fori_loop(0, dm.local // TILE, step, 0)

    norm_block(b)
    arrived(xg.at[sib], xc_r, (sib, s))
    norm_block(sib)
    for k in range(NX):
        arrived(xg.at[across, pl.ds(k * XR, XR)], xx_r.at[k], (across, s))
        x_relay(k).start()
        if k == 1:
            z_forward(0, 0)
    norm_block(across)
    for k in range(NX):
        arrived(xg.at[diag, pl.ds(k * XR, XR)], xl_r.at[k], (sib, s))
    norm_block(diag)
    normed_copy = local_copy(normed, normed_out, 0)

    def vrow(k, fc):
        return vecf[k : k + 1, pl.ds(pl.multiple_of(b * dm.q + fc * F, F), F)]

    def p1(fc):
        y_wait(0, fc)
        vf, bf, br = vrow(1, fc), vrow(2, fc), vrow(4, fc)

        def seq_step(i, carry):
            rows = pl.ds(pl.multiple_of(i * dm.steps, dm.steps), dm.steps)
            m = jnp.dot(normed[rows, :], wq0[fc].reshape(dm.d, 3 * F), preferred_element_type=F32)
            fS[fc, rows, :] = sigmoid(m[:, F : 2 * F] + vf * xo[fc, rows, :] + bf)
            cS[fc, rows, :] = m[:, :F]
            rS[fc, rows, :] = m[:, 2 * F :] + br
            return carry

        lax.fori_loop(0, dm.nseq, seq_step, 0)

        def scan_step(t, carry):
            a, v = carry
            at = seq_rows(t, dm.nseq, dm.steps)
            f, cand = fS[fc, at, :], cS[fc, at, :]
            return a * f, cand + f * (v - cand)

        a, v = lax.fori_loop(
            0, dm.steps, scan_step, (jnp.ones((dm.nseq, F), F32), jnp.zeros((dm.nseq, F), F32)), unroll=8
        )
        totS[fc, 0] = a
        totS[fc, 1] = v
        tot[fc, s] = totS[fc]
        for p in seq_peers:
            remote(totS.at[fc], tot.at[fc, s], t_s.at[fc, p], t_r.at[fc, s], (b, p)).start()

    def p2(fc):
        for p in seq_peers:
            arrived(tot.at[fc, p], t_r.at[fc, p], (b, p))
        vr = vrow(3, fc)

        def fold(j, c):
            return jnp.where(j < s, tot[fc, j, 0] * c + tot[fc, j, 1], c)

        c0 = lax.fori_loop(0, ns, fold, jnp.zeros((dm.nseq, F), F32))
        incS[fc] = c0

        def scan_step(t, prev):
            at = seq_rows(t, dm.nseq, dm.steps)
            f, cand, x = fS[fc, at, :], cS[fc, at, :], xo[fc, at, :]
            r = sigmoid(rS[fc, at, :] + vr * prev)
            c = cand + f * (prev - cand)
            cellS[fc, at, :] = c
            rS[fc, at, :] = r
            x1S[fc, at, :] = x + r * (c - x)
            return c

        lax.fori_loop(0, dm.steps, scan_step, c0, unroll=8)
        x1b[fc] = x1S[fc].astype(BF16)
        remote(x1b.at[fc], x1g_out.at[b, fc], h_s.at[fc], h_r.at[fc], (across, s)).start()
        remote(x1b.at[fc], x1g_out.at[b, fc], hc_s.at[fc], hc_r.at[fc], (sib, s)).start()
        cs = [local_copy(x1b.at[fc], x1g_out.at[b, fc], 2 + fc)]
        for k, (src, dst) in enumerate(
            [(fS, f_out), (cS, c_out), (rS, r_out), (cellS, cell_out), (x1S, x1_out), (xo, xo_out)]
        ):
            cs.append(local_copy(src.at[fc], dst.at[fc], 2 + (k + 1) * nf + fc))
        return cs

    def h_relay(fc):
        arrived(x1g_out.at[across, fc], h_r.at[fc], (across, s))
        remote(x1g_out.at[across, fc], x1g_out.at[across, fc], hl_s.at[fc], hl_r.at[fc], (sib, s)).start()

    pend = []
    for fc in range(1, nf):
        z_forward(0, fc)
        p1(fc - 1)
        if fc >= 2:
            pend += p2(fc - 2)
    for fc in range(nf):
        z_start(1, fc)
    p1(nf - 1)
    pend += p2(nf - 2)
    pend += p2(nf - 1)
    wq_copy = local_copy(wq0, wq0_out, 1)
    for fc in range(nf):
        z_forward(1, fc)
        h_relay(fc)
    inc_out[...] = incS[...]
    for fc in range(nf):
        y_wait(1, fc)
        arrived(x1g_out.at[sib, fc], hc_r.at[fc], (sib, s))
        arrived(x1g_out.at[diag, fc], hl_r.at[fc], (sib, s))
    for p in batch_peers:
        arrived(cot_out.at[p], cot_r.at[p], (p, s))
    for c in pend:
        c.wait()
    normed_copy.wait()
    wq_copy.wait()
    for p in batch_peers:
        sent(vec_in, vp_s.at[p], (p, s))
        sent(cot_out.at[p], cot_s.at[p], (p, s))
        for l in range(2):
            for fc in range(nf):
                sent(w_in.at[l, p, fc], pre_s.at[l, fc, p], (p, s))
    for p in outer_peers:
        sent(vecg.at[:, s], vz_s.at[p], (b, p * inner + y))
        for l in range(2):
            for fc in range(nf):
                sent(strip(l, fc, s), z_s.at[l, fc, p], (b, p * inner + y))
    for p in inner_peers:
        for o in range(outer):
            sent(vecg.at[:, s], vy_s.at[o, p], (b, z * inner + p))
            for l in range(2):
                for fc in range(nf):
                    sent(strip(l, fc, s), y_s.at[l, fc, o, p], (b, z * inner + p))
    sent(x_in, xc_s, (sib, s))
    for k in range(NX):
        x_send(k).wait_send()
        x_relay(k).wait_send()
    for fc in range(nf):
        for p in seq_peers:
            sent(totS.at[fc], t_s.at[fc, p], (b, p))
        sent(x1b.at[fc], h_s.at[fc], (across, s))
        sent(x1b.at[fc], hc_s.at[fc], (sib, s))
        sent(x1b.at[fc], hl_s.at[fc], (sib, s))


def call_forward_one(dm, x, w, vec, cot):
    nb, ns, nf, inner, outer, R = dm.nb, dm.ns, dm.nf, dm.inner, dm.outer, dm.rows
    D, q, tok = dm.d, dm.q, dm.tok
    sd = jax.ShapeDtypeStruct
    chunk = sd((nf, tok, F), F32)
    wshape = (nf, nb, ns * R, 3 * F)
    DMA = pltpu.SemaphoreType.DMA
    V = pltpu.VMEM
    out_shape = [
        sd((tok, D), BF16), sd(wshape, BF16), sd(wshape, BF16), sd((nb, dm.local, q), BF16),
        sd((nb, nf, tok, F), BF16), chunk, chunk, chunk, chunk, chunk, chunk,
        sd((nf, dm.nseq, F), F32), sd((16, D), F32),
    ]
    chunkV = V((nf, tok, F), F32)
    L = 2
    scratch = [
        V((nb, dm.local, D), BF16), V((tok, D), BF16), V(wshape, BF16), V((nb, ns, 16, F), F32), V((16, D), F32),
        chunkV, chunkV, chunkV, chunkV, chunkV, chunkV, V((nf, tok, F), BF16),
        V((nf, ns, 2, dm.nseq, F), F32), V((nf, dm.nseq, F), F32), V((nf, 2, dm.nseq, F), F32),
        DMA((L, nf, nb)), DMA((L, nf, nb)), DMA((L, nf, outer)), DMA((L, nf, outer)),
        DMA((L, nf, outer, inner)), DMA((L, nf, outer, inner)),
        DMA((nb,)), DMA((nb,)), DMA((outer,)), DMA((outer,)), DMA((outer, inner)), DMA((outer, inner)),
        DMA((4,)), DMA((4,)), DMA, DMA, DMA((4,)), DMA((4,)), DMA((nb,)), DMA((nb,)),
        DMA((nf, ns)), DMA((nf, ns)), DMA((nf,)), DMA((nf,)), DMA((nf,)), DMA((nf,)), DMA((nf,)), DMA((nf,)),
        DMA((2 + 8 * nf,)),
    ]
    return pl.pallas_call(
        functools.partial(forward_one, dm),
        out_shape=out_shape,
        in_specs=[ANY, ANY, VM, ANY],
        out_specs=[ANY] * 11 + [VM, VM],
        scratch_shapes=scratch,
        compiler_params=pltpu.CompilerParams(collective_id=0, has_side_effects=True, vmem_limit_bytes=62 * 2**20),
        name="forward_one",
    )(x, w, vec, cot)


def prepare(dm, block_input, weight, vectors, cotangent):
    D, q, nf, nb, R = dm.d, dm.q, dm.nf, dm.nb, dm.rows
    x = block_input.reshape(dm.local, D)
    cot = cotangent.reshape(dm.local, D)
    w = weight.reshape(dm.layers, R, 3, nb, nf, F).transpose(0, 3, 4, 1, 2, 5).reshape(dm.layers, nb, nf, R, 3 * F)
    s = lax.axis_index("seq")
    v = jnp.pad(vectors.reshape(dm.layers * 5, R), ((0, 16 - dm.layers * 5), (0, 0)))
    lane = lax.broadcasted_iota(jnp.int32, (16, F), 1) // R
    v = jnp.where(lane == lax.rem(s, F // R), jnp.tile(v, (1, F // R)), 0.0)
    return x, w, v, cot


def prefix(value, axis, join, neutral, backward):
    count, mine = (lax.axis_size(axis), lax.axis_index(axis))
    pieces = jax.tree.map(lambda part: lax.all_gather(part, axis), value)
    if backward:
        pieces = jax.tree.map(lambda part: part[::-1], pieces)
        mine = count - 1 - mine
    subtotal = jax.tree.map(
        lambda part, zero: jnp.full_like(part, 0) + jnp.asarray(zero, part.dtype), value, neutral
    )

    def step(position, subtotal):
        longer = join(subtotal, jax.tree.map(lambda part: part[position], pieces))
        return jax.tree.map(lambda new, old: jnp.where(position < mine, new, old), longer, subtotal)

    return lax.fori_loop(0, count - 1, step, subtotal)


def compose(earlier, later):
    return (later[0] * earlier[0], later[0] * earlier[1] + later[1])


def rebuild_forward(stream, full, vec):
    norm_scale, vforget, bforget = (vec[0], vec[1], vec[2])
    sequence_batch, time_steps, hidden_width = stream.shape
    center = jnp.mean(stream, axis=-1, keepdims=True)
    shifted_input = stream - center
    inverse_deviation = lax.rsqrt(
        jnp.mean(shifted_input * shifted_input, axis=-1, keepdims=True) + epsilon
    )
    centered_input = shifted_input * inverse_deviation
    normed_input = (
        (centered_input * norm_scale)
        .astype(jnp.bfloat16)
        .reshape(sequence_batch * time_steps, hidden_width)
    )
    mixed = jnp.dot(normed_input, full, preferred_element_type=jnp.float32).reshape(
        sequence_batch, time_steps, 3 * hidden_width
    )
    candidate_value = mixed[..., :hidden_width]
    reset_input = mixed[..., 2 * hidden_width :]
    forget_gate = jax.nn.sigmoid(
        mixed[..., hidden_width : 2 * hidden_width] + vforget * stream + bforget
    )
    gate_values, norm_bias = lax.associative_scan(
        compose, (forget_gate, (1.0 - forget_gate) * candidate_value), axis=1
    )
    return (
        centered_input,
        inverse_deviation,
        normed_input,
        candidate_value,
        reset_input,
        forget_gate,
        gate_values,
        norm_bias,
    )


def finish(vec, reset_input, gate_values, norm_bias, incoming):
    vreset, breset = (vec[3], vec[4])
    cells = gate_values * incoming[:, None, :] + norm_bias
    previous = jnp.concatenate([incoming[:, None, :], cells[:, :-1]], axis=1)
    reset = jax.nn.sigmoid(reset_input + vreset * previous + breset)
    return (cells, previous, reset)


def general_body(block_input, weight, vectors, cotangent):
    sequence_batch, time_steps, hidden_width = block_input.shape
    layers = weight.shape[0]
    params = lax.all_gather(vectors, ("batch", "seq"), axis=2, tiled=True)
    stream = block_input.astype(jnp.float32)
    ones = jnp.ones((sequence_batch, hidden_width), jnp.float32)
    zeros = jnp.zeros((sequence_batch, hidden_width), jnp.float32)
    inputs = []
    entering = []
    for layer in range(layers):
        full = lax.all_gather(weight[layer], ("batch", "seq"), axis=0, tiled=True)
        vec = params[layer]
        pieces = rebuild_forward(stream, full, vec)
        gate_values, norm_bias = (pieces[6], pieces[7])
        arrived = prefix(
            (gate_values[:, -1], norm_bias[:, -1]), "seq", compose, (ones, zeros), False
        )
        incoming = arrived[1]
        cells, previous, reset = finish(vec, pieces[4], gate_values, norm_bias, incoming)
        inputs.append(stream)
        entering.append(incoming)
        stream = reset * cells + (1.0 - reset) * stream
    block_output = stream.astype(jnp.bfloat16)
    grad_out = cotangent.astype(jnp.float32)
    weight_grads = [None] * layers
    vector_terms = [None] * layers
    rows = weight.shape[1]
    for layer in reversed(range(layers)):
        full = lax.all_gather(weight[layer], ("batch", "seq"), axis=0, tiled=True)
        vec = params[layer]
        norm_scale, vforget, vreset = (vec[0], vec[1], vec[3])
        stream = inputs[layer]
        (
            centered_input,
            inverse_deviation,
            normed_input,
            candidate_value,
            reset_input,
            forget_gate,
            gate_values,
            norm_bias,
        ) = rebuild_forward(stream, full, vec)
        cells, previous, reset = finish(vec, reset_input, gate_values, norm_bias, entering[layer])
        dreset = grad_out * (cells - stream) * reset * (1.0 - reset)
        direct = grad_out * reset
        inject = forget_gate * direct + dreset * vreset
        back_gates, back_offsets = lax.associative_scan(
            compose, (jnp.flip(forget_gate, 1), jnp.flip(inject, 1)), axis=1
        )
        back_gates = jnp.flip(back_gates, 1)
        back_offsets = jnp.flip(back_offsets, 1)
        arrived = prefix(
            (back_gates[:, 0], back_offsets[:, 0]), "seq", compose, (ones, zeros), True
        )
        later = arrived[1]
        carried = back_gates * later[:, None, :] + back_offsets
        following = jnp.concatenate([carried[:, 1:], later[:, None, :]], axis=1)
        dcell = direct + following
        dcandidate = dcell * (1.0 - forget_gate)
        dforget = dcell * (previous - candidate_value) * forget_gate * (1.0 - forget_gate)
        dmixed = jnp.concatenate([dcandidate, dforget, dreset], axis=-1).astype(jnp.bfloat16)
        dmixed = dmixed.reshape(sequence_batch * time_steps, 3 * hidden_width)

        def weight_term(start, count, normed_input=normed_input, dmixed=dmixed):
            return lax.dot_general(
                normed_input, dmixed, (((0,), (0,)), ((), ())), preferred_element_type=jnp.float32
            )

        weight_grads[layer] = lax.psum_scatter(
            weight_term(jnp.int32(0), rows * lax.axis_size(("batch", "seq"))),
            ("batch", "seq"),
            scatter_dimension=0,
            tiled=True,
        )
        normed_gradient = lax.dot_general(
            dmixed, full, (((1,), (1,)), ((), ())), preferred_element_type=jnp.float32
        )
        normed_gradient = normed_gradient.reshape(sequence_batch, time_steps, hidden_width)
        vector_terms[layer] = jnp.stack(
            [
                jnp.sum(normed_gradient * centered_input, axis=(0, 1)),
                jnp.sum(dforget * stream, axis=(0, 1)),
                jnp.sum(dforget, axis=(0, 1)),
                jnp.sum(dreset * previous, axis=(0, 1)),
                jnp.sum(dreset, axis=(0, 1)),
            ],
            axis=0,
        )
        centered_gradient = normed_gradient * norm_scale
        through_norm = inverse_deviation * (
            centered_gradient
            - jnp.mean(centered_gradient, axis=-1, keepdims=True)
            - centered_input * jnp.mean(centered_gradient * centered_input, axis=-1, keepdims=True)
        )
        grad_out = grad_out * (1.0 - reset) + dforget * vforget + through_norm
    weight_grad = jnp.stack(weight_grads, axis=0)
    vector_grad = lax.psum_scatter(
        jnp.stack(vector_terms, axis=0), ("batch", "seq"), scatter_dimension=2, tiled=True
    )
    return (block_output, grad_out, weight_grad, vector_grad)


def tuned_body(nb, ns, block_input, weight, vectors, cotangent):
    sequence_batch, time_steps, hidden_width = block_input.shape
    layers = weight.shape[0]
    params = lax.all_gather(vectors, ("batch", "seq"), axis=2, tiled=True)
    stream = block_input.astype(jnp.float32)
    ones = jnp.ones((sequence_batch, hidden_width), jnp.float32)
    zeros = jnp.zeros((sequence_batch, hidden_width), jnp.float32)
    inputs = []
    entering = []
    dm = Dims(nb, ns, block_input.shape, weight.shape)
    made = call_forward_one(dm, *prepare(dm, block_input, weight, vectors, cotangent))
    mine = made[5].reshape(dm.nf, nb, dm.sb, dm.steps, F).transpose(1, 2, 3, 0, 4).reshape(nb, dm.sb, dm.steps, dm.q)
    mine = lax.all_to_all(mine, "batch", 0, 0, tiled=True)
    entry = lax.all_gather(made[11], "batch", axis=0)
    entry = entry.transpose(2, 0, 1, 3).reshape(dm.nseq, dm.d)
    entry = lax.dynamic_slice_in_dim(entry, lax.axis_index("batch") * dm.sb, dm.sb, 0)
    inputs.append(stream)
    entering.append(entry)
    stream = mine.transpose(1, 2, 0, 3).reshape(stream.shape)
    for layer in range(1, layers):
        full = lax.all_gather(weight[layer], ("batch", "seq"), axis=0, tiled=True)
        vec = params[layer]
        pieces = rebuild_forward(stream, full, vec)
        gate_values, norm_bias = (pieces[6], pieces[7])
        arrived = prefix(
            (gate_values[:, -1], norm_bias[:, -1]), "seq", compose, (ones, zeros), False
        )
        incoming = arrived[1]
        cells, previous, reset = finish(vec, pieces[4], gate_values, norm_bias, incoming)
        inputs.append(stream)
        entering.append(incoming)
        stream = reset * cells + (1.0 - reset) * stream
    block_output = stream.astype(jnp.bfloat16)
    grad_out = cotangent.astype(jnp.float32)
    weight_grads = [None] * layers
    vector_terms = [None] * layers
    rows = weight.shape[1]
    for layer in reversed(range(layers)):
        full = lax.all_gather(weight[layer], ("batch", "seq"), axis=0, tiled=True)
        vec = params[layer]
        norm_scale, vforget, vreset = (vec[0], vec[1], vec[3])
        stream = inputs[layer]
        (
            centered_input,
            inverse_deviation,
            normed_input,
            candidate_value,
            reset_input,
            forget_gate,
            gate_values,
            norm_bias,
        ) = rebuild_forward(stream, full, vec)
        cells, previous, reset = finish(vec, reset_input, gate_values, norm_bias, entering[layer])
        dreset = grad_out * (cells - stream) * reset * (1.0 - reset)
        direct = grad_out * reset
        inject = forget_gate * direct + dreset * vreset
        back_gates, back_offsets = lax.associative_scan(
            compose, (jnp.flip(forget_gate, 1), jnp.flip(inject, 1)), axis=1
        )
        back_gates = jnp.flip(back_gates, 1)
        back_offsets = jnp.flip(back_offsets, 1)
        arrived = prefix(
            (back_gates[:, 0], back_offsets[:, 0]), "seq", compose, (ones, zeros), True
        )
        later = arrived[1]
        carried = back_gates * later[:, None, :] + back_offsets
        following = jnp.concatenate([carried[:, 1:], later[:, None, :]], axis=1)
        dcell = direct + following
        dcandidate = dcell * (1.0 - forget_gate)
        dforget = dcell * (previous - candidate_value) * forget_gate * (1.0 - forget_gate)
        dmixed = jnp.concatenate([dcandidate, dforget, dreset], axis=-1).astype(jnp.bfloat16)
        dmixed = dmixed.reshape(sequence_batch * time_steps, 3 * hidden_width)

        def weight_term(start, count, normed_input=normed_input, dmixed=dmixed):
            return lax.dot_general(
                normed_input, dmixed, (((0,), (0,)), ((), ())), preferred_element_type=jnp.float32
            )

        weight_grads[layer] = lax.psum_scatter(
            weight_term(jnp.int32(0), rows * lax.axis_size(("batch", "seq"))),
            ("batch", "seq"),
            scatter_dimension=0,
            tiled=True,
        )
        normed_gradient = lax.dot_general(
            dmixed, full, (((1,), (1,)), ((), ())), preferred_element_type=jnp.float32
        )
        normed_gradient = normed_gradient.reshape(sequence_batch, time_steps, hidden_width)
        vector_terms[layer] = jnp.stack(
            [
                jnp.sum(normed_gradient * centered_input, axis=(0, 1)),
                jnp.sum(dforget * stream, axis=(0, 1)),
                jnp.sum(dforget, axis=(0, 1)),
                jnp.sum(dreset * previous, axis=(0, 1)),
                jnp.sum(dreset, axis=(0, 1)),
            ],
            axis=0,
        )
        centered_gradient = normed_gradient * norm_scale
        through_norm = inverse_deviation * (
            centered_gradient
            - jnp.mean(centered_gradient, axis=-1, keepdims=True)
            - centered_input * jnp.mean(centered_gradient * centered_input, axis=-1, keepdims=True)
        )
        grad_out = grad_out * (1.0 - reset) + dforget * vforget + through_norm
    weight_grad = jnp.stack(weight_grads, axis=0)
    vector_grad = lax.psum_scatter(
        jnp.stack(vector_terms, axis=0), ("batch", "seq"), scatter_dimension=2, tiled=True
    )
    return (block_output, grad_out, weight_grad, vector_grad)


def solution(mesh):
    nb, ns = mesh.shape["batch"], mesh.shape["seq"]
    body = functools.partial(tuned_body, nb, ns) if (nb, ns) == (4, 8) else general_body
    placed = (
        P("batch", "seq", None),
        P(None, ("batch", "seq"), None),
        P(None, None, ("batch", "seq")),
        P("batch", "seq", None),
    )
    return jax.shard_map(
        body,
        mesh=mesh,
        in_specs=placed,
        out_specs=(
            P("batch", "seq", None),
            P("batch", "seq", None),
            P(None, ("batch", "seq"), None),
            P(None, None, ("batch", "seq")),
        ),
        check_vma=False,
    )
```

```python
import functools
import types

import jax
import jax.numpy as jnp
from jax import lax
from jax.experimental import pallas as pl
from jax.experimental.pallas import tpu as pltpu
from jax.sharding import PartitionSpec as P

MESH = pl.DeviceIdType.MESH
F32, BF16 = jnp.float32, jnp.bfloat16
V, DMA = pltpu.VMEM, pltpu.SemaphoreType.DMA
epsilon = 1e-05
F = 128
G3 = 3 * F
HBM = pl.BlockSpec(memory_space=pl.ANY)
INV = pl.BlockSpec(memory_space=pltpu.VMEM)


class Dims:
    def __init__(self, nb, ns, x_shape, w_shape):
        self.nb, self.ns = nb, ns
        self.inner = 2
        self.outer = ns // 2
        self.sb, self.steps, self.d = x_shape
        self.local = self.sb * self.steps
        self.nseq = self.sb * nb
        self.tok = self.local * nb
        self.q = self.d // nb
        self.nf = self.q // F
        self.cols = 3 * self.q
        self.layers, self.rows = w_shape[0], w_shape[1]


class Net:
    def __init__(self, dm):
        nb, ns, inner, outer = dm.nb, dm.ns, dm.inner, dm.outer
        self.b, self.s = lax.axis_index("batch"), lax.axis_index("seq")
        b, s = self.b, self.s
        self.z, self.y = s // inner, lax.rem(s, inner)
        self.across, self.sib, self.diag = b ^ 2, b ^ 1, b ^ 3
        self.batch_peers = [lax.rem(b + j, nb) for j in range(1, nb)]
        self.outer_peers = [lax.rem(self.z + j, outer) for j in range(1, outer)]
        self.inner_peers = [lax.rem(self.y + j, inner) for j in range(1, inner)]
        self.seq_peers = [lax.rem(s + j, ns) for j in range(1, ns)]
        barrier = pltpu.get_barrier_semaphore()
        for p in self.batch_peers:
            pl.semaphore_signal(barrier, inc=1, device_id=(p, s), device_id_type=MESH)
        for p in self.seq_peers:
            pl.semaphore_signal(barrier, inc=1, device_id=(b, p), device_id_type=MESH)
        pl.semaphore_wait(barrier, nb - 1 + ns - 1)


def remote(src, dst, ssem, rsem, dev):
    return pltpu.make_async_remote_copy(
        src_ref=src, dst_ref=dst, send_sem=ssem, recv_sem=rsem, device_id=dev, device_id_type=MESH
    )


def arrived(dst, rsem, dev):
    remote(dst, dst, rsem, rsem, dev).wait_recv()


def sent(src, ssem, dev):
    remote(src, src, ssem, ssem, dev).wait_send()


def local_copy(src, dst, sem):
    c = pltpu.make_async_copy(src, dst, sem)
    c.start()
    return c


def at128(v):
    return pl.multiple_of(v, F)


def sigmoid(v):
    return 1.0 / (1.0 + jnp.exp(jnp.minimum(-v, 80.0)))


def launch(dm, name, cid, kernel, ins, outs, scratch):
    names = list(ins) + list(outs) + list(scratch)

    def run(*refs):
        kernel(dm, types.SimpleNamespace(**dict(zip(names, refs))))

    got = pl.pallas_call(
        run,
        out_shape=[jax.ShapeDtypeStruct(shape, dtype) for shape, dtype, _ in outs.values()],
        in_specs=[spec for _, spec in ins.values()],
        out_specs=[spec for _, _, spec in outs.values()],
        scratch_shapes=list(scratch.values()),
        compiler_params=pltpu.CompilerParams(collective_id=cid, has_side_effects=True, vmem_limit_bytes=63 * 2**20),
        name=name,
    )(*[array for array, _ in ins.values()])
    return types.SimpleNamespace(**dict(zip(outs, got)))


def norm_rows(x, gain):
    mu = jnp.mean(x, axis=-1, keepdims=True)
    xc = x - mu
    rstd = lax.rsqrt(jnp.mean(xc * xc, axis=-1, keepdims=True) + epsilon)
    return mu, rstd, (xc * rstd * gain).astype(BF16)


def vrow(dm, r, n, k, fc):
    return r.vec[k : k + 1, pl.ds(at128(n.b * dm.q + fc * F), F)]


def products(dm, r, n, w, chunks, base):
    lo, hi = chunks[0] * G3, (chunks[-1] + 1) * G3

    def step(i, carry):
        rows = pl.ds(pl.multiple_of(i * dm.steps, dm.steps), dm.steps)
        m = jnp.dot(r.normed[rows, :], w[:, :, lo:hi].reshape(dm.d, hi - lo), preferred_element_type=F32)
        for k, fc in enumerate(chunks):
            o = k * G3
            vf, bf, br = [vrow(dm, r, n, base + j, fc) for j in (1, 2, 4)]
            r.fS[fc, rows, :] = sigmoid(m[:, o + F : o + 2 * F] + vf * r.xS[fc, rows, :] + bf)
            r.cS[fc, rows, :] = m[:, o : o + F]
            r.rS[fc, rows, :] = m[:, o + 2 * F : o + G3] + br
        return carry

    lax.fori_loop(0, dm.nseq, step, 0)


def at_time(dm, t):
    return pl.ds(t, dm.nseq, stride=dm.steps)


def scan_totals(dm, r, n, fc):
    def step(t, carry):
        a, v = carry
        at = at_time(dm, t)
        f, cand = r.fS[fc, at, :], r.cS[fc, at, :]
        return a * f, cand + f * (v - cand)

    one, zero = jnp.ones((dm.nseq, F), F32), jnp.zeros((dm.nseq, F), F32)
    a, v = lax.fori_loop(0, dm.steps, step, (one, zero), unroll=8)
    r.totS[fc, 0] = a
    r.totS[fc, 1] = v
    r.tot[fc, n.s, 0] = a
    r.tot[fc, n.s, 1] = v
    for p in n.seq_peers:
        remote(r.totS.at[fc], r.tot.at[fc, n.s], r.t_s.at[fc, p], r.t_r.at[fc, n.s], (n.b, p)).start()


def scan_finish(dm, r, n, fc, base):
    for p in n.seq_peers:
        arrived(r.tot.at[fc, p], r.t_r.at[fc, p], (n.b, p))
    vr = vrow(dm, r, n, base + 3, fc)

    def fold(j, c):
        return jnp.where(j < n.s, r.tot[fc, j, 0] * c + r.tot[fc, j, 1], c)

    entering = lax.fori_loop(0, dm.ns, fold, jnp.zeros((dm.nseq, F), F32))
    r.incS[fc] = entering

    def step(t, prev):
        at = at_time(dm, t)
        f, cand, x = r.fS[fc, at, :], r.cS[fc, at, :], r.xS[fc, at, :]
        reset = sigmoid(r.rS[fc, at, :] + vr * prev)
        c = cand + f * (prev - cand)
        r.cellS[fc, at, :] = c
        r.rS[fc, at, :] = reset
        r.hS[fc, at, :] = x + reset * (c - x)
        return c

    lax.fori_loop(0, dm.steps, step, entering, unroll=8)


def totals_sent(dm, r, n):
    for fc in range(dm.nf):
        for p in n.seq_peers:
            sent(r.totS.at[fc], r.t_s.at[fc, p], (n.b, p))


def back_totals(dm, r, n, fc, base):
    vr = vrow(dm, r, n, base + 3, fc)

    def step(i, carry):
        at = at_time(dm, dm.steps - 1 - i)
        reset, dh = r.rS[fc, at, :], r.dhS[fc, at, :]
        direct = dh * reset
        dreset = (r.cellS[fc, at, :] - r.xS[fc, at, :]) * direct * (1.0 - reset)
        r.rS[fc, at, :] = direct
        r.drS[fc, at, :] = dreset
        return r.fS[fc, at, :] * (direct + carry) + dreset * vr

    v = lax.fori_loop(0, dm.steps, step, jnp.zeros((dm.nseq, F), F32), unroll=8)
    r.bkS[fc] = v
    r.bk[fc, n.s] = v
    for p in n.seq_peers:
        remote(r.bkS.at[fc], r.bk.at[fc, n.s], r.k_s.at[fc, p], r.k_r.at[fc, n.s], (n.b, p)).start()


def back_finish(dm, r, n, fc, base):
    for p in n.seq_peers:
        arrived(r.bk.at[fc, p], r.k_r.at[fc, p], (n.b, p))
    vf, vr = vrow(dm, r, n, base + 1, fc), vrow(dm, r, n, base + 3, fc)

    def fold(i, c):
        j = dm.ns - 1 - i
        return jnp.where(j > n.s, r.tot[fc, j, 0] * c + r.bk[fc, j], c)

    zero = jnp.zeros((dm.nseq, F), F32)
    carry = lax.fori_loop(0, dm.ns, fold, zero)

    def one(at, prev, state):
        carry, s1, s2, s3, s4 = state
        f, cand, x = r.fS[fc, at, :], r.cS[fc, at, :], r.xS[fc, at, :]
        direct, dreset = r.rS[fc, at, :], r.drS[fc, at, :]
        dcell = direct + carry
        dcand = dcell * (1.0 - f)
        dforget = dcand * f * (prev - cand)
        r.cS[fc, at, :] = dcand
        r.fS[fc, at, :] = dforget
        r.rS[fc, at, :] = r.dhS[fc, at, :] - direct + dforget * vf
        return (f * dcell + dreset * vr, s1 + dforget * x, s2 + dforget, s3 + dreset * prev, s4 + dreset)

    def step(i, state):
        t = dm.steps - 1 - i
        return one(at_time(dm, t), r.cellS[fc, at_time(dm, t - 1), :], state)

    state = lax.fori_loop(0, dm.steps - 1, step, (carry, zero, zero, zero, zero), unroll=5)
    state = one(at_time(dm, 0), r.incS[fc], state)
    for k in range(4):
        r.vsum_out[fc, k] = state[k + 1]
    r.dmixed[:, fc * G3 : fc * G3 + F] = r.cS[fc].astype(BF16)
    r.dmixed[:, fc * G3 + F : fc * G3 + 2 * F] = r.fS[fc].astype(BF16)
    r.dmixed[:, fc * G3 + 2 * F : fc * G3 + G3] = r.drS[fc].astype(BF16)


def back_sent(dm, r, n):
    for fc in range(dm.nf):
        for p in n.seq_peers:
            sent(r.bkS.at[fc], r.k_s.at[fc, p], (n.b, p))


def back_outputs(dm, r, fc):
    cols = pl.ds(fc * G3, G3)
    return [
        local_copy(r.dmixed.at[:, cols], r.dmixed_out.at[:, cols], r.out_sem.at[fc, 0]),
        local_copy(r.rS.at[fc], r.dtail_out.at[fc], r.out_sem.at[fc, 1]),
    ]


class Gather:
    def __init__(self, dm, n, r, l, w):
        self.dm, self.n, self.r, self.l, self.w = dm, n, r, l, w

    def strip(self, fc, pos):
        R = self.dm.rows
        return self.w.at[:, pl.ds(pl.multiple_of(pos * R, R), R), pl.ds(fc * G3, G3)]

    def piece(self, fc, b):
        n, R = self.n, self.dm.rows
        return self.w.at[b, pl.ds(pl.multiple_of(n.s * R, R), R), pl.ds(fc * G3, G3)]

    def pre(self, fc):
        n, r, l = self.n, self.r, self.l
        for p in n.batch_peers:
            remote(r.w_in.at[l, p, fc], self.piece(fc, n.b), r.pre_s.at[l, fc, p], r.pre_r.at[l, fc, n.b], (p, n.s)).start()

    def hop(self, fc, src, to):
        n, r, l, dm = self.n, self.r, self.l, self.dm
        at = self.strip(fc, src * dm.inner + n.y)
        side = 1 if to > 0 else 0
        return remote(at, at, r.z_s.at[l, fc, src, side], r.z_r.at[l, fc, src], (n.b, (n.z + to) * dm.inner + n.y))

    def to_inner(self, fc, src):
        n, r, l, dm = self.n, self.r, self.l, self.dm
        at = self.strip(fc, src * dm.inner + n.y)
        return [
            remote(at, at, r.y_s.at[l, fc, src, p], r.y_r.at[l, fc, src, n.y], (n.b, n.z * dm.inner + p))
            for p in n.inner_peers
        ]

    def start(self, fc):
        n, r, l, dm = self.n, self.r, self.l, self.dm
        for p in n.batch_peers:
            arrived(self.piece(fc, p), r.pre_r.at[l, fc, p], (p, n.s))
        pl.when(n.z < dm.outer - 1)(lambda: self.hop(fc, n.z, 1).start())
        pl.when(n.z > 0)(lambda: self.hop(fc, n.z, -1).start())
        for c in self.to_inner(fc, n.z):
            c.start()

    def forward(self, fc):
        n, r, l, dm = self.n, self.r, self.l, self.dm
        for h in range(1, dm.outer):
            for way in (-1, 1):
                src = n.z + way * h
                has = (src >= 0) if way < 0 else (src < dm.outer)
                on = (n.z < dm.outer - 1) if way < 0 else (n.z > 0)

                def take(src=src, on=on, way=way):
                    at = self.strip(fc, src * dm.inner + n.y)
                    arrived(at, r.z_r.at[l, fc, src], (n.b, n.s))
                    pl.when(on)(lambda: self.hop(fc, src, -way).start())
                    for c in self.to_inner(fc, src):
                        c.start()

                pl.when(has)(take)

    def complete(self, fc):
        n, r, l, dm = self.n, self.r, self.l, self.dm
        for o in range(dm.outer):
            for p in n.inner_peers:
                arrived(self.strip(fc, o * dm.inner + p), r.y_r.at[l, fc, o, p], (n.b, n.s))

    def drain(self, fc):
        n, r, l, dm = self.n, self.r, self.l, self.dm
        for p in n.batch_peers:
            sent(r.w_in.at[l, p, fc], r.pre_s.at[l, fc, p], (p, n.s))
        for o in range(dm.outer):
            for p in n.inner_peers:
                sent(self.strip(fc, n.s), r.y_s.at[l, fc, o, p], (n.b, n.s))
            right = jnp.logical_and(o <= n.z, n.z < dm.outer - 1)
            left = jnp.logical_and(o >= n.z, n.z > 0)
            for ok, side in ((right, 1), (left, 0)):
                pl.when(ok)(lambda o=o, side=side: sent(self.strip(fc, n.s), r.z_s.at[l, fc, o, side], (n.b, n.s)))


def kernel_one(dm, r):
    n = Net(dm)
    nb, ns, nf, inner, outer, R = dm.nb, dm.ns, dm.nf, dm.inner, dm.outer, dm.rows
    b, s, z, y = n.b, n.s, n.z, n.y
    w0, w1 = Gather(dm, n, r, 0, r.wq0), Gather(dm, n, r, 1, r.wq1_out)
    NX = 4
    XR = dm.local // NX

    r.vecg[b, s] = r.vec_in[...]
    for p in n.batch_peers:
        remote(r.vec_in, r.vecg.at[b, s], r.vp_s.at[p], r.vp_r.at[b], (p, s)).start()
    first = [local_copy(r.w_in.at[l, b, fc], g.piece(fc, b), r.loc.at[l * nf + fc]) for l, g in ((0, w0), (1, w1)) for fc in range(nf)]
    own_x = local_copy(r.x_in, r.xg.at[b], r.loc.at[2 * nf])
    for fc in range(nf):
        w0.pre(fc)
    remote(r.x_in, r.xg.at[b], r.xc_s, r.xc_r, (n.sib, s)).start()

    def x_send(k):
        rows = pl.ds(k * XR, XR)
        return remote(r.x_in.at[rows], r.xg.at[b, rows], r.xx_s.at[k], r.xx_r.at[k], (n.across, s))

    def x_relay(k):
        at = r.xg.at[n.across, pl.ds(k * XR, XR)]
        return remote(at, at, r.xl_s.at[k], r.xl_r.at[k], (n.sib, s))

    def relay(k):
        arrived(r.xg.at[n.across, pl.ds(k * XR, XR)], r.xx_r.at[k], (n.across, s))
        x_relay(k).start()

    for k in range(NX):
        x_send(k).start()
    for p in n.batch_peers:
        arrived(r.vecg.at[p, s], r.vp_r.at[p], (p, s))
    for p in n.outer_peers:
        remote(r.vecg.at[:, s], r.vecg.at[:, s], r.vz_s.at[p], r.vz_r.at[z], (b, p * inner + y)).start()
    for c in first:
        c.wait()
    w0.start(0)
    for p in n.outer_peers:
        arrived(r.vecg.at[:, p * inner + y], r.vz_r.at[p], (b, s))
    for o in range(outer):
        for p in n.inner_peers:
            at = r.vecg.at[:, o * inner + y]
            remote(at, at, r.vy_s.at[o, p], r.vy_r.at[o, y], (b, z * inner + p)).start()
    for fc in range(1, nf):
        w0.start(fc)
    for o in range(outer):
        for p in n.inner_peers:
            arrived(r.vecg.at[:, o * inner + p], r.vy_r.at[o, p], (b, s))
    per = F // R
    for k in range(dm.d // F):
        bb, s0 = (k * per) // ns, (k * per) % ns
        total = r.vecg[bb, s0]
        for j in range(1, per):
            total = total + r.vecg[bb, s0 + j]
        r.vec[:, k * F : (k + 1) * F] = total
    own_x.wait()

    TILE = 32

    def norm_block(bb):
        def step(i, carry):
            rows = pl.ds(pl.multiple_of(i * TILE, TILE), TILE)
            x = r.xg[bb, rows, :].astype(F32)
            mu, rstd, normed = norm_rows(x, r.vec[0:1, :])
            every = pl.ds(pl.multiple_of(bb * dm.local + i * TILE, TILE), TILE)
            r.normed[every, :] = normed
            r.mu_out[every, :] = jnp.broadcast_to(mu, (TILE, F))
            r.rstd_out[every, :] = jnp.broadcast_to(rstd, (TILE, F))
            for fc in range(nf):
                r.xS[fc, every, :] = r.xg[bb, rows, pl.ds(at128(b * dm.q + fc * F), F)].astype(F32)
            return carry

        lax.fori_loop(0, dm.local // TILE, step, 0)

    norm_block(b)
    arrived(r.xg.at[n.sib], r.xc_r, (n.sib, s))
    norm_block(n.sib)
    w0.forward(0)
    relay(0)
    relay(1)
    for fc in range(nf):
        w1.pre(fc)
    w0.forward(1)
    relay(2)
    w0.forward(2)
    relay(3)
    norm_block(n.across)
    w0.forward(3)
    for fc in range(nf):
        w1.start(fc)
    for k in range(NX):
        arrived(r.xg.at[n.diag, pl.ds(k * XR, XR)], r.xl_r.at[k], (n.sib, s))
    norm_block(n.diag)
    normed_copy = local_copy(r.normed, r.normed_out, r.loc.at[0])

    def p1(fc):
        w0.complete(fc)
        products(dm, r, n, r.wq0, (fc,), 0)
        scan_totals(dm, r, n, fc)

    pend = []

    def p2(fc):
        scan_finish(dm, r, n, fc, 0)
        r.hb[fc] = r.hS[fc].astype(BF16)
        remote(r.hb.at[fc], r.x1g_out.at[b, fc], r.h_s.at[fc], r.h_r.at[fc], (n.across, s)).start()
        remote(r.hb.at[fc], r.x1g_out.at[b, fc], r.hc_s.at[fc], r.hc_r.at[fc], (n.sib, s)).start()
        pend.append(local_copy(r.hb.at[fc], r.x1g_out.at[b, fc], r.out_sem.at[fc, 0]))
        pairs = [(r.fS, r.f_out), (r.cS, r.c_out), (r.rS, r.r_out), (r.cellS, r.cell_out), (r.hS, r.x1_out), (r.xS, r.xo_out)]
        for k, (src, dst) in enumerate(pairs):
            pend.append(local_copy(src.at[fc], dst.at[fc], r.out_sem.at[fc, k + 1]))

    def h_relay(fc):
        at = r.x1g_out.at[n.across, fc]
        arrived(at, r.h_r.at[fc], (n.across, s))
        remote(at, at, r.hl_s.at[fc], r.hl_r.at[fc], (n.sib, s)).start()

    p1(0)
    p1(1)
    p2(0)
    for p in n.batch_peers:
        cols = pl.ds(at128(p * dm.q), dm.q)
        remote(r.cot_in.at[:, cols], r.cot_out.at[b], r.cot_s.at[p], r.cot_r.at[b], (p, s)).start()
    pend.append(local_copy(r.cot_in.at[:, pl.ds(at128(b * dm.q), dm.q)], r.cot_out.at[b], r.loc.at[1]))
    p1(2)
    p2(1)
    w1.forward(0)
    p1(3)
    p2(2)
    p2(3)
    wq_copy = local_copy(r.wq0, r.wq0_out, r.loc.at[2])
    for fc in range(nf):
        if fc:
            w1.forward(fc)
        h_relay(fc)
    r.inc_out[...] = r.incS[...]
    r.tot_out[...] = r.tot[...]
    r.vec_out[...] = r.vec[...]
    for fc in range(nf):
        w1.complete(fc)
        arrived(r.x1g_out.at[n.sib, fc], r.hc_r.at[fc], (n.sib, s))
        arrived(r.x1g_out.at[n.diag, fc], r.hl_r.at[fc], (n.sib, s))
    for p in n.batch_peers:
        arrived(r.cot_out.at[p], r.cot_r.at[p], (p, s))
    for c in pend:
        c.wait()
    normed_copy.wait()
    wq_copy.wait()
    for p in n.batch_peers:
        sent(r.vec_in, r.vp_s.at[p], (p, s))
        sent(r.cot_out.at[p], r.cot_s.at[p], (p, s))
    for p in n.outer_peers:
        sent(r.vecg.at[:, s], r.vz_s.at[p], (b, s))
    for p in n.inner_peers:
        for o in range(outer):
            sent(r.vecg.at[:, s], r.vy_s.at[o, p], (b, s))
    sent(r.x_in, r.xc_s, (n.sib, s))
    for k in range(NX):
        x_send(k).wait_send()
        x_relay(k).wait_send()
    totals_sent(dm, r, n)
    for fc in range(nf):
        w0.drain(fc)
        w1.drain(fc)
        for sem in (r.h_s, r.hc_s, r.hl_s):
            sent(r.hb.at[fc], sem.at[fc], (b, s))


def scan_scratch(dm):
    nf, ns = dm.nf, dm.ns
    return {
        "totS": V((nf, 2, dm.nseq, F), F32),
        "t_s": DMA((nf, ns)), "t_r": DMA((nf, ns)),
    }


def call_one(dm, x, w, vec, cot):
    nb, ns, nf, inner, outer, R = dm.nb, dm.ns, dm.nf, dm.inner, dm.outer, dm.rows
    D, q, tok, L = dm.d, dm.q, dm.tok, dm.layers
    wshape = (nb, ns * R, dm.cols)
    chunk, cV = ((nf, tok, F), F32, HBM), V((nf, tok, F), F32)
    ins = {"x_in": (x, HBM), "w_in": (w, HBM), "vec_in": (vec, INV), "cot_in": (cot, HBM)}
    outs = {
        "normed_out": ((tok, D), BF16, HBM), "wq0_out": (wshape, BF16, HBM), "wq1_out": (wshape, BF16, HBM),
        "cot_out": ((nb, dm.local, q), BF16, HBM), "x1g_out": ((nb, nf, tok, F), BF16, HBM),
        "x1_out": chunk, "xo_out": chunk, "f_out": chunk, "c_out": chunk, "r_out": chunk, "cell_out": chunk,
        "inc_out": ((nf, dm.nseq, F), F32, INV), "tot_out": ((nf, ns, 2, dm.nseq, F), F32, INV),
        "vec_out": ((16, D), F32, INV), "mu_out": ((tok, F), F32, INV), "rstd_out": ((tok, F), F32, INV),
    }
    scratch = {
        "xg": V((nb, dm.local, D), BF16), "normed": V((tok, D), BF16), "wq0": V(wshape, BF16),
        "vecg": V((nb, ns, 16, F), F32), "vec": V((16, D), F32),
        "xS": cV, "fS": cV, "cS": cV, "rS": cV, "cellS": cV, "hS": cV, "hb": V((nf, tok, F), BF16),
        "incS": V((nf, dm.nseq, F), F32), "tot": V((nf, ns, 2, dm.nseq, F), F32),
        "pre_s": DMA((L, nf, nb)), "pre_r": DMA((L, nf, nb)), "z_s": DMA((L, nf, outer, 2)), "z_r": DMA((L, nf, outer)),
        "y_s": DMA((L, nf, outer, inner)), "y_r": DMA((L, nf, outer, inner)),
        "vp_s": DMA((nb,)), "vp_r": DMA((nb,)), "vz_s": DMA((outer,)), "vz_r": DMA((outer,)),
        "vy_s": DMA((outer, inner)), "vy_r": DMA((outer, inner)),
        "xx_s": DMA((4,)), "xx_r": DMA((4,)), "xc_s": DMA, "xc_r": DMA, "xl_s": DMA((4,)), "xl_r": DMA((4,)),
        "cot_s": DMA((nb,)), "cot_r": DMA((nb,)),
        "h_s": DMA((nf,)), "h_r": DMA((nf,)), "hc_s": DMA((nf,)), "hc_r": DMA((nf,)), "hl_s": DMA((nf,)), "hl_r": DMA((nf,)),
        "loc": DMA((2 * nf + 1,)), "out_sem": DMA((nf, 7)),
        **scan_scratch(dm),
    }
    return launch(dm, "forward_one", 0, kernel_one, ins, outs, scratch)


def kernel_two(dm, r):
    n = Net(dm)
    nb, nf = dm.nb, dm.nf
    b, s = n.b, n.s
    w_copy = local_copy(r.w_in, r.wq, r.loc.at[0])
    x_copy = local_copy(r.x1_in, r.xS, r.loc.at[1])
    cot_copy = [local_copy(r.cot_in.at[k], r.cot.at[pl.ds(k * dm.local, dm.local)], r.loc.at[2 + k]) for k in range(nb)]
    TT, TILE = 256, 32

    def fetch(k):
        return pltpu.make_async_copy(r.x1g_in.at[:, :, pl.ds(k * TT, TT)], r.xt.at[k % 2], r.xt_sem.at[k % 2])

    fetch(0).start()
    for k in range(dm.tok // TT):
        if (k + 1) * TT < dm.tok:
            fetch(k + 1).start()
        fetch(k).wait()

        def step(i, carry, k=k):
            rows = pl.ds(pl.multiple_of(i * TILE, TILE), TILE)
            x = jnp.concatenate([r.xt[k % 2, q, fc, rows, :] for q in range(nb) for fc in range(nf)], axis=1).astype(F32)
            mu, rstd, normed = norm_rows(x, r.vec[5:6, :])
            every = pl.ds(pl.multiple_of(k * TT + i * TILE, TILE), TILE)
            r.normed[every, :] = normed
            r.mu_out[every, :] = jnp.broadcast_to(mu, (TILE, F))
            r.rstd_out[every, :] = jnp.broadcast_to(rstd, (TILE, F))
            return carry

        lax.fori_loop(0, TT // TILE, step, 0)
    normed_copy = local_copy(r.normed, r.normed_out, r.xt_sem.at[0])
    for c in [w_copy, x_copy] + cot_copy:
        c.wait()

    def p1(fcs):
        products(dm, r, n, r.wq, fcs, 5)
        for fc in fcs:
            scan_totals(dm, r, n, fc)

    def block_send(fc, p):
        cols = pl.ds(at128(b * dm.q + fc * F), F)
        src = r.hb.at[fc, pl.ds(pl.multiple_of(p * dm.local, dm.local), dm.local)]
        return remote(src, r.block_out.at[:, cols], r.o_s.at[fc, p], r.o_r.at[fc, b], (p, s))

    pend = []

    def p2(fc):
        scan_finish(dm, r, n, fc, 5)
        r.hb[fc] = r.hS[fc].astype(BF16)
        for p in n.batch_peers:
            block_send(fc, p).start()
        cols = pl.ds(at128(b * dm.q + fc * F), F)
        src = r.hb.at[fc, pl.ds(pl.multiple_of(b * dm.local, dm.local), dm.local)]
        pend.append(local_copy(src, r.block_out.at[:, cols], r.out_sem.at[fc, 2]))
        r.dhS[fc] = r.cot[:, fc * F : (fc + 1) * F].astype(F32)
        back_totals(dm, r, n, fc, 5)

    def p3(fc):
        back_finish(dm, r, n, fc, 5)
        pend.extend(back_outputs(dm, r, fc))

    p1((0, 1))
    p1((2, 3))
    for fc in range(nf):
        p2(fc)
    for fc in range(nf):
        p3(fc)
    for fc in range(nf):
        for p in n.batch_peers:
            block_send(fc, p).wait_send()
            arrived(r.block_out.at[:, pl.ds(at128(p * dm.q + fc * F), F)], r.o_r.at[fc, p], (p, s))
    for c in pend:
        c.wait()
    normed_copy.wait()
    totals_sent(dm, r, n)
    back_sent(dm, r, n)


def call_two(dm, one):
    nb, ns, nf = dm.nb, dm.ns, dm.nf
    tok = dm.tok
    cV = V((nf, tok, F), F32)
    ins = {
        "w_in": (one.wq1_out, HBM), "x1_in": (one.x1_out, HBM), "cot_in": (one.cot_out, HBM),
        "x1g_in": (one.x1g_out, HBM), "vec": (one.vec_out, INV),
    }
    outs = {
        "normed_out": ((tok, dm.d), BF16, HBM), "block_out": ((dm.local, dm.d), BF16, HBM),
        "dmixed_out": ((tok, dm.cols), BF16, HBM), "dtail_out": ((nf, tok, F), F32, HBM),
        "vsum_out": ((nf, 4, dm.nseq, F), F32, INV), "mu_out": ((tok, F), F32, INV), "rstd_out": ((tok, F), F32, INV),
    }
    scratch = {
        "wq": V((nb, ns * dm.rows, dm.cols), BF16), "cot": V((tok, dm.q), BF16), "xt": V((2, nb, nf, 256, F), BF16),
        "normed": V((tok, dm.d), BF16), "dmixed": V((tok, dm.cols), BF16),
        "xS": cV, "fS": cV, "cS": cV, "rS": cV, "cellS": cV, "drS": cV, "hS": cV, "hb": V((nf, tok, F), BF16),
        "incS": V((nf, dm.nseq, F), F32), "tot": V((nf, ns, 2, dm.nseq, F), F32),
        "bk": V((nf, ns, dm.nseq, F), F32), "bkS": V((nf, dm.nseq, F), F32),
        "k_s": DMA((nf, ns)), "k_r": DMA((nf, ns)), "o_s": DMA((nf, nb)), "o_r": DMA((nf, nb)),
        "loc": DMA((2 + nb,)), "xt_sem": DMA((2,)), "out_sem": DMA((nf, 3)),
        **scan_scratch(dm),
    }
    alias = dict(scratch)

    def kernel(dm, r):
        r.dhS = r.hS
        kernel_two(dm, r)

    return launch(dm, "layer_two", 1, kernel, ins, outs, alias)


def kernel_three(dm, r):
    n = Net(dm)
    nf = dm.nf
    loads = []
    for fc in range(nf):
        pairs = [(r.f_in.at[fc], r.fS), (r.c_in.at[fc], r.cS), (r.r_in.at[fc], r.rS), (r.cell_in.at[fc], r.cellS),
                 (r.xo_in.at[fc], r.xS), (r.dh_in.at[:, pl.ds(fc * F, F)], r.dhS)]
        loads.append([local_copy(src, dst.at[fc], r.loc.at[fc, k]) for k, (src, dst) in enumerate(pairs)])
    pend = []
    for fc in range(nf):
        for c in loads[fc]:
            c.wait()
        back_totals(dm, r, n, fc, 0)
    for fc in range(nf):
        back_finish(dm, r, n, fc, 0)
        pend.extend(back_outputs(dm, r, fc))
    for c in pend:
        c.wait()
    back_sent(dm, r, n)


def call_three(dm, one, dh):
    nb, ns, nf, tok = dm.nb, dm.ns, dm.nf, dm.tok
    cV = V((nf, tok, F), F32)
    ins = {
        "f_in": (one.f_out, HBM), "c_in": (one.c_out, HBM), "r_in": (one.r_out, HBM), "cell_in": (one.cell_out, HBM),
        "xo_in": (one.xo_out, HBM), "dh_in": (dh, HBM), "vec": (one.vec_out, INV), "incS": (one.inc_out, INV), "tot": (one.tot_out, INV),
    }
    outs = {
        "dmixed_out": ((tok, dm.cols), BF16, HBM), "dtail_out": ((nf, tok, F), F32, HBM), "vsum_out": ((nf, 4, dm.nseq, F), F32, INV),
    }
    scratch = {
        "dmixed": V((tok, dm.cols), BF16), "xS": cV, "fS": cV, "cS": cV, "rS": cV, "cellS": cV, "drS": cV, "dhS": cV,
        "bk": V((nf, ns, dm.nseq, F), F32), "bkS": V((nf, dm.nseq, F), F32),
        "k_s": DMA((nf, ns)), "k_r": DMA((nf, ns)), "loc": DMA((nf, 6)), "out_sem": DMA((nf, 3)),
    }
    return launch(dm, "layer_one_back", 2, kernel_three, ins, outs, scratch)


def kernel_grads(first, dm, r):
    n = Net(dm)
    nb, ns, nf, inner, outer, R, q, tok = dm.nb, dm.ns, dm.nf, dm.inner, dm.outer, dm.rows, dm.q, dm.tok
    b, s, z, y = n.b, n.s, n.z, n.y
    base = 0 if first else 5
    NT = nb
    TR = tok // NT
    H = 2
    HC = dm.cols // H
    loads = [local_copy(r.dm_in, r.dmS, r.loc.at[0]), local_copy(r.w_in, r.wS, r.loc.at[1])]
    n_load = local_copy(r.normed_in, r.nS, r.loc.at[2])
    for c in loads:
        c.wait()

    def part(quarter, k):
        return lax.dot_general(
            r.dmS[k * TR : (k + 1) * TR, :], r.wS[quarter], (((1,), (1,)), ((), ())), preferred_element_type=F32
        )

    def to_sib(buf, got, k, i):
        return remote(buf.at[k], got.at[k], r.p_s.at[i, k], r.p_r.at[i, k], (n.sib, s))

    def to_across(k):
        return remote(r.pb.at[k], r.prb.at[k], r.p_s.at[1, k], r.p_r.at[1, k], (n.across, s))

    def stage_a(k):
        r.pa[k] = part(n.diag, k).astype(BF16)
        to_sib(r.pa, r.pra, k, 0).start()

    def stage_b(k):
        v = part(n.across, k)
        arrived(r.pra.at[k], r.p_r.at[0, k], (n.sib, s))
        r.pb[k] = (v + r.pra[k].astype(F32)).astype(BF16)
        to_across(k).start()

    def stage_c(k):
        to_sib(r.pa, r.pra, k, 0).wait_send()
        r.pa[k] = part(n.sib, k).astype(BF16)
        to_sib(r.pa, r.prc, k, 2).start()

    def stage_d(k):
        r.acc[k * TR : (k + 1) * TR, :] = part(b, k)

    def stage_e(k):
        arrived(r.prc.at[k], r.p_r.at[2, k], (n.sib, s))
        arrived(r.prb.at[k], r.p_r.at[1, k], (n.across, s))
        rows = slice(k * TR, (k + 1) * TR)
        r.acc[rows, :] = r.acc[rows, :] + r.prc[k].astype(F32) + r.prb[k].astype(F32)

    def strip(bb, h, pos):
        return r.wg.at[bb, pl.ds(pl.multiple_of(pos * R, R), R), pl.ds(h * HC, HC)]

    def wgrad(bb, h):
        r.wg[bb, :, h * HC : (h + 1) * HC] = lax.dot_general(
            r.nS[:, bb * q : (bb + 1) * q], r.dmS[:, h * HC : (h + 1) * HC], (((0,), (0,)), ((), ())), preferred_element_type=F32
        ).astype(BF16)

    def y_copy(ch, j, o):
        bb, h = ch // H, ch % H
        p = lax.rem(y + j, inner)
        return remote(strip(bb, h, o * inner + p), r.yr.at[ch, inner - j - 1, o], r.y_s.at[ch, j - 1, o], r.y_r.at[ch, inner - j - 1, o], (b, z * inner + p))

    def z_copy(ch, j):
        p = lax.rem(z + j, outer)
        return remote(r.zs.at[ch, p], r.zr.at[ch, outer - j - 1], r.z_s.at[ch, j - 1], r.z_r.at[ch, outer - j - 1], (b, p * inner + y))

    def f_copy(ch):
        bb, h = ch // H, ch % H
        return remote(r.fs.at[ch], r.fr.at[b, h], r.f_s.at[ch], r.f_r.at[b, h], (bb, s))

    def rs_start(ch):
        wgrad(ch // H, ch % H)
        for j in range(1, inner):
            for o in range(outer):
                y_copy(ch, j, o).start()

    def rs_mid(ch):
        bb, h = ch // H, ch % H
        for j in range(1, inner):
            for o in range(outer):
                arrived(r.yr.at[ch, j - 1, o], r.y_r.at[ch, j - 1, o], (b, s))
        for jz in range(outer):
            o = lax.rem(z + jz, outer)
            pos = pl.ds(pl.multiple_of((o * inner + y) * R, R), R)
            total = r.wg[bb, pos, h * HC : (h + 1) * HC].astype(F32)
            for j in range(1, inner):
                total = total + r.yr[ch, j - 1, o].astype(F32)
            r.zs[ch, o] = total.astype(BF16)
            if jz:
                z_copy(ch, jz).start()

    def rs_last(ch):
        bb, h = ch // H, ch % H
        for j in range(1, outer):
            arrived(r.zr.at[ch, j - 1], r.z_r.at[ch, j - 1], (b, s))
        total = r.zs[ch, z].astype(F32)
        for j in range(1, outer):
            total = total + r.zr[ch, j - 1].astype(F32)
        r.fs[ch] = total.astype(BF16)

        @pl.when(b != bb)
        def _():
            f_copy(ch).start()

        @pl.when(b == bb)
        def _():
            r.fr[b, h] = r.fs[ch]

    NCH = nb * H
    stage_a(0)
    stage_a(1)
    n_load.wait()
    rs_start(0)
    for k in range(NT):
        if k + 2 < NT:
            stage_a(k + 2)
        stage_b(k)
    rs_start(1)
    rs_start(2)
    for k in range(NT):
        stage_c(k)
        stage_d(k)
    rs_start(3)
    rs_mid(0)
    rs_start(4)
    rs_start(5)
    rs_mid(1)
    rs_start(6)
    rs_start(7)
    rs_last(0)
    rs_mid(2)
    rs_last(1)
    for k in range(NT):
        stage_e(k)
    rs_mid(3)

    NTILE = tok // F

    def fetch(i, slot):
        rows = pl.ds(pl.multiple_of(i * F, F), F)
        return [
            pltpu.make_async_copy(r.x_in.at[:, rows], r.xt.at[slot], r.tile_sem.at[slot, 0]),
            pltpu.make_async_copy(r.dtail_in.at[:, rows], r.dt.at[slot], r.tile_sem.at[slot, 1]),
            pltpu.make_async_copy(r.mu_in.at[rows], r.mt.at[slot], r.tile_sem.at[slot, 2]),
            pltpu.make_async_copy(r.rstd_in.at[rows], r.rt.at[slot], r.tile_sem.at[slot, 3]),
        ]

    def tiles(body, init):
        for c in fetch(0, 0):
            c.start()

        def step(i, carry):
            slot = lax.rem(i, 2)

            @pl.when(i + 1 < NTILE)
            def _():
                for c in fetch(i + 1, 1 - slot):
                    c.start()

            for c in fetch(i, slot):
                c.wait()
            return body(i, slot, carry)

        return lax.fori_loop(0, NTILE, step, init)

    gains = [vrow(dm, r, n, base, fc) for fc in range(nf)]

    def stats(i, slot, sums):
        rows = pl.ds(pl.multiple_of(i * F, F), F)
        t1, t2 = jnp.zeros((F, F), F32), jnp.zeros((F, F), F32)
        new = []
        for fc in range(nf):
            xhat = (r.xt[slot, fc] - r.mt[slot]) * r.rt[slot]
            dn = r.acc[rows, fc * F : (fc + 1) * F]
            dx = dn * gains[fc]
            t1 = t1 + dx
            t2 = t2 + dx * xhat
            new.append(sums[fc] + jnp.sum((dn * xhat).reshape(F // 8, 8, F), axis=0))
        r.st[b, 0, pl.ds(i, 1), :] = jnp.sum(t1.T, axis=0, keepdims=True)
        r.st[b, 1, pl.ds(i, 1), :] = jnp.sum(t2.T, axis=0, keepdims=True)
        return tuple(new)

    sums = tiles(stats, tuple(jnp.zeros((8, F), F32) for _ in range(nf)))
    for fc in range(nf):
        r.gsum[fc] = sums[fc]
    for p in n.batch_peers:
        remote(r.st.at[b], r.st.at[b], r.st_s.at[p], r.st_r.at[b], (p, s)).start()
    rs_mid(4)
    rs_last(2)
    for p in n.batch_peers:
        arrived(r.st.at[p], r.st_r.at[p], (p, s))
    for k in range(2):
        total = r.st[0, k]
        for j in range(1, nb):
            total = total + r.st[j, k]
        r.stt[k] = total * (1.0 / dm.d)

    for k in range(NT):
        to_across(k).wait_send()

    def final(i, slot, carry):
        rows = pl.ds(pl.multiple_of(i * F, F), F)
        m1 = jnp.broadcast_to(r.stt[0, pl.ds(i, 1), :], (F, F)).T
        m2 = jnp.broadcast_to(r.stt[1, pl.ds(i, 1), :], (F, F)).T
        for fc in range(nf):
            xhat = (r.xt[slot, fc] - r.mt[slot]) * r.rt[slot]
            dx = r.acc[rows, fc * F : (fc + 1) * F] * gains[fc]
            out = r.dt[slot, fc] + r.rt[slot] * (dx - m1 - xhat * m2)
            if first:
                per = TR // F
                r.pb[i // per, pl.ds(pl.multiple_of(lax.rem(i, per) * F, F), F), fc * F : (fc + 1) * F] = out.astype(BF16)
            else:
                r.acc[rows, fc * F : (fc + 1) * F] = out
        return carry

    tiles(final, 0)
    pend = []
    if first:
        for p in n.batch_peers:
            remote(r.pb.at[p], r.fin.at[b], r.g_s.at[p], r.g_r.at[b], (p, s)).start()
        r.fin[b] = r.pb[b]
        vector_start(dm, r, n)
    else:
        pend.append(local_copy(r.acc, r.dx_out, r.loc.at[0]))
        r.gsum_out[...] = r.gsum[...]
    rs_mid(5)
    rs_last(3)
    rs_mid(6)
    rs_last(4)
    rs_mid(7)
    rs_last(5)
    if first:
        for k in range(nb):
            @pl.when(k != b)
            def _(k=k):
                arrived(r.fin.at[k], r.g_r.at[k], (b, s))

            r.acc[k * TR : (k + 1) * TR, :] = r.fin[k].astype(F32)
            pend.append(local_copy(r.acc.at[pl.ds(k * TR, TR)], r.dx_out.at[:, pl.ds(k * q, q)], r.loc.at[3 + k]))
        vector_finish(dm, r, n)
    rs_last(6)
    rs_last(7)
    for p in n.batch_peers:
        for h in range(H):
            arrived(r.fr.at[p, h], r.f_r.at[p, h], (p, s))
    for k in range(nb):
        for fc in range(nf):
            h, o = (fc * G3) // HC, (fc * G3) % HC
            for gate in range(3):
                to = gate * dm.d + k * q + fc * F
                r.wg_out[:, to : to + F] = r.fr[k, h, :, o + gate * F : o + (gate + 1) * F].astype(F32)
    for c in pend:
        c.wait()
    for k in range(NT):
        to_sib(r.pa, r.prc, k, 2).wait_send()
    for p in n.batch_peers:
        sent(r.st.at[b], r.st_s.at[p], (p, s))
        if first:
            sent(r.pb.at[p], r.g_s.at[p], (p, s))
    for ch in range(NCH):
        for j in range(1, inner):
            for o in range(outer):
                y_copy(ch, j, o).wait_send()
        for j in range(1, outer):
            z_copy(ch, j).wait_send()

        @pl.when(b != ch // H)
        def _(ch=ch):
            f_copy(ch).wait_send()


def vector_start(dm, r, n):
    r.vg[n.s] = jnp.zeros((16, dm.q), F32)
    for l, (vs, gs) in enumerate(((r.vsum0, r.gsum), (r.vsum1, r.gsum1))):
        for fc in range(dm.nf):
            cols = slice(fc * F, (fc + 1) * F)
            r.vg[n.s, 5 * l : 5 * l + 1, cols] = jnp.sum(gs[fc], axis=0, keepdims=True)
            for k in range(4):
                r.vg[n.s, 5 * l + 1 + k : 5 * l + 2 + k, cols] = jnp.sum(vs[fc, k], axis=0, keepdims=True)
    for p in n.seq_peers:
        remote(r.vg.at[n.s], r.vg.at[n.s], r.v_s.at[p], r.v_r.at[n.s], (n.b, p)).start()


def vector_finish(dm, r, n):
    for p in n.seq_peers:
        arrived(r.vg.at[p], r.v_r.at[p], (n.b, p))
    total = r.vg[0]
    for j in range(1, dm.ns):
        total = total + r.vg[j]
    r.vg_out[...] = total
    for p in n.seq_peers:
        sent(r.vg.at[n.s], r.v_s.at[p], (n.b, p))


def call_grads(dm, first, w, normed, x, mu, rstd, vec, scans, more):
    nb, ns, nf, inner, outer, R, q, tok = dm.nb, dm.ns, dm.nf, dm.inner, dm.outer, dm.rows, dm.q, dm.tok
    TR, H = tok // nb, 2
    HC, NCH = dm.cols // H, nb * H
    ins = {
        "dm_in": (scans.dmixed_out, HBM), "w_in": (w, HBM), "normed_in": (normed, HBM), "x_in": (x, HBM),
        "dtail_in": (scans.dtail_out, HBM), "mu_in": (mu, HBM), "rstd_in": (rstd, HBM), "vec": (vec, INV),
    }
    outs = {"wg_out": ((R, 3 * dm.d), F32, INV)}
    if first:
        outs["dx_out"] = ((dm.local, dm.d), F32, HBM)
        outs["vg_out"] = ((16, q), F32, INV)
        ins.update({k: (v, INV) for k, v in more.items()})
    else:
        outs["dx_out"] = ((tok, q), F32, HBM)
        outs["gsum_out"] = ((nf, 8, F), F32, INV)
    bV = V((nb, TR, q), BF16)
    scratch = {
        "dmS": V((tok, dm.cols), BF16), "wS": V((nb, ns * R, dm.cols), BF16), "nS": V((tok, dm.d), BF16),
        "acc": V((tok, q), F32), "pa": bV, "pra": bV, "pb": bV, "prb": bV, "prc": bV,
        "wg": V((nb, ns * R, dm.cols), BF16), "yr": V((NCH, inner - 1, outer, R, HC), BF16),
        "zs": V((NCH, outer, R, HC), BF16), "zr": V((NCH, outer - 1, R, HC), BF16),
        "fs": V((NCH, R, HC), BF16), "fr": V((nb, H, R, HC), BF16),
        "xt": V((2, nf, F, F), F32), "dt": V((2, nf, F, F), F32), "mt": V((2, F, F), F32), "rt": V((2, F, F), F32),
        "st": V((nb, 2, tok // F, F), F32), "stt": V((2, tok // F, F), F32), "gsum": V((nf, 8, F), F32),
        "loc": DMA((3 + nb,)), "tile_sem": DMA((2, 4)), "p_s": DMA((3, nb)), "p_r": DMA((3, nb)),
        "y_s": DMA((NCH, inner - 1, outer)), "y_r": DMA((NCH, inner - 1, outer)),
        "z_s": DMA((NCH, outer - 1)), "z_r": DMA((NCH, outer - 1)),
        "f_s": DMA((NCH,)), "f_r": DMA((nb, H)), "st_s": DMA((nb,)), "st_r": DMA((nb,)),
    }
    if first:
        scratch.update({"fin": bV, "g_s": DMA((nb,)), "g_r": DMA((nb,)), "vg": V((ns, 16, q), F32), "v_s": DMA((ns,)), "v_r": DMA((ns,))})
    return launch(dm, "grads_one" if first else "grads_two", 3 if first else 4, functools.partial(kernel_grads, first), ins, outs, scratch)


def prepare(dm, block_input, weight, vectors, cotangent):
    D, nf, nb, R = dm.d, dm.nf, dm.nb, dm.rows
    x = block_input.reshape(dm.local, D)
    cot = cotangent.reshape(dm.local, D)
    w = weight.reshape(dm.layers, R, 3, nb, nf, F).transpose(0, 3, 4, 1, 2, 5).reshape(dm.layers, nb, nf, R, G3)
    s = lax.axis_index("seq")
    v = jnp.pad(vectors.reshape(dm.layers * 5, R), ((0, 16 - dm.layers * 5), (0, 0)))
    lane = lax.broadcasted_iota(jnp.int32, (16, F), 1) // R
    v = jnp.where(lane == lax.rem(s, F // R), jnp.tile(v, (1, F // R)), 0.0)
    return x, w, v, cot


def tuned_body(nb, ns, block_input, weight, vectors, cotangent):
    dm = Dims(nb, ns, block_input.shape, weight.shape)
    one = call_one(dm, *prepare(dm, block_input, weight, vectors, cotangent))
    two = call_two(dm, one)
    g1 = call_grads(dm, False, one.wq1_out, two.normed_out, one.x1_out, two.mu_out, two.rstd_out, one.vec_out, two, {})
    three = call_three(dm, one, g1.dx_out)
    more = {"vsum0": three.vsum_out, "vsum1": two.vsum_out, "gsum1": g1.gsum_out}
    g0 = call_grads(dm, True, one.wq0_out, one.normed_out, one.xo_out, one.mu_out, one.rstd_out, one.vec_out, three, more)
    weight_grad = jnp.stack([g0.wg_out, g1.wg_out], axis=0)
    s = lax.axis_index("seq")
    mine = lax.dynamic_slice_in_dim(g0.vg_out, s * dm.rows, dm.rows, axis=1)[: dm.layers * 5]
    vector_grad = mine.reshape(dm.layers, 5, dm.rows)
    return (
        two.block_out.reshape(block_input.shape), g0.dx_out.reshape(block_input.shape), weight_grad, vector_grad,
    )


def prefix(value, axis, join, neutral, backward):
    count, mine = (lax.axis_size(axis), lax.axis_index(axis))
    pieces = jax.tree.map(lambda part: lax.all_gather(part, axis), value)
    if backward:
        pieces = jax.tree.map(lambda part: part[::-1], pieces)
        mine = count - 1 - mine
    subtotal = jax.tree.map(
        lambda part, zero: jnp.full_like(part, 0) + jnp.asarray(zero, part.dtype), value, neutral
    )

    def step(position, subtotal):
        longer = join(subtotal, jax.tree.map(lambda part: part[position], pieces))
        return jax.tree.map(lambda new, old: jnp.where(position < mine, new, old), longer, subtotal)

    return lax.fori_loop(0, count - 1, step, subtotal)


def compose(earlier, later):
    return (later[0] * earlier[0], later[0] * earlier[1] + later[1])


def rebuild_forward(stream, full, vec):
    norm_scale, vforget, bforget = (vec[0], vec[1], vec[2])
    sequence_batch, time_steps, hidden_width = stream.shape
    center = jnp.mean(stream, axis=-1, keepdims=True)
    shifted_input = stream - center
    inverse_deviation = lax.rsqrt(
        jnp.mean(shifted_input * shifted_input, axis=-1, keepdims=True) + epsilon
    )
    centered_input = shifted_input * inverse_deviation
    normed_input = (
        (centered_input * norm_scale)
        .astype(jnp.bfloat16)
        .reshape(sequence_batch * time_steps, hidden_width)
    )
    mixed = jnp.dot(normed_input, full, preferred_element_type=jnp.float32).reshape(
        sequence_batch, time_steps, 3 * hidden_width
    )
    candidate_value = mixed[..., :hidden_width]
    reset_input = mixed[..., 2 * hidden_width :]
    forget_gate = jax.nn.sigmoid(
        mixed[..., hidden_width : 2 * hidden_width] + vforget * stream + bforget
    )
    gate_values, norm_bias = lax.associative_scan(
        compose, (forget_gate, (1.0 - forget_gate) * candidate_value), axis=1
    )
    return (
        centered_input,
        inverse_deviation,
        normed_input,
        candidate_value,
        reset_input,
        forget_gate,
        gate_values,
        norm_bias,
    )


def finish(vec, reset_input, gate_values, norm_bias, incoming):
    vreset, breset = (vec[3], vec[4])
    cells = gate_values * incoming[:, None, :] + norm_bias
    previous = jnp.concatenate([incoming[:, None, :], cells[:, :-1]], axis=1)
    reset = jax.nn.sigmoid(reset_input + vreset * previous + breset)
    return (cells, previous, reset)


def general_body(block_input, weight, vectors, cotangent):
    sequence_batch, time_steps, hidden_width = block_input.shape
    layers = weight.shape[0]
    params = lax.all_gather(vectors, ("batch", "seq"), axis=2, tiled=True)
    stream = block_input.astype(jnp.float32)
    ones = jnp.ones((sequence_batch, hidden_width), jnp.float32)
    zeros = jnp.zeros((sequence_batch, hidden_width), jnp.float32)
    inputs = []
    entering = []
    for layer in range(layers):
        full = lax.all_gather(weight[layer], ("batch", "seq"), axis=0, tiled=True)
        vec = params[layer]
        pieces = rebuild_forward(stream, full, vec)
        gate_values, norm_bias = (pieces[6], pieces[7])
        arrived = prefix(
            (gate_values[:, -1], norm_bias[:, -1]), "seq", compose, (ones, zeros), False
        )
        incoming = arrived[1]
        cells, previous, reset = finish(vec, pieces[4], gate_values, norm_bias, incoming)
        inputs.append(stream)
        entering.append(incoming)
        stream = reset * cells + (1.0 - reset) * stream
    block_output = stream.astype(jnp.bfloat16)
    grad_out = cotangent.astype(jnp.float32)
    weight_grads = [None] * layers
    vector_terms = [None] * layers
    rows = weight.shape[1]
    for layer in reversed(range(layers)):
        full = lax.all_gather(weight[layer], ("batch", "seq"), axis=0, tiled=True)
        vec = params[layer]
        norm_scale, vforget, vreset = (vec[0], vec[1], vec[3])
        stream = inputs[layer]
        (
            centered_input,
            inverse_deviation,
            normed_input,
            candidate_value,
            reset_input,
            forget_gate,
            gate_values,
            norm_bias,
        ) = rebuild_forward(stream, full, vec)
        cells, previous, reset = finish(vec, reset_input, gate_values, norm_bias, entering[layer])
        dreset = grad_out * (cells - stream) * reset * (1.0 - reset)
        direct = grad_out * reset
        inject = forget_gate * direct + dreset * vreset
        back_gates, back_offsets = lax.associative_scan(
            compose, (jnp.flip(forget_gate, 1), jnp.flip(inject, 1)), axis=1
        )
        back_gates = jnp.flip(back_gates, 1)
        back_offsets = jnp.flip(back_offsets, 1)
        arrived = prefix(
            (back_gates[:, 0], back_offsets[:, 0]), "seq", compose, (ones, zeros), True
        )
        later = arrived[1]
        carried = back_gates * later[:, None, :] + back_offsets
        following = jnp.concatenate([carried[:, 1:], later[:, None, :]], axis=1)
        dcell = direct + following
        dcandidate = dcell * (1.0 - forget_gate)
        dforget = dcell * (previous - candidate_value) * forget_gate * (1.0 - forget_gate)
        dmixed = jnp.concatenate([dcandidate, dforget, dreset], axis=-1).astype(jnp.bfloat16)
        dmixed = dmixed.reshape(sequence_batch * time_steps, 3 * hidden_width)

        def weight_term(start, count, normed_input=normed_input, dmixed=dmixed):
            return lax.dot_general(
                normed_input, dmixed, (((0,), (0,)), ((), ())), preferred_element_type=jnp.float32
            )

        weight_grads[layer] = lax.psum_scatter(
            weight_term(jnp.int32(0), rows * lax.axis_size(("batch", "seq"))),
            ("batch", "seq"),
            scatter_dimension=0,
            tiled=True,
        )
        normed_gradient = lax.dot_general(
            dmixed, full, (((1,), (1,)), ((), ())), preferred_element_type=jnp.float32
        )
        normed_gradient = normed_gradient.reshape(sequence_batch, time_steps, hidden_width)
        vector_terms[layer] = jnp.stack(
            [
                jnp.sum(normed_gradient * centered_input, axis=(0, 1)),
                jnp.sum(dforget * stream, axis=(0, 1)),
                jnp.sum(dforget, axis=(0, 1)),
                jnp.sum(dreset * previous, axis=(0, 1)),
                jnp.sum(dreset, axis=(0, 1)),
            ],
            axis=0,
        )
        centered_gradient = normed_gradient * norm_scale
        through_norm = inverse_deviation * (
            centered_gradient
            - jnp.mean(centered_gradient, axis=-1, keepdims=True)
            - centered_input * jnp.mean(centered_gradient * centered_input, axis=-1, keepdims=True)
        )
        grad_out = grad_out * (1.0 - reset) + dforget * vforget + through_norm
    weight_grad = jnp.stack(weight_grads, axis=0)
    vector_grad = lax.psum_scatter(
        jnp.stack(vector_terms, axis=0), ("batch", "seq"), scatter_dimension=2, tiled=True
    )
    return (block_output, grad_out, weight_grad, vector_grad)


def solution(mesh):
    nb, ns = mesh.shape["batch"], mesh.shape["seq"]
    body = functools.partial(tuned_body, nb, ns) if (nb, ns) == (4, 8) else general_body
    placed = (
        P("batch", "seq", None),
        P(None, ("batch", "seq"), None),
        P(None, None, ("batch", "seq")),
        P("batch", "seq", None),
    )
    return jax.shard_map(
        body,
        mesh=mesh,
        in_specs=placed,
        out_specs=(
            P("batch", "seq", None),
            P("batch", "seq", None),
            P(None, ("batch", "seq"), None),
            P(None, None, ("batch", "seq")),
        ),
        check_vma=False,
    )
```

```python
import functools
import types

import jax
import jax.numpy as jnp
from jax import lax
from jax.experimental import pallas as pl
from jax.experimental.pallas import tpu as pltpu
from jax.sharding import PartitionSpec as P

MESH = pl.DeviceIdType.MESH
F32, BF16 = jnp.float32, jnp.bfloat16
V, DMA = pltpu.VMEM, pltpu.SemaphoreType.DMA
epsilon = 1e-05
F = 128
HBM = pl.BlockSpec(memory_space=pl.ANY)
INV = None


class Dims:
    def __init__(self, nb, ns, x_shape, w_shape):
        self.nb, self.ns = nb, ns
        self.inner = 2
        self.outer = ns // 2
        self.sb, self.steps, self.d = x_shape
        self.local = self.sb * self.steps
        self.runs = 8
        self.stretch = self.runs // self.sb
        self.length = self.local // self.runs
        self.tok = self.local * nb
        self.q = self.d // nb
        self.nf = self.q // F
        self.on_time = 10
        self.early = 2
        self.layers, self.rows = w_shape[0], w_shape[1]


class Net:
    def __init__(self, dm):
        nb, ns, inner, outer = dm.nb, dm.ns, dm.inner, dm.outer
        self.b, self.s = lax.axis_index("batch"), lax.axis_index("seq")
        b, s = self.b, self.s
        self.z, self.y = s // inner, lax.rem(s, inner)
        self.across, self.sib, self.diag = b ^ 2, b ^ 1, b ^ 3
        self.batch_peers = [lax.rem(b + j, nb) for j in range(1, nb)]
        self.outer_peers = [lax.rem(self.z + j, outer) for j in range(1, outer)]
        self.inner_peers = [lax.rem(self.y + j, inner) for j in range(1, inner)]
        self.seq_peers = [lax.rem(s + j, ns) for j in range(1, ns)]
        barrier = pltpu.get_barrier_semaphore()
        for p in self.batch_peers:
            pl.semaphore_signal(barrier, inc=1, device_id=(p, s), device_id_type=MESH)
        for p in self.seq_peers:
            pl.semaphore_signal(barrier, inc=1, device_id=(b, p), device_id_type=MESH)
        self.count = nb - 1 + ns - 1

    def ready(self):
        pl.semaphore_wait(pltpu.get_barrier_semaphore(), self.count)


def remote(src, dst, ssem, rsem, dev):
    return pltpu.make_async_remote_copy(
        src_ref=src, dst_ref=dst, send_sem=ssem, recv_sem=rsem, device_id=dev, device_id_type=MESH
    )


def arrived(dst, rsem, dev):
    remote(dst, dst, rsem, rsem, dev).wait_recv()


def sent(src, ssem, dev):
    remote(src, src, ssem, ssem, dev).wait_send()


def local_copy(src, dst, sem):
    c = pltpu.make_async_copy(src, dst, sem)
    c.start()
    return c


def at128(v):
    return pl.multiple_of(v, F)


def sigmoid(v):
    return 1.0 / (1.0 + jnp.exp(jnp.minimum(-v, 80.0)))


def launch(dm, name, cid, kernel, ins, outs, scratch):
    keep_in = [k for k, (_, kind) in ins.items() if kind is INV]
    keep_out = [k for k, (_, _, kind) in outs.items() if kind is INV]
    names = [k + ("_far" if k in keep_in else "") for k in ins] + [k + ("_far" if k in keep_out else "") for k in outs]
    scratch = dict(scratch)
    for k in keep_in:
        scratch[k] = V(ins[k][0].shape, ins[k][0].dtype)
    for k in keep_out:
        scratch[k] = V(outs[k][0], outs[k][1])
    scratch["keep_sem"] = DMA((len(keep_in) + len(keep_out) + 1,))
    names += list(scratch)

    def run(*refs):
        r = types.SimpleNamespace(**dict(zip(names, refs)))
        far = vars(r)
        loads = {k: local_copy(far[k + "_far"], far[k], r.keep_sem.at[i]) for i, k in enumerate(keep_in)}
        stores = []

        def need(*which):
            for k in which:
                loads.pop(k).wait()

        def store(k):
            stores.append(local_copy(far[k], far[k + "_far"], r.keep_sem.at[len(keep_in) + keep_out.index(k)]))

        r.need, r.store = need, store
        kernel(dm, r)
        for c in stores:
            c.wait()

    got = pl.pallas_call(
        run,
        out_shape=[jax.ShapeDtypeStruct(shape, dtype) for shape, dtype, _ in outs.values()],
        in_specs=[HBM for _ in ins],
        out_specs=[HBM for _ in outs],
        scratch_shapes=list(scratch.values()),
        compiler_params=pltpu.CompilerParams(collective_id=cid, has_side_effects=True, vmem_limit_bytes=63 * 2**20),
        name=name,
    )(*[array for array, _ in ins.values()])
    return types.SimpleNamespace(**dict(zip(outs, got)))


def norm_rows(x, gain):
    mu = jnp.mean(x, axis=-1, keepdims=True)
    xc = x - mu
    rstd = lax.rsqrt(jnp.mean(xc * xc, axis=-1, keepdims=True) + epsilon)
    return mu, rstd, (xc * rstd * gain).astype(BF16)


def vrow(dm, r, n, k, fc):
    return r.vec[k : k + 1, pl.ds(at128(n.b * dm.q + fc * F), F)]


def products(dm, r, n, w, chunks, base, pieces):
    TM = 256

    def step(first, i, carry):
        rows = pl.ds(pl.multiple_of(first + i * TM, TM), TM)
        right = jnp.concatenate(
            [w[fc, g].reshape(dm.d, F) for fc in chunks for g in range(3)], axis=1
        )
        m = jnp.dot(r.normed[rows, :], right, preferred_element_type=F32)
        for k, fc in enumerate(chunks):
            o = 3 * k * F
            vf, bf, br = [vrow(dm, r, n, base + j, fc) for j in (1, 2, 4)]
            r.fS[fc, rows, :] = sigmoid(m[:, o + F : o + 2 * F] + vf * r.xS[fc, rows, :] + bf)
            r.cS[fc, rows, :] = m[:, o : o + F]
            r.rS[fc, rows, :] = m[:, o + 2 * F : o + 3 * F] + br
        return carry

    if pieces is None:
        lax.fori_loop(0, dm.tok // TM, functools.partial(step, 0), 0)
    else:
        for g, part in pieces:
            step(g * dm.local, part, 0)


def at_time(dm, g, t):
    return pl.ds(pl.multiple_of(g * dm.local + t * dm.runs, dm.runs), dm.runs)


def run_index(dm):
    return lax.rem(lax.broadcasted_iota(jnp.int32, (dm.runs, F), 0), dm.stretch)


def turn(v, by):
    return pltpu.roll(v, by % v.shape[0], 0)


def pack(dm, parts, end):
    row = lax.broadcasted_iota(jnp.int32, (dm.runs, F), 0)
    out = jnp.zeros((dm.runs, F), F32)
    for g in range(dm.nb):
        for j in range(dm.sb):
            to = g * dm.sb + j
            out = jnp.where(row == to, turn(parts[g], to - (j * dm.stretch + end)), out)
    return out


def unpack(dm, packed, g, end):
    row = lax.broadcasted_iota(jnp.int32, (dm.runs, F), 0)
    out = jnp.zeros((dm.runs, F), F32)
    for j in range(dm.sb):
        to = j * dm.stretch + end
        out = jnp.where(row == to, turn(packed, to - (g * dm.sb + j)), out)
    return out


def enter(dm, a, v, first, back):
    start = dm.stretch - 1 if back else 0
    index = run_index(dm)
    state = first
    for _ in range(dm.stretch - 1):
        state = jnp.where(index == start, first, turn(a * state + v, -1 if back else 1))
    return state


def scan_totals(dm, r, n, fc):
    groups = range(dm.nb)

    def step(t, carry):
        new = []
        for g in groups:
            a, v = carry[g]
            at = at_time(dm, g, t)
            f, cand = r.fS[fc, at, :], r.cS[fc, at, :]
            new.append((a * f, cand + f * (v - cand)))
        return tuple(new)

    one, zero = jnp.ones((dm.runs, F), F32), jnp.zeros((dm.runs, F), F32)
    got = lax.fori_loop(0, dm.length, step, tuple((one, zero) for _ in groups), unroll=4)
    index = run_index(dm)
    for_a, for_v = [], []
    for g in groups:
        a, v = got[g]
        r.runA[fc, g] = a
        r.runV[fc, g] = v
        product = a
        for _ in range(dm.stretch - 1):
            product = jnp.where(index == 0, a, a * turn(product, 1))
        for_a.append(product)
        for_v.append(a * enter(dm, a, v, zero, False) + v)
    a, v = pack(dm, for_a, dm.stretch - 1), pack(dm, for_v, dm.stretch - 1)
    r.totS[fc, 0] = a
    r.totS[fc, 1] = v
    r.tot[fc, n.s, 0] = a
    r.tot[fc, n.s, 1] = v
    for p in n.seq_peers:
        remote(r.totS.at[fc], r.tot.at[fc, n.s], r.t_s.at[fc, p], r.t_r.at[fc, n.s], (n.b, p)).start()


def scan_finish(dm, r, n, fc, base):
    for p in n.seq_peers:
        arrived(r.tot.at[fc, p], r.t_r.at[fc, p], (n.b, p))
    vr = vrow(dm, r, n, base + 3, fc)

    def fold(j, c):
        return jnp.where(j < n.s, r.tot[fc, j, 0] * c + r.tot[fc, j, 1], c)

    packed = lax.fori_loop(0, dm.ns, fold, jnp.zeros((dm.runs, F), F32))
    entering = []
    for g in range(dm.nb):
        e = enter(dm, r.runA[fc, g], r.runV[fc, g], unpack(dm, packed, g, 0), False)
        r.incS[fc, g] = e
        entering.append(e)

    def step(t, carry):
        new = []
        for g in range(dm.nb):
            prev = carry[g]
            at = at_time(dm, g, t)
            f, cand, x = r.fS[fc, at, :], r.cS[fc, at, :], r.xS[fc, at, :]
            reset = sigmoid(r.rS[fc, at, :] + vr * prev)
            c = cand + f * (prev - cand)
            r.cellS[fc, at, :] = c
            r.rS[fc, at, :] = reset
            r.hS[fc, at, :] = x + reset * (c - x)
            new.append(c)
        return tuple(new)

    lax.fori_loop(0, dm.length, step, tuple(entering), unroll=2)


def totals_sent(dm, r, n):
    for fc in range(dm.nf):
        for p in n.seq_peers:
            sent(r.totS.at[fc], r.t_s.at[fc, p], (n.b, p))


def back_totals(dm, r, n, fc, base):
    vr = vrow(dm, r, n, base + 3, fc)
    zero = jnp.zeros((dm.runs, F), F32)

    def step(i, carry):
        new = []
        for g in range(dm.nb):
            at = at_time(dm, g, dm.length - 1 - i)
            reset, dh = r.rS[fc, at, :], r.dhS[fc, at, :]
            direct = dh * reset
            dreset = (r.cellS[fc, at, :] - r.xS[fc, at, :]) * direct * (1.0 - reset)
            r.rS[fc, at, :] = direct
            r.drS[fc, at, :] = dreset
            new.append(r.fS[fc, at, :] * (direct + carry[g]) + dreset * vr)
        return tuple(new)

    got = lax.fori_loop(0, dm.length, step, tuple(zero for _ in range(dm.nb)), unroll=2)
    parts = []
    for g in range(dm.nb):
        a, v = r.runA[fc, g], got[g]
        r.backV[fc, g] = v
        parts.append(a * enter(dm, a, v, zero, True) + v)
    v = pack(dm, parts, 0)
    r.bkS[fc] = v
    r.bk[fc, n.s] = v
    for p in n.seq_peers:
        remote(r.bkS.at[fc], r.bk.at[fc, n.s], r.k_s.at[fc, p], r.k_r.at[fc, n.s], (n.b, p)).start()


def back_finish(dm, r, n, fc, base):
    for p in n.seq_peers:
        arrived(r.bk.at[fc, p], r.k_r.at[fc, p], (n.b, p))
    vf, vr = vrow(dm, r, n, base + 1, fc), vrow(dm, r, n, base + 3, fc)

    def fold(i, c):
        j = dm.ns - 1 - i
        return jnp.where(j > n.s, r.tot[fc, j, 0] * c + r.bk[fc, j], c)

    zero = jnp.zeros((dm.runs, F), F32)
    packed = lax.fori_loop(0, dm.ns, fold, zero)
    carries = [
        enter(dm, r.runA[fc, g], r.backV[fc, g], unpack(dm, packed, g, dm.stretch - 1), True) for g in range(dm.nb)
    ]

    def one(at, prev, carry, sums):
        s1, s2, s3, s4 = sums
        f, cand, x = r.fS[fc, at, :], r.cS[fc, at, :], r.xS[fc, at, :]
        direct, dreset = r.rS[fc, at, :], r.drS[fc, at, :]
        dcell = direct + carry
        dcand = dcell * (1.0 - f)
        dforget = dcand * f * (prev - cand)
        r.cS[fc, at, :] = dcand
        r.fS[fc, at, :] = dforget
        r.rS[fc, at, :] = r.dhS[fc, at, :] - direct + dforget * vf
        return f * dcell + dreset * vr, (s1 + dforget * x, s2 + dforget, s3 + dreset * prev, s4 + dreset)

    def step(i, state):
        t = dm.length - 1 - i
        carry, sums = state
        new = []
        for g in range(dm.nb):
            c, sums = one(at_time(dm, g, t), r.cellS[fc, at_time(dm, g, t - 1), :], carry[g], sums)
            new.append(c)
        return tuple(new), sums

    carry, sums = lax.fori_loop(0, dm.length - 1, step, (tuple(carries), (zero, zero, zero, zero)), unroll=3)
    for g in range(dm.nb):
        _, sums = one(at_time(dm, g, 0), r.incS[fc, g], carry[g], sums)
    for k in range(4):
        r.vsum_out[fc, k] = sums[k]
    for g, part in enumerate((r.cS, r.fS, r.drS)):
        r.dmixed[fc, g] = part[fc].astype(BF16)


def back_sent(dm, r, n):
    for fc in range(dm.nf):
        for p in n.seq_peers:
            sent(r.bkS.at[fc], r.k_s.at[fc, p], (n.b, p))


def back_outputs(dm, r, fc):
    return [
        local_copy(r.dmixed.at[fc], r.dmixed_out.at[fc], r.out_sem.at[fc, 0]),
        local_copy(r.rS.at[fc], r.dtail_out.at[fc], r.out_sem.at[fc, 1]),
    ]


class Gather:
    def __init__(self, dm, n, r, l, w):
        self.dm, self.n, self.r, self.l, self.w = dm, n, r, l, w

    def strip(self, fc, pos):
        R = self.dm.rows
        return self.w.at[fc, :, :, pl.ds(pl.multiple_of(pos * R, R), R)]

    def piece(self, fc, b, gates=slice(0, 3)):
        n, R = self.n, self.dm.rows
        return self.w.at[fc, gates, b, pl.ds(pl.multiple_of(n.s * R, R), R)]

    def source(self, fc, p, gate):
        dm = self.dm
        return self.r.w_in.at[self.l, :, pl.ds(at128(gate * dm.d + p * dm.q + fc * F), F)]

    def own(self, fc):
        r, l, b = self.r, self.l, self.n.b
        return [local_copy(self.source(fc, b, g), self.piece(fc, b, g), r.own_sem.at[l, fc, g]) for g in range(3)]

    def pre(self, fc):
        n, r, l = self.n, self.r, self.l
        for p in n.batch_peers:
            for g in range(3):
                remote(
                    self.source(fc, p, g), self.piece(fc, n.b, g), r.pre_s.at[l, fc, p], r.pre_r.at[l, fc, n.b], (p, n.s)
                ).start()

    def hop(self, fc, src, to):
        n, r, l, dm = self.n, self.r, self.l, self.dm
        at = self.strip(fc, src * dm.inner + n.y)
        side = 1 if to > 0 else 0
        return remote(at, at, r.z_s.at[l, fc, src, side], r.z_r.at[l, fc, src], (n.b, (n.z + to) * dm.inner + n.y))

    def to_inner(self, fc, src):
        n, r, l, dm = self.n, self.r, self.l, self.dm
        at = self.strip(fc, src * dm.inner + n.y)
        return [
            remote(at, at, r.y_s.at[l, fc, src, p], r.y_r.at[l, fc, src, n.y], (n.b, n.z * dm.inner + p))
            for p in n.inner_peers
        ]

    def start(self, fc, inner=True):
        n, r, l, dm = self.n, self.r, self.l, self.dm
        for p in n.batch_peers:
            arrived(self.piece(fc, p), r.pre_r.at[l, fc, p], (p, n.s))
        pl.when(n.z < dm.outer - 1)(lambda: self.hop(fc, n.z, 1).start())
        pl.when(n.z > 0)(lambda: self.hop(fc, n.z, -1).start())
        if inner:
            for c in self.to_inner(fc, n.z):
                c.start()

    def step(self, fc, h, inner=True):
        n, r, l, dm = self.n, self.r, self.l, self.dm
        for way in (-1, 1):
            src = n.z + way * h
            has = (src >= 0) if way < 0 else (src < dm.outer)
            on = (n.z < dm.outer - 1) if way < 0 else (n.z > 0)

            def take(src=src, on=on, way=way):
                at = self.strip(fc, src * dm.inner + n.y)
                arrived(at, r.z_r.at[l, fc, src], (n.b, n.s))
                pl.when(on)(lambda: self.hop(fc, src, -way).start())
                if inner:
                    for c in self.to_inner(fc, src):
                        c.start()

            pl.when(has)(take)

    def complete(self, fc):
        n, r, l, dm = self.n, self.r, self.l, self.dm
        for o in range(dm.outer):
            for p in n.inner_peers:
                arrived(self.strip(fc, o * dm.inner + p), r.y_r.at[l, fc, o, p], (n.b, n.s))

    def drain_inner(self, fc):
        for o in range(self.dm.outer):
            for p in self.n.inner_peers:
                sent(self.strip(fc, self.n.s), self.r.y_s.at[self.l, fc, o, p], (self.n.b, self.n.s))

    def drain(self, fc, inner=True):
        n, r, l, dm = self.n, self.r, self.l, self.dm
        if inner:
            self.drain_inner(fc)
        for p in n.batch_peers:
            sent(self.piece(fc, p), r.pre_s.at[l, fc, p], (p, n.s))
        for o in range(dm.outer):
            right = jnp.logical_and(o <= n.z, n.z < dm.outer - 1)
            left = jnp.logical_and(o >= n.z, n.z > 0)
            for ok, side in ((right, 1), (left, 0)):
                pl.when(ok)(lambda o=o, side=side: sent(self.strip(fc, n.s), r.z_s.at[l, fc, o, side], (n.b, n.s)))


def kernel_one(dm, r):
    n = Net(dm)
    nb, ns, nf, inner, outer, R = dm.nb, dm.ns, dm.nf, dm.inner, dm.outer, dm.rows
    b, s, z, y = n.b, n.s, n.z, n.y
    w0, w1 = Gather(dm, n, r, 0, r.wq0), Gather(dm, n, r, 1, r.wq1_out)
    NX, NA = 4, dm.early
    XR = dm.local // NX

    own_w = [w0.own(fc) for fc in range(nf)]
    own_x = local_copy(r.x_in, r.xg.at[b], r.loc.at[2 * nf])
    r.need("vec_in")
    n.ready()
    for fc in range(nf):
        w0.pre(fc)
        if fc == 0:
            r.vecg[b, s] = r.vec_in[...]
            for p in n.batch_peers:
                remote(r.vec_in, r.vecg.at[b, s], r.vp_s.at[p], r.vp_r.at[b], (p, s)).start()
    remote(r.x_in, r.xg.at[b], r.xc_s, r.xc_r, (n.sib, s)).start()

    def x_send(k):
        rows = pl.ds(k * XR, XR)
        return remote(r.x_in.at[rows], r.xg.at[b, rows], r.xx_s.at[k], r.xx_r.at[k], (n.across, s))

    def x_relay(k):
        at = r.xg.at[n.across, pl.ds(k * XR, XR)]
        return remote(at, at, r.xl_s.at[k], r.xl_r.at[k], (n.sib, s))

    def relay(k):
        arrived(r.xg.at[n.across, pl.ds(k * XR, XR)], r.xx_r.at[k], (n.across, s))
        x_relay(k).start()

    def w0_start(fc):
        for c in own_w[fc]:
            c.wait()
        w0.start(fc)

    w0_start(0)
    for k in range(NX):
        x_send(k).start()
    for p in n.batch_peers:
        arrived(r.vecg.at[p, s], r.vp_r.at[p], (p, s))
    for p in n.outer_peers:
        remote(r.vecg.at[:, s], r.vecg.at[:, s], r.vz_s.at[p], r.vz_r.at[z], (b, p * inner + y)).start()
    w0.step(0, 1)
    for p in n.outer_peers:
        arrived(r.vecg.at[:, p * inner + y], r.vz_r.at[p], (b, s))
    for o in range(outer):
        for p in n.inner_peers:
            at = r.vecg.at[:, o * inner + y]
            remote(at, at, r.vy_s.at[o, p], r.vy_r.at[o, y], (b, z * inner + p)).start()
    w0.step(0, 2)
    w0_start(1)
    w0.step(0, 3)
    for o in range(outer):
        for p in n.inner_peers:
            arrived(r.vecg.at[:, o * inner + p], r.vy_r.at[o, p], (b, s))
    per = F // R
    for k in range(dm.d // F):
        bb, s0 = (k * per) // ns, (k * per) % ns
        total = r.vecg[bb, s0]
        for j in range(1, per):
            total = total + r.vecg[bb, s0 + j]
        r.vec[:, k * F : (k + 1) * F] = total
    own_x.wait()

    TILE = 32

    def norm_block(bb, lo=0, count=dm.local):
        def step(i, carry):
            rows = pl.ds(pl.multiple_of(lo + i * TILE, TILE), TILE)
            x = r.xg[bb, rows, :].astype(F32)
            mu, rstd, normed = norm_rows(x, r.vec[0:1, :])
            every = pl.ds(pl.multiple_of(bb * dm.local + lo + i * TILE, TILE), TILE)
            r.normed[every, :] = normed
            r.mu_out[every, :] = jnp.broadcast_to(mu, (TILE, F))
            r.rstd_out[every, :] = jnp.broadcast_to(rstd, (TILE, F))
            for fc in range(nf):
                r.xS[fc, every, :] = r.xg[bb, rows, pl.ds(at128(b * dm.q + fc * F), F)].astype(F32)
            return carry

        lax.fori_loop(0, count // TILE, step, 0)

    def diag_norm(k):
        arrived(r.xg.at[n.diag, pl.ds(k * XR, XR)], r.xl_r.at[k], (n.sib, s))
        norm_block(n.diag, k * XR, XR)

    def across_norm(k):
        norm_block(n.across, k * XR, XR)

    def prod(fc, *pieces):
        products(dm, r, n, r.wq0, (fc,), 0, pieces)

    near = [(g, part) for g in (b, n.sib) for part in range(2)]
    w0.step(1, 1)
    norm_block(b)
    w0.step(1, 2)
    w0_start(2)
    arrived(r.xg.at[n.sib], r.xc_r, (n.sib, s))
    norm_block(n.sib)
    w0.step(1, 3)
    w0.step(2, 1)
    relay(0)
    w0.complete(0)
    prod(0, *near)
    w0.step(2, 2)
    w0_start(3)
    across_norm(0)
    relay(1)
    across_norm(1)
    w0.step(2, 3)
    w0.step(3, 1)
    prod(0, (n.across, 0))
    diag_norm(0)
    w0.step(3, 2)
    diag_norm(1)
    w0.complete(1)
    prod(1, *near)
    w0.step(3, 3)
    relay(2)
    across_norm(2)
    prod(0, (n.diag, 0))
    prod(1, (n.across, 0), (n.diag, 0))
    diag_norm(2)
    second = [c for fc in range(nf) for c in w1.own(fc)]
    relay(3)
    for fc in range(nf):
        w1.pre(fc)
    across_norm(3)
    prod(0, (n.across, 1))
    diag_norm(3)
    prod(0, (n.diag, 1))
    scan_totals(dm, r, n, 0)
    prod(1, (n.across, 1), (n.diag, 1))
    scan_totals(dm, r, n, 1)
    normed_copy = local_copy(r.normed, r.normed_out, r.loc.at[0])
    r.store("mu_out")
    r.store("rstd_out")

    pend = []

    def p2(fc):
        scan_finish(dm, r, n, fc, 0)
        r.hb[fc] = r.hS[fc].astype(BF16)
        remote(r.hb.at[fc], r.x1g_out.at[b, fc], r.h_s.at[fc], r.h_r.at[fc], (n.across, s)).start()
        remote(r.hb.at[fc], r.x1g_out.at[b, fc], r.hc_s.at[fc], r.hc_r.at[fc], (n.sib, s)).start()
        pend.append(local_copy(r.hb.at[fc], r.x1g_out.at[b, fc], r.out_sem.at[fc, 0]))
        pairs = [(r.fS, r.f_out), (r.cS, r.c_out), (r.rS, r.r_out), (r.cellS, r.cell_out), (r.hS, r.x1_out), (r.xS, r.xo_out)]
        for k, (src, dst) in enumerate(pairs):
            pend.append(local_copy(src.at[fc], dst.at[fc], r.out_sem.at[fc, k + 1]))

    def h_relay(fc):
        at = r.x1g_out.at[n.across, fc]
        arrived(at, r.h_r.at[fc], (n.across, s))
        remote(at, at, r.hl_s.at[fc], r.hl_r.at[fc], (n.sib, s)).start()

    for c in second:
        c.wait()
    w1.start(0, 0 < NA)
    w0.complete(2)
    products(dm, r, n, r.wq0, (2,), 0, None)
    scan_totals(dm, r, n, 2)
    w1.step(0, 1, 0 < NA)
    p2(0)
    w1.step(0, 2, 0 < NA)
    w1.start(1, 1 < NA)
    p2(1)
    w0.complete(3)
    products(dm, r, n, r.wq0, (3,), 0, None)
    wq_copy = local_copy(r.wq0, r.wq0_out, r.loc.at[2])
    scan_totals(dm, r, n, 3)
    w1.step(0, 3, 0 < NA)
    p2(2)
    w1.step(1, 1, 1 < NA)
    h_relay(0)
    p2(3)
    r.inc_out[...] = r.incS[...]
    r.runA_out[...] = r.runA[...]
    r.tot_out[...] = r.tot[...]
    r.vec_out[...] = r.vec[...]
    for k in ("inc_out", "runA_out", "tot_out", "vec_out"):
        r.store(k)
    w1.step(1, 2, 1 < NA)
    w1.start(2, 2 < NA)
    w1.step(1, 3, 1 < NA)
    h_relay(1)
    w1.step(2, 1, 2 < NA)
    w1.step(2, 2, 2 < NA)
    w1.start(3, 3 < NA)
    w1.step(2, 3, 2 < NA)
    h_relay(2)
    for h in range(1, outer):
        w1.step(3, h, 3 < NA)
    h_relay(3)
    for fc in range(nf):
        if fc < NA:
            w1.complete(fc)
        arrived(r.x1g_out.at[n.sib, fc], r.hc_r.at[fc], (n.sib, s))
        arrived(r.x1g_out.at[n.diag, fc], r.hl_r.at[fc], (n.sib, s))
    for c in pend:
        c.wait()
    normed_copy.wait()
    wq_copy.wait()
    for p in n.batch_peers:
        sent(r.vec_in, r.vp_s.at[p], (p, s))
    for p in n.outer_peers:
        sent(r.vecg.at[:, s], r.vz_s.at[p], (b, s))
    for p in n.inner_peers:
        for o in range(outer):
            sent(r.vecg.at[:, s], r.vy_s.at[o, p], (b, s))
    sent(r.x_in, r.xc_s, (n.sib, s))
    for k in range(NX):
        x_send(k).wait_send()
        x_relay(k).wait_send()
    totals_sent(dm, r, n)
    for fc in range(nf):
        w0.drain(fc)
        w1.drain(fc, fc < NA)
        for sem in (r.h_s, r.hc_s, r.hl_s):
            sent(r.hb.at[fc], sem.at[fc], (b, s))


def scan_scratch(dm):
    nf, ns = dm.nf, dm.ns
    return dict(
        totS=V((nf, 2, dm.runs, F), F32),
        t_s=DMA((nf, ns)), t_r=DMA((nf, ns)),
    )


def call_one(dm, x, w, vec):
    nb, ns, nf, inner, outer, R = dm.nb, dm.ns, dm.nf, dm.inner, dm.outer, dm.rows
    D, q, tok, L = dm.d, dm.q, dm.tok, dm.layers
    wshape = (nf, 3, nb, ns * R, F)
    chunk, cV = ((nf, tok, F), F32, HBM), V((nf, tok, F), F32)
    ins = dict(x_in=(x, HBM), w_in=(w, HBM), vec_in=(vec, INV))
    outs = dict(
        normed_out=((tok, D), BF16, HBM), wq0_out=(wshape, BF16, HBM), wq1_out=(wshape, BF16, HBM),
        x1g_out=((nb, nf, tok, F), BF16, HBM),
        x1_out=chunk, xo_out=chunk, f_out=chunk, c_out=chunk, r_out=chunk, cell_out=chunk,
        inc_out=((nf, nb, dm.runs, F), F32, INV), runA_out=((nf, nb, dm.runs, F), F32, INV), tot_out=((nf, ns, 2, dm.runs, F), F32, INV),
        vec_out=((16, D), F32, INV), mu_out=((tok, F), F32, INV), rstd_out=((tok, F), F32, INV),
    )
    scratch = dict(
        xg=V((nb, dm.local, D), BF16), normed=V((tok, D), BF16), wq0=V(wshape, BF16),
        vecg=V((nb, ns, 16, F), F32), vec=V((16, D), F32),
        xS=cV, fS=cV, cS=cV, rS=cV, cellS=cV, hS=cV, hb=V((nf, tok, F), BF16),
        incS=V((nf, nb, dm.runs, F), F32), tot=V((nf, ns, 2, dm.runs, F), F32),
        pre_s=DMA((L, nf, nb)), pre_r=DMA((L, nf, nb)), z_s=DMA((L, nf, outer, 2)), z_r=DMA((L, nf, outer)),
        y_s=DMA((L, nf, outer, inner)), y_r=DMA((L, nf, outer, inner)),
        vp_s=DMA((nb,)), vp_r=DMA((nb,)), vz_s=DMA((outer,)), vz_r=DMA((outer,)),
        vy_s=DMA((outer, inner)), vy_r=DMA((outer, inner)),
        xx_s=DMA((4,)), xx_r=DMA((4,)), xc_s=DMA, xc_r=DMA, xl_s=DMA((4,)), xl_r=DMA((4,)),
        h_s=DMA((nf,)), h_r=DMA((nf,)), hc_s=DMA((nf,)), hc_r=DMA((nf,)), hl_s=DMA((nf,)), hl_r=DMA((nf,)),
        loc=DMA((2 * nf + 1,)), own_sem=DMA((L, nf, 3)), out_sem=DMA((nf, 7)),
        runA=V((nf, nb, dm.runs, F), F32), runV=V((nf, nb, dm.runs, F), F32),
        **scan_scratch(dm),
    )
    return launch(dm, "forward_one", 0, kernel_one, ins, outs, scratch)


def kernel_two(dm, r):
    n = Net(dm)
    nb, nf = dm.nb, dm.nf
    b, s = n.b, n.s
    w1 = Gather(dm, n, r, 1, r.wq)
    NA = dm.early
    x_copy = local_copy(r.x1_in, r.xS, r.loc.at[0])
    w_copy = []
    for fc in range(NA):
        w_copy.append(local_copy(r.w_in.at[fc], r.wq.at[fc], r.w_sem.at[fc, 0]))
    w_late, y_sends = [], {fc: [] for fc in range(NA, nf)}
    for fc in range(NA, nf):
        for o in range(dm.outer):
            rows = pl.ds(pl.multiple_of((o * dm.inner + n.y) * dm.rows, dm.rows), dm.rows)
            at = (fc, slice(None), slice(None), rows)
            for p in n.inner_peers:
                y_sends[fc].append(
                    remote(r.w_in.at[at], r.wq.at[at], r.y_s.at[1, fc, o, p], r.y_r.at[1, fc, o, n.y], (b, n.z * dm.inner + p))
                )
            w_late.append(local_copy(r.w_in.at[at], r.wq.at[at], r.w_sem.at[fc, o]))

    def cot_send(p):
        cols = pl.ds(at128(p * dm.q), dm.q)
        at = r.cot.at[pl.ds(pl.multiple_of(b * dm.local, dm.local), dm.local)]
        return remote(r.cot_in.at[:, cols], at, r.c_s.at[p], r.c_r.at[b], (p, s))

    cot_copy = local_copy(
        r.cot_in.at[:, pl.ds(at128(b * dm.q), dm.q)], r.cot.at[pl.ds(pl.multiple_of(b * dm.local, dm.local), dm.local)], r.loc.at[1]
    )
    TT, TILE = 256, 32

    def fetch(k):
        return pltpu.make_async_copy(r.x1g_in.at[:, :, pl.ds(k * TT, TT)], r.xt.at[k % 2], r.xt_sem.at[k % 2])

    fetch(0).start()
    r.need("vec")
    n.ready()
    for c in y_sends[NA]:
        c.start()
    for p in n.batch_peers:
        cot_send(p).start()
    for k in range(dm.tok // TT):
        if (k + 1) * TT < dm.tok:
            fetch(k + 1).start()
        fetch(k).wait()

        def step(i, carry, k=k):
            rows = pl.ds(pl.multiple_of(i * TILE, TILE), TILE)
            x = jnp.concatenate([r.xt[k % 2, q, fc, rows, :] for q in range(nb) for fc in range(nf)], axis=1).astype(F32)
            mu, rstd, normed = norm_rows(x, r.vec[5:6, :])
            every = pl.ds(pl.multiple_of(k * TT + i * TILE, TILE), TILE)
            r.normed[every, :] = normed
            r.mu_out[every, :] = jnp.broadcast_to(mu, (TILE, F))
            r.rstd_out[every, :] = jnp.broadcast_to(rstd, (TILE, F))
            return carry

        lax.fori_loop(0, TT // TILE, step, 0)
    normed_copy = local_copy(r.normed, r.normed_out, r.xt_sem.at[0])
    r.store("mu_out")
    r.store("rstd_out")
    for c in [x_copy, cot_copy] + w_copy:
        c.wait()

    def p1(fcs):
        products(dm, r, n, r.wq, fcs, 5, None)
        for fc in fcs:
            scan_totals(dm, r, n, fc)

    pend = []

    def p2(fc):
        scan_finish(dm, r, n, fc, 5)
        r.hb[fc] = r.hS[fc].astype(BF16)
        pend.append(local_copy(r.hb.at[fc], r.h_out.at[fc], r.out_sem.at[fc, 2]))
        r.dhS[fc] = r.cot[:, fc * F : (fc + 1) * F].astype(F32)
        back_totals(dm, r, n, fc, 5)

    def p3(fc):
        back_finish(dm, r, n, fc, 5)
        pend.extend(back_outputs(dm, r, fc))

    p1((0, 1))
    for fc in range(NA + 1, nf):
        for c in y_sends[fc]:
            c.start()
    for p in n.batch_peers:
        arrived(r.cot.at[pl.ds(pl.multiple_of(p * dm.local, dm.local), dm.local)], r.c_r.at[p], (p, s))
    p2(0)
    p2(1)
    for c in w_late:
        c.wait()
    for fc in range(NA, nf):
        w1.complete(fc)
        p1((fc,))
    pend.append(local_copy(r.wq, r.wq_out, r.loc.at[0]))
    for fc in range(NA, nf):
        p2(fc)
    for fc in range(nf):
        p3(fc)
    r.store("vsum_out")
    for c in pend:
        c.wait()
    normed_copy.wait()
    for p in n.batch_peers:
        cot_send(p).wait_send()
    for fc in range(NA, nf):
        w1.drain_inner(fc)
    totals_sent(dm, r, n)
    back_sent(dm, r, n)


def call_two(dm, one, cot):
    nb, ns, nf = dm.nb, dm.ns, dm.nf
    tok = dm.tok
    cV = V((nf, tok, F), F32)
    ins = dict(
        w_in=(one.wq1_out, HBM), x1_in=(one.x1_out, HBM), cot_in=(cot, HBM),
        x1g_in=(one.x1g_out, HBM), vec=(one.vec_out, INV),
    )
    outs = dict(
        wq_out=((nf, 3, nb, ns * dm.rows, F), BF16, HBM),
        normed_out=((tok, dm.d), BF16, HBM), h_out=((nf, tok, F), BF16, HBM),
        dmixed_out=((nf, 3, tok, F), BF16, HBM), dtail_out=((nf, tok, F), F32, HBM),
        vsum_out=((nf, 4, dm.runs, F), F32, INV), mu_out=((tok, F), F32, INV), rstd_out=((tok, F), F32, INV),
    )
    scratch = dict(
        wq=V((nf, 3, nb, ns * dm.rows, F), BF16), cot=V((tok, dm.q), BF16), xt=V((2, nb, nf, 256, F), BF16),
        normed=V((tok, dm.d), BF16), dmixed=V((nf, 3, tok, F), BF16),
        xS=cV, fS=cV, cS=cV, rS=cV, cellS=cV, drS=cV, hS=cV, hb=V((nf, tok, F), BF16),
        incS=V((nf, nb, dm.runs, F), F32), tot=V((nf, ns, 2, dm.runs, F), F32),
        bk=V((nf, ns, dm.runs, F), F32), bkS=V((nf, dm.runs, F), F32), backV=V((nf, nb, dm.runs, F), F32),
        runA=V((nf, nb, dm.runs, F), F32), runV=V((nf, nb, dm.runs, F), F32),
        k_s=DMA((nf, ns)), k_r=DMA((nf, ns)),
        c_s=DMA((nb,)), c_r=DMA((nb,)), w_sem=DMA((nf, dm.outer)),
        y_s=DMA((2, nf, dm.outer, dm.inner)), y_r=DMA((2, nf, dm.outer, dm.inner)),
        loc=DMA((2,)), xt_sem=DMA((2,)), out_sem=DMA((nf, 3)),
        **scan_scratch(dm),
    )
    alias = dict(scratch)

    def kernel(dm, r):
        r.dhS = r.hS
        kernel_two(dm, r)

    return launch(dm, "layer_two", 1, kernel, ins, outs, alias)


def kernel_three(dm, r):
    n = Net(dm)
    nf = dm.nf
    loads = []
    for fc in range(nf):
        pairs = [(r.f_in.at[fc], r.fS), (r.c_in.at[fc], r.cS), (r.r_in.at[fc], r.rS), (r.cell_in.at[fc], r.cellS),
                 (r.xo_in.at[fc], r.xS), (r.dh_in.at[:, pl.ds(fc * F, F)], r.dhS)]
        loads.append([local_copy(src, dst.at[fc], r.loc.at[fc, k]) for k, (src, dst) in enumerate(pairs)])
    rs = Scatter(dm, n, r, dm.on_time)
    late = range(dm.on_time, rs.count)
    b, s = n.b, n.s

    def block_send(fc, p):
        cols = pl.ds(at128(b * dm.q + fc * F), F)
        src = r.h_in.at[fc, pl.ds(pl.multiple_of(p * dm.local, dm.local), dm.local)]
        return remote(src, r.block_out.at[:, cols], r.o_s.at[fc, p], r.o_r.at[fc, b], (p, s))

    pend = []
    for fc in range(nf):
        cols = pl.ds(at128(b * dm.q + fc * F), F)
        src = r.h_in.at[fc, pl.ds(pl.multiple_of(b * dm.local, dm.local), dm.local)]
        pend.append(local_copy(src, r.block_out.at[:, cols], r.out_sem.at[fc, 2]))
    r.need("wg")
    n.ready()
    rs.start(late[0])
    for fc in range(nf):
        for p in n.batch_peers:
            block_send(fc, p).start()
    r.need("vec", "incS", "runA", "tot")
    for fc in range(nf):
        for c in loads[fc]:
            c.wait()
        back_totals(dm, r, n, fc, 0)
    for ch in late[1:]:
        rs.start(ch)
    rs.mid(late[0])
    for fc in range(nf):
        back_finish(dm, r, n, fc, 0)
        pend.extend(back_outputs(dm, r, fc))
        if 0 < fc < len(late):
            rs.mid(late[fc])
            rs.last(late[fc - 1])
    rs.last(late[-1])
    r.store("vsum_out")
    r.need("fr_early")
    rs.assemble(r.fr_early)
    r.store("wg_out")
    for c in pend:
        c.wait()
    back_sent(dm, r, n)
    for fc in range(nf):
        for p in n.batch_peers:
            block_send(fc, p).wait_send()
            arrived(r.block_out.at[:, pl.ds(at128(p * dm.q + fc * F), F)], r.o_r.at[fc, p], (p, s))
    rs.drain(late)


def call_three(dm, one, two, g1):
    nb, ns, nf, tok = dm.nb, dm.ns, dm.nf, dm.tok
    cV = V((nf, tok, F), F32)
    ins = dict(
        f_in=(one.f_out, HBM), c_in=(one.c_out, HBM), r_in=(one.r_out, HBM), cell_in=(one.cell_out, HBM),
        xo_in=(one.xo_out, HBM), dh_in=(g1.dx_out, HBM), vec=(one.vec_out, INV), incS=(one.inc_out, INV),
        runA=(one.runA_out, INV), tot=(one.tot_out, INV), wg=(g1.late_out, INV), fr_early=(g1.fr_out, INV),
        h_in=(two.h_out, HBM),
    )
    outs = dict(
        block_out=((dm.local, dm.d), BF16, HBM),
        dmixed_out=((nf, 3, tok, F), BF16, HBM), dtail_out=((nf, tok, F), F32, HBM), vsum_out=((nf, 4, dm.runs, F), F32, INV),
        wg_out=((dm.rows, 3 * dm.d), F32, INV),
    )
    scratch = dict(
        dmixed=V((nf, 3, tok, F), BF16), xS=cV, fS=cV, cS=cV, rS=cV, cellS=cV, drS=cV, dhS=cV,
        bk=V((nf, ns, dm.runs, F), F32), bkS=V((nf, dm.runs, F), F32), backV=V((nf, nb, dm.runs, F), F32),
        k_s=DMA((nf, ns)), k_r=DMA((nf, ns)), loc=DMA((nf, 6)), out_sem=DMA((nf, 3)), o_s=DMA((nf, nb)), o_r=DMA((nf, nb)),
        fr=V((nb, 3, dm.rows, dm.q), BF16), **scatter_scratch(dm, 3 * nb - dm.on_time),
    )
    return launch(dm, "layer_one_back", 2, kernel_three, ins, outs, scratch)


class Scatter:
    def __init__(self, dm, n, r, lo):
        self.dm, self.n, self.r, self.lo = dm, n, r, lo
        self.H = 3
        self.count = dm.nb * self.H

    def strip(self, ch, pos):
        R = self.dm.rows
        return self.r.wg.at[ch - self.lo, pl.ds(pl.multiple_of(pos * R, R), R)]

    def y_copy(self, ch, j, o):
        n, r, I, k = self.n, self.r, self.dm.inner, ch - self.lo
        p = lax.rem(n.y + j, I)
        return remote(
            self.strip(ch, o * I + p), r.yr.at[k, I - j - 1, o], r.ry_s.at[k, j - 1, o], r.ry_r.at[k, I - j - 1, o], (n.b, n.z * I + p)
        )

    def z_copy(self, ch, j):
        n, r, O, k = self.n, self.r, self.dm.outer, ch - self.lo
        p = lax.rem(n.z + j, O)
        return remote(
            r.zs.at[k, p], r.zr.at[k, O - j - 1], r.rz_s.at[k, j - 1], r.rz_r.at[k, O - j - 1], (n.b, p * self.dm.inner + n.y)
        )

    def f_copy(self, ch):
        n, r, k = self.n, self.r, ch - self.lo
        return remote(r.fs.at[k], r.fr.at[n.b, ch % self.H], r.rf_s.at[k], r.rf_r.at[n.b, ch % self.H], (ch // self.H, n.s))

    def start(self, ch):
        for j in range(1, self.dm.inner):
            for o in range(self.dm.outer):
                self.y_copy(ch, j, o).start()

    def mid(self, ch):
        n, r, dm, k = self.n, self.r, self.dm, ch - self.lo
        for j in range(1, dm.inner):
            for o in range(dm.outer):
                arrived(r.yr.at[k, j - 1, o], r.ry_r.at[k, j - 1, o], (n.b, n.s))
        for jz in range(dm.outer):
            o = lax.rem(n.z + jz + 1, dm.outer)
            pos = pl.ds(pl.multiple_of((o * dm.inner + n.y) * dm.rows, dm.rows), dm.rows)
            total = r.wg[k, pos, :].astype(F32)
            for j in range(1, dm.inner):
                total = total + r.yr[k, j - 1, o].astype(F32)
            r.zs[k, o] = total.astype(BF16)
            if jz + 1 < dm.outer:
                self.z_copy(ch, jz + 1).start()

    def last(self, ch):
        n, r, dm, k = self.n, self.r, self.dm, ch - self.lo
        for j in range(1, dm.outer):
            arrived(r.zr.at[k, j - 1], r.rz_r.at[k, j - 1], (n.b, n.s))
        total = r.zs[k, n.z].astype(F32)
        for j in range(1, dm.outer):
            total = total + r.zr[k, j - 1].astype(F32)
        r.fs[k] = total.astype(BF16)
        pl.when(n.b != ch // self.H)(lambda: self.f_copy(ch).start())

        @pl.when(n.b == ch // self.H)
        def _():
            r.fr[n.b, ch % self.H] = r.fs[k]

    def receive(self, chunks):
        n, r = self.n, self.r
        for ch in chunks:

            @pl.when(n.b == ch // self.H)
            def _(ch=ch):
                for p in n.batch_peers:
                    arrived(r.fr.at[p, ch % self.H], r.rf_r.at[p, ch % self.H], (p, n.s))

    def assemble(self, early=None):
        n, r, dm = self.n, self.r, self.dm
        self.receive(range(self.lo, self.count))
        for h in range(self.H):
            here = n.b * self.H + h >= self.lo
            for k in range(dm.nb):
                to = h * dm.d + k * dm.q

                @pl.when(here)
                def _(h=h, k=k, to=to):
                    r.wg_out[:, to : to + dm.q] = r.fr[k, h].astype(F32)

                if early is not None:

                    @pl.when(jnp.logical_not(here))
                    def _(h=h, k=k, to=to):
                        r.wg_out[:, to : to + dm.q] = early[k, h].astype(F32)

    def drain(self, chunks):
        for ch in chunks:
            for j in range(1, self.dm.inner):
                for o in range(self.dm.outer):
                    self.y_copy(ch, j, o).wait_send()
            for j in range(1, self.dm.outer):
                self.z_copy(ch, j).wait_send()
            pl.when(self.n.b != ch // self.H)(lambda ch=ch: self.f_copy(ch).wait_send())


def scatter_scratch(dm, count):
    inner, outer, R, q = dm.inner, dm.outer, dm.rows, dm.q
    return dict(
        yr=V((count, inner - 1, outer, R, q), BF16), zs=V((count, outer, R, q), BF16), zr=V((count, outer - 1, R, q), BF16),
        fs=V((count, R, q), BF16),
        ry_s=DMA((count, inner - 1, outer)), ry_r=DMA((count, inner - 1, outer)),
        rz_s=DMA((count, outer - 1)), rz_r=DMA((count, outer - 1)), rf_s=DMA((count,)), rf_r=DMA((dm.nb, 3)),
    )


def kernel_grads(first, dm, r):
    n = Net(dm)
    nb, nf, q, tok = dm.nb, dm.nf, dm.q, dm.tok
    b, s = n.b, n.s
    base = 0 if first else 5
    NT = nb
    TR = tok // NT
    PER = TR // F
    rs = Scatter(dm, n, r, 0)
    H, NCH = rs.H, rs.count
    mine = range(NCH if first else dm.on_time)
    dm_load = local_copy(r.dm_in, r.dmS, r.loc.at[0])
    n_load = [local_copy(r.normed_in.at[:, pl.ds(k * q, q)], r.nS.at[:, pl.ds(k * q, q)], r.n_sem.at[k]) for k in range(nb)]
    w_load = local_copy(r.w_in, r.wS, r.loc.at[1])
    half = nb // 2
    order = [j + half * k for j in range(half) for k in range(2)]

    def fetch(k):
        rows, slot = pl.ds(order[k] * TR, TR), k % 2
        return [
            pltpu.make_async_copy(r.x_in.at[:, rows], r.xt.at[slot], r.tile_sem.at[slot, 0]),
            pltpu.make_async_copy(r.dtail_in.at[:, rows], r.dt.at[slot], r.tile_sem.at[slot, 1]),
            pltpu.make_async_copy(r.mu_in.at[rows], r.mt.at[slot], r.tile_sem.at[slot, 2]),
            pltpu.make_async_copy(r.rstd_in.at[rows], r.rt.at[slot], r.tile_sem.at[slot, 3]),
        ]

    def part(quarter, c):
        left = jnp.concatenate([r.dmS[fc, g, c * TR : (c + 1) * TR, :] for fc in range(nf) for g in range(3)], axis=1)
        right = jnp.concatenate([r.wS[fc, g, quarter] for fc in range(nf) for g in range(3)], axis=1)
        return lax.dot_general(left, right, (((1,), (1,)), ((), ())), preferred_element_type=F32)

    def to_sib(buf, got, c, i):
        return remote(buf.at[c], got.at[c], r.p_s.at[i, c], r.p_r.at[i, c], (n.sib, s))

    def to_across(c):
        return remote(r.pb.at[c], r.prb.at[c], r.p_s.at[1, c], r.p_r.at[1, c], (n.across, s))

    def sums_of(k, v, quarter, fresh=False):
        c = order[k]
        cols = pl.ds(at128(quarter * q), q)
        t1 = v * r.vec[base : base + 1, cols]
        t2 = v * r.nS[c * TR : (c + 1) * TR, cols].astype(F32)
        for j, t in enumerate((t1, t2)):
            total = t[:, :F]
            for fc in range(1, nf):
                total = total + t[:, fc * F : (fc + 1) * F]
            r.rows[j] = total if fresh else r.rows[j] + total

    def stage(k, between=None):
        c = order[k]
        v = part(n.diag, c)
        r.pa[c] = v.astype(BF16)
        to_sib(r.pa, r.pra, c, 0).start()
        sums_of(k, v, n.diag, True)
        v = part(b, c)
        r.acc[c * TR : (c + 1) * TR, :] = v
        sums_of(k, v, b)
        if between is not None:
            between()
        to_sib(r.pa, r.pra, c, 0).wait_send()
        v = part(n.sib, c)
        r.pa[c] = v.astype(BF16)
        to_sib(r.pa, r.prc, c, 2).start()
        sums_of(k, v, n.sib)
        v = part(n.across, c)
        sums_of(k, v, n.across)
        for i in range(PER):
            for j in range(2):
                r.st[b, k, j, i : i + 1, :] = jnp.sum(r.rows[j, i * F : (i + 1) * F, :].T, axis=0, keepdims=True)
        for p in n.batch_peers:
            stats_copy(k, p).start()
        arrived(r.pra.at[c], r.p_r.at[0, c], (n.sib, s))
        r.pb[c] = (v + r.pra[c].astype(F32)).astype(BF16)
        to_across(c).start()

    def wgrad(ch, begin=None):
        bb, h = ch // H, ch % H
        right = jnp.concatenate([r.dmS[fc, h] for fc in range(nf)], axis=1)
        r.wg[ch] = lax.dot_general(
            r.nS[:, bb * q : (bb + 1) * q], right, (((0,), (0,)), ((), ())), preferred_element_type=F32
        ).astype(BF16)
        if begin is not None:
            begin()
        if ch in mine:
            rs.start(ch)

    def mid(ch):
        if ch in mine:
            rs.mid(ch)

    def last(ch):
        if ch in mine:
            rs.last(ch)

    def gain(fc):
        return vrow(dm, r, n, base, fc)

    def stats_copy(k, p):
        return remote(r.st.at[b, k], r.st.at[b, k], r.st_s.at[k, p], r.st_r.at[k, b], (p, s))

    pend = []

    def final(k):
        c, slot = order[k], k % 2
        for p in n.batch_peers:
            arrived(r.st.at[p, k], r.st_r.at[k, p], (p, s))
        arrived(r.prc.at[c], r.p_r.at[2, c], (n.sib, s))
        arrived(r.prb.at[c], r.p_r.at[1, c], (n.across, s))
        for copy in fetch(k):
            copy.wait()
        if first:
            to_across(c).wait_send()

        def step(i, sums):
            near = pl.ds(pl.multiple_of(i * F, F), F)
            rows = pl.ds(pl.multiple_of(c * TR + i * F, F), F)
            mu, rstd = r.mt[slot, near, :], r.rt[slot, near, :]
            means = []
            for j in range(2):
                total = r.st[0, k, j, pl.ds(i, 1), :]
                for m in range(1, nb):
                    total = total + r.st[m, k, j, pl.ds(i, 1), :]
                means.append(jnp.broadcast_to(total * (1.0 / dm.d), (F, F)).T)
            new = []
            for fc in range(nf):
                cols = slice(fc * F, (fc + 1) * F)
                dn = r.acc[rows, cols] + r.prc[c, near, cols].astype(F32) + r.prb[c, near, cols].astype(F32)
                xhat = (r.xt[slot, fc, near, :] - mu) * rstd
                new.append(sums[fc] + jnp.sum((dn * xhat).reshape(F // 8, 8, F), axis=0))
                out = r.dt[slot, fc, near, :] + rstd * (dn * gain(fc) - means[0] - xhat * means[1])
                if first:
                    r.pb[c, near, cols] = out.astype(BF16)
                else:
                    r.acc[rows, cols] = out
            return tuple(new)

        sums = lax.fori_loop(0, PER, step, tuple(jnp.zeros((8, F), F32) for _ in range(nf)))
        for fc in range(nf):
            r.gsum[fc] = sums[fc] if k == 0 else r.gsum[fc] + sums[fc]
        if k + 2 < NT:
            for copy in fetch(k + 2):
                copy.start()
        if first:
            pl.when(b != c)(lambda: to_owner(c).start())
        else:
            rows = pl.ds(c * TR, TR)
            pend.append(local_copy(r.acc.at[rows], r.dx_out.at[rows], r.loc.at[3 + c]))

    def to_owner(c):
        return remote(r.pb.at[c], r.fin.at[b], r.g_s.at[c], r.g_r.at[b], (c, s))

    dm_load.wait()
    n_load[0].wait()
    wgrad(0, n.ready)
    wgrad(1)
    wgrad(2)
    r.need("vec")
    for c in n_load[1:] + [w_load]:
        c.wait()
    stage(0, lambda: mid(0))
    for k in range(2):
        for copy in fetch(k):
            copy.start()
    wgrad(3)
    stage(1, lambda: mid(1))
    wgrad(4)
    mid(2)
    stage(2)
    wgrad(5)
    stage(3, lambda: mid(3))
    wgrad(6)
    mid(4)
    for ch in range(3):
        last(ch)
    final(0)
    wgrad(7)
    mid(5)
    last(3)
    final(1)
    wgrad(8)
    last(4)
    mid(6)
    wgrad(9)
    last(5)
    mid(7)
    final(2)
    wgrad(10)
    last(6)
    mid(8)
    wgrad(11)
    last(7)
    final(3)
    mid(9)
    if not first:
        r.late[...] = r.wg[dm.on_time :]
        pend.append(local_copy(r.late, r.late_out, r.loc.at[0]))
    if first:
        vector_start(dm, r, n)
    else:
        r.store("gsum")
    last(8)
    mid(10)
    last(9)
    mid(11)
    last(10)
    if first:

        r.fin[b] = r.pb[b]
        for k in range(nb):

            @pl.when(k != b)
            def _(k=k):
                arrived(r.fin.at[k], r.g_r.at[k], (b, s))

            r.acc[k * TR : (k + 1) * TR, :] = r.fin[k].astype(F32)
            pend.append(local_copy(r.acc.at[pl.ds(k * TR, TR)], r.dx_out.at[:, pl.ds(k * q, q)], r.loc.at[3 + k]))
    if first:
        vector_finish(dm, r, n)
    last(11)
    if first:
        rs.assemble()
        r.store("wg_out")
    else:
        rs.receive(mine)
        pend.append(local_copy(r.fr, r.fr_out, r.loc.at[1]))
    for c in pend:
        c.wait()
    for k in range(NT):
        c = order[k]
        to_sib(r.pa, r.prc, c, 2).wait_send()
        if first:
            pl.when(b != c)(lambda c=c: to_owner(c).wait_send())
        else:
            to_across(c).wait_send()
        for p in n.batch_peers:
            stats_copy(k, p).wait_send()
    rs.drain(mine)


def vector_start(dm, r, n):
    r.need("vsum0", "vsum1", "gsum1")
    r.vg[n.s] = jnp.zeros((16, dm.q), F32)
    for l, (vs, gs) in enumerate(((r.vsum0, r.gsum), (r.vsum1, r.gsum1))):
        for fc in range(dm.nf):
            cols = slice(fc * F, (fc + 1) * F)
            r.vg[n.s, 5 * l : 5 * l + 1, cols] = jnp.sum(gs[fc], axis=0, keepdims=True)
            for k in range(4):
                r.vg[n.s, 5 * l + 1 + k : 5 * l + 2 + k, cols] = jnp.sum(vs[fc, k], axis=0, keepdims=True)
    for p in n.seq_peers:
        remote(r.vg.at[n.s], r.vg.at[n.s], r.v_s.at[p], r.v_r.at[n.s], (n.b, p)).start()


def vector_finish(dm, r, n):
    for p in n.seq_peers:
        arrived(r.vg.at[p], r.v_r.at[p], (n.b, p))
    total = r.vg[0]
    for j in range(1, dm.ns):
        total = total + r.vg[j]
    r.vg_out[...] = total
    r.store("vg_out")
    for p in n.seq_peers:
        sent(r.vg.at[n.s], r.v_s.at[p], (n.b, p))


def call_grads(dm, first, w, normed, x, mu, rstd, vec, scans, more):
    nb, ns, nf, R, q, tok = dm.nb, dm.ns, dm.nf, dm.rows, dm.q, dm.tok
    TR, H = tok // nb, 3
    NCH = nb * H
    late = NCH - dm.on_time
    ins = dict(
        dm_in=(scans.dmixed_out, HBM), w_in=(w, HBM), normed_in=(normed, HBM), x_in=(x, HBM),
        dtail_in=(scans.dtail_out, HBM), mu_in=(mu, HBM), rstd_in=(rstd, HBM), vec=(vec, INV),
    )
    bV = V((nb, TR, q), BF16)
    scratch = dict(
        dmS=V((nf, 3, tok, F), BF16), wS=V((nf, 3, nb, ns * R, F), BF16), nS=V((tok, dm.d), BF16),
        acc=V((tok, q), F32), pa=bV, pra=bV, pb=bV, prb=bV, prc=bV,
        wg=V((NCH, ns * R, q), BF16), fr=V((nb, H, R, q), BF16), **scatter_scratch(dm, NCH if first else dm.on_time),
        xt=V((2, nf, TR, F), F32), dt=V((2, nf, TR, F), F32), mt=V((2, TR, F), F32), rt=V((2, TR, F), F32),
        st=V((nb, nb, 2, TR // F, F), F32), rows=V((2, TR, F), F32),
        loc=DMA((3 + nb,)), n_sem=DMA((nb,)), tile_sem=DMA((2, 4)), p_s=DMA((3, nb)), p_r=DMA((3, nb)),
        st_s=DMA((nb, nb)), st_r=DMA((nb, nb)),
    )
    if first:
        outs = dict(wg_out=((R, 3 * dm.d), F32, INV), dx_out=((dm.local, dm.d), F32, HBM), vg_out=((16, q), F32, INV))
        ins.update({k: (v, INV) for k, v in more.items()})
        scratch.update(
            dict(fin=bV, g_s=DMA((nb,)), g_r=DMA((nb,)), vg=V((ns, 16, q), F32), v_s=DMA((ns,)), v_r=DMA((ns,)),
             gsum=V((nf, 8, F), F32))
        )
    else:
        outs = dict(
            dx_out=((tok, q), F32, HBM), gsum=((nf, 8, F), F32, INV), fr_out=((nb, H, R, q), BF16, HBM),
            late_out=((late, ns * R, q), BF16, HBM),
        )
        scratch["late"] = V((late, ns * R, q), BF16)
    return launch(dm, "grads_one" if first else "grads_two", 3 if first else 4, functools.partial(kernel_grads, first), ins, outs, scratch)


def prepare(dm, block_input, weight, vectors, cotangent):
    D, nf, nb, R = dm.d, dm.nf, dm.nb, dm.rows
    x, cot = [v.reshape(dm.runs, dm.length, D).swapaxes(0, 1).reshape(dm.local, D) for v in (block_input, cotangent)]
    s = lax.axis_index("seq")
    v = jnp.pad(vectors.reshape(dm.layers * 5, R), ((0, 16 - dm.layers * 5), (0, 0)))
    lane = lax.broadcasted_iota(jnp.int32, (16, F), 1) // R
    v = jnp.where(lane == lax.rem(s, F // R), jnp.tile(v, (1, F // R)), 0.0)
    return x, weight, v, cot


def natural(dm, v, shape):
    return v.reshape(dm.length, dm.runs, dm.d).swapaxes(0, 1).reshape(shape)


def tuned_body(nb, ns, block_input, weight, vectors, cotangent):
    dm = Dims(nb, ns, block_input.shape, weight.shape)
    x, w, vec, cot = prepare(dm, block_input, weight, vectors, cotangent)
    one = call_one(dm, x, w, vec)
    two = call_two(dm, one, cot)
    g1 = call_grads(dm, False, two.wq_out, two.normed_out, one.x1_out, two.mu_out, two.rstd_out, one.vec_out, two, {})
    three = call_three(dm, one, two, g1)
    more = dict(vsum0=three.vsum_out, vsum1=two.vsum_out, gsum1=g1.gsum)
    g0 = call_grads(dm, True, one.wq0_out, one.normed_out, one.xo_out, one.mu_out, one.rstd_out, one.vec_out, three, more)
    weight_grad = jnp.stack([g0.wg_out, three.wg_out], axis=0)
    s = lax.axis_index("seq")
    mine = lax.dynamic_slice_in_dim(g0.vg_out, s * dm.rows, dm.rows, axis=1)[: dm.layers * 5]
    vector_grad = mine.reshape(dm.layers, 5, dm.rows)
    return (
        natural(dm, three.block_out, block_input.shape), natural(dm, g0.dx_out, block_input.shape), weight_grad, vector_grad,
    )


def prefix(value, axis, join, neutral, backward):
    count, mine = (lax.axis_size(axis), lax.axis_index(axis))
    pieces = jax.tree.map(lambda part: lax.all_gather(part, axis), value)
    if backward:
        pieces = jax.tree.map(lambda part: part[::-1], pieces)
        mine = count - 1 - mine
    subtotal = jax.tree.map(
        lambda part, zero: jnp.full_like(part, 0) + jnp.asarray(zero, part.dtype), value, neutral
    )

    def step(position, subtotal):
        longer = join(subtotal, jax.tree.map(lambda part: part[position], pieces))
        return jax.tree.map(lambda new, old: jnp.where(position < mine, new, old), longer, subtotal)

    return lax.fori_loop(0, count - 1, step, subtotal)


def compose(earlier, later):
    return (later[0] * earlier[0], later[0] * earlier[1] + later[1])


def rebuild_forward(stream, full, vec):
    norm_scale, vforget, bforget = (vec[0], vec[1], vec[2])
    sequence_batch, time_steps, hidden_width = stream.shape
    center = jnp.mean(stream, axis=-1, keepdims=True)
    shifted_input = stream - center
    inverse_deviation = lax.rsqrt(
        jnp.mean(shifted_input * shifted_input, axis=-1, keepdims=True) + epsilon
    )
    centered_input = shifted_input * inverse_deviation
    normed_input = (
        (centered_input * norm_scale)
        .astype(jnp.bfloat16)
        .reshape(sequence_batch * time_steps, hidden_width)
    )
    mixed = jnp.dot(normed_input, full, preferred_element_type=jnp.float32).reshape(
        sequence_batch, time_steps, 3 * hidden_width
    )
    candidate_value = mixed[..., :hidden_width]
    reset_input = mixed[..., 2 * hidden_width :]
    forget_gate = jax.nn.sigmoid(
        mixed[..., hidden_width : 2 * hidden_width] + vforget * stream + bforget
    )
    gate_values, norm_bias = lax.associative_scan(
        compose, (forget_gate, (1.0 - forget_gate) * candidate_value), axis=1
    )
    return (
        centered_input,
        inverse_deviation,
        normed_input,
        candidate_value,
        reset_input,
        forget_gate,
        gate_values,
        norm_bias,
    )


def finish(vec, reset_input, gate_values, norm_bias, incoming):
    vreset, breset = (vec[3], vec[4])
    cells = gate_values * incoming[:, None, :] + norm_bias
    previous = jnp.concatenate([incoming[:, None, :], cells[:, :-1]], axis=1)
    reset = jax.nn.sigmoid(reset_input + vreset * previous + breset)
    return (cells, previous, reset)


def general_body(block_input, weight, vectors, cotangent):
    sequence_batch, time_steps, hidden_width = block_input.shape
    layers = weight.shape[0]
    params = lax.all_gather(vectors, ("batch", "seq"), axis=2, tiled=True)
    stream = block_input.astype(jnp.float32)
    ones = jnp.ones((sequence_batch, hidden_width), jnp.float32)
    zeros = jnp.zeros((sequence_batch, hidden_width), jnp.float32)
    inputs = []
    entering = []
    for layer in range(layers):
        full = lax.all_gather(weight[layer], ("batch", "seq"), axis=0, tiled=True)
        vec = params[layer]
        pieces = rebuild_forward(stream, full, vec)
        gate_values, norm_bias = (pieces[6], pieces[7])
        arrived = prefix(
            (gate_values[:, -1], norm_bias[:, -1]), "seq", compose, (ones, zeros), False
        )
        incoming = arrived[1]
        cells, previous, reset = finish(vec, pieces[4], gate_values, norm_bias, incoming)
        inputs.append(stream)
        entering.append(incoming)
        stream = reset * cells + (1.0 - reset) * stream
    block_output = stream.astype(jnp.bfloat16)
    grad_out = cotangent.astype(jnp.float32)
    weight_grads = [None] * layers
    vector_terms = [None] * layers
    rows = weight.shape[1]
    for layer in reversed(range(layers)):
        full = lax.all_gather(weight[layer], ("batch", "seq"), axis=0, tiled=True)
        vec = params[layer]
        norm_scale, vforget, vreset = (vec[0], vec[1], vec[3])
        stream = inputs[layer]
        (
            centered_input,
            inverse_deviation,
            normed_input,
            candidate_value,
            reset_input,
            forget_gate,
            gate_values,
            norm_bias,
        ) = rebuild_forward(stream, full, vec)
        cells, previous, reset = finish(vec, reset_input, gate_values, norm_bias, entering[layer])
        dreset = grad_out * (cells - stream) * reset * (1.0 - reset)
        direct = grad_out * reset
        inject = forget_gate * direct + dreset * vreset
        back_gates, back_offsets = lax.associative_scan(
            compose, (jnp.flip(forget_gate, 1), jnp.flip(inject, 1)), axis=1
        )
        back_gates = jnp.flip(back_gates, 1)
        back_offsets = jnp.flip(back_offsets, 1)
        arrived = prefix(
            (back_gates[:, 0], back_offsets[:, 0]), "seq", compose, (ones, zeros), True
        )
        later = arrived[1]
        carried = back_gates * later[:, None, :] + back_offsets
        following = jnp.concatenate([carried[:, 1:], later[:, None, :]], axis=1)
        dcell = direct + following
        dcandidate = dcell * (1.0 - forget_gate)
        dforget = dcell * (previous - candidate_value) * forget_gate * (1.0 - forget_gate)
        dmixed = jnp.concatenate([dcandidate, dforget, dreset], axis=-1).astype(jnp.bfloat16)
        dmixed = dmixed.reshape(sequence_batch * time_steps, 3 * hidden_width)

        def weight_term(start, count, normed_input=normed_input, dmixed=dmixed):
            return lax.dot_general(
                normed_input, dmixed, (((0,), (0,)), ((), ())), preferred_element_type=jnp.float32
            )

        weight_grads[layer] = lax.psum_scatter(
            weight_term(jnp.int32(0), rows * lax.axis_size(("batch", "seq"))),
            ("batch", "seq"),
            scatter_dimension=0,
            tiled=True,
        )
        normed_gradient = lax.dot_general(
            dmixed, full, (((1,), (1,)), ((), ())), preferred_element_type=jnp.float32
        )
        normed_gradient = normed_gradient.reshape(sequence_batch, time_steps, hidden_width)
        vector_terms[layer] = jnp.stack(
            [
                jnp.sum(normed_gradient * centered_input, axis=(0, 1)),
                jnp.sum(dforget * stream, axis=(0, 1)),
                jnp.sum(dforget, axis=(0, 1)),
                jnp.sum(dreset * previous, axis=(0, 1)),
                jnp.sum(dreset, axis=(0, 1)),
            ],
            axis=0,
        )
        centered_gradient = normed_gradient * norm_scale
        through_norm = inverse_deviation * (
            centered_gradient
            - jnp.mean(centered_gradient, axis=-1, keepdims=True)
            - centered_input * jnp.mean(centered_gradient * centered_input, axis=-1, keepdims=True)
        )
        grad_out = grad_out * (1.0 - reset) + dforget * vforget + through_norm
    weight_grad = jnp.stack(weight_grads, axis=0)
    vector_grad = lax.psum_scatter(
        jnp.stack(vector_terms, axis=0), ("batch", "seq"), scatter_dimension=2, tiled=True
    )
    return (block_output, grad_out, weight_grad, vector_grad)


def solution(mesh):
    nb, ns = mesh.shape["batch"], mesh.shape["seq"]
    body = functools.partial(tuned_body, nb, ns) if (nb, ns) == (4, 8) else general_body
    placed = (
        P("batch", "seq", None),
        P(None, ("batch", "seq"), None),
        P(None, None, ("batch", "seq")),
        P("batch", "seq", None),
    )
    return jax.shard_map(
        body,
        mesh=mesh,
        in_specs=placed,
        out_specs=(
            P("batch", "seq", None),
            P("batch", "seq", None),
            P(None, ("batch", "seq"), None),
            P(None, None, ("batch", "seq")),
        ),
        check_vma=False,
    )
```

```python
import functools
import types

import jax
import jax.numpy as jnp
from jax import lax
from jax.experimental import pallas as pl
from jax.experimental.pallas import tpu as pltpu
from jax.sharding import PartitionSpec as P

MESH = pl.DeviceIdType.MESH
F32, BF16 = jnp.float32, jnp.bfloat16
V, DMA = pltpu.VMEM, pltpu.SemaphoreType.DMA
epsilon = 1e-05
F = 128
HBM = pl.BlockSpec(memory_space=pl.ANY)
INV = None


class Dims:
    def __init__(self, nb, ns, x_shape, w_shape):
        self.nb, self.ns = nb, ns
        self.inner = 2
        self.outer = ns // 2
        self.sb, self.steps, self.d = x_shape
        self.local = self.sb * self.steps
        self.runs = 8
        self.stretch = self.runs // self.sb
        self.length = self.local // self.runs
        self.tok = self.local * nb
        self.q = self.d // nb
        self.nf = self.q // F
        self.on_time = 10
        self.early = 2
        self.layers, self.rows = w_shape[0], w_shape[1]


class Net:
    def __init__(self, dm):
        nb, ns, inner, outer = dm.nb, dm.ns, dm.inner, dm.outer
        self.b, self.s = lax.axis_index("batch"), lax.axis_index("seq")
        b, s = self.b, self.s
        self.z, self.y = s // inner, lax.rem(s, inner)
        self.across, self.sib, self.diag = b ^ 2, b ^ 1, b ^ 3
        self.batch_peers = [lax.rem(b + j, nb) for j in range(1, nb)]
        self.outer_peers = [lax.rem(self.z + j, outer) for j in range(1, outer)]
        self.inner_peers = [lax.rem(self.y + j, inner) for j in range(1, inner)]
        self.seq_peers = [lax.rem(s + j, ns) for j in range(1, ns)]
        barrier = pltpu.get_barrier_semaphore()
        for p in self.batch_peers:
            pl.semaphore_signal(barrier, inc=1, device_id=(p, s), device_id_type=MESH)
        for p in self.seq_peers:
            pl.semaphore_signal(barrier, inc=1, device_id=(b, p), device_id_type=MESH)
        self.count = nb - 1 + ns - 1

    def ready(self):
        pl.semaphore_wait(pltpu.get_barrier_semaphore(), self.count)


def remote(src, dst, ssem, rsem, dev):
    return pltpu.make_async_remote_copy(
        src_ref=src, dst_ref=dst, send_sem=ssem, recv_sem=rsem, device_id=dev, device_id_type=MESH
    )


def arrived(dst, rsem, dev):
    remote(dst, dst, rsem, rsem, dev).wait_recv()


def sent(src, ssem, dev):
    remote(src, src, ssem, ssem, dev).wait_send()


def local_copy(src, dst, sem):
    c = pltpu.make_async_copy(src, dst, sem)
    c.start()
    return c


def at128(v):
    return pl.multiple_of(v, F)


def sigmoid(v):
    return 1.0 / (1.0 + jnp.exp(jnp.minimum(-v, 80.0)))


def launch(dm, name, cid, kernel, ins, outs, scratch):
    keep_in = [k for k, (_, kind) in ins.items() if kind is INV]
    keep_out = [k for k, (_, _, kind) in outs.items() if kind is INV]
    names = [k + ("_far" if k in keep_in else "") for k in ins] + [k + ("_far" if k in keep_out else "") for k in outs]
    scratch = dict(scratch)
    for k in keep_in:
        scratch[k] = V(ins[k][0].shape, ins[k][0].dtype)
    for k in keep_out:
        scratch[k] = V(outs[k][0], outs[k][1])
    scratch["keep_sem"] = DMA((len(keep_in) + len(keep_out) + 1,))
    names += list(scratch)

    def run(*refs):
        r = types.SimpleNamespace(**dict(zip(names, refs)))
        far = vars(r)
        loads = {k: local_copy(far[k + "_far"], far[k], r.keep_sem.at[i]) for i, k in enumerate(keep_in)}
        stores = []

        def need(*which):
            for k in which:
                loads.pop(k).wait()

        def store(k):
            stores.append(local_copy(far[k], far[k + "_far"], r.keep_sem.at[len(keep_in) + keep_out.index(k)]))

        r.need, r.store = need, store
        kernel(dm, r)
        for c in stores:
            c.wait()

    got = pl.pallas_call(
        run,
        out_shape=[jax.ShapeDtypeStruct(shape, dtype) for shape, dtype, _ in outs.values()],
        in_specs=[HBM for _ in ins],
        out_specs=[HBM for _ in outs],
        scratch_shapes=list(scratch.values()),
        compiler_params=pltpu.CompilerParams(collective_id=cid, has_side_effects=True, vmem_limit_bytes=63 * 2**20),
        name=name,
    )(*[array for array, _ in ins.values()])
    return types.SimpleNamespace(**dict(zip(outs, got)))


def norm_rows(x, gain):
    mu = jnp.mean(x, axis=-1, keepdims=True)
    xc = x - mu
    rstd = lax.rsqrt(jnp.mean(xc * xc, axis=-1, keepdims=True) + epsilon)
    return mu, rstd, (xc * rstd * gain).astype(BF16)


def vrow(dm, r, n, k, fc):
    return r.vec[k : k + 1, pl.ds(at128(n.b * dm.q + fc * F), F)]


def products(dm, r, n, w, chunks, base, pieces):
    TM = 256

    def step(first, i, carry):
        rows = pl.ds(pl.multiple_of(first + i * TM, TM), TM)
        right = jnp.concatenate(
            [w[fc, g].reshape(dm.d, F) for fc in chunks for g in range(3)], axis=1
        )
        m = jnp.dot(r.normed[rows, :], right, preferred_element_type=F32)
        for k, fc in enumerate(chunks):
            o = 3 * k * F
            vf, bf, br = [vrow(dm, r, n, base + j, fc) for j in (1, 2, 4)]
            r.fS[fc, rows, :] = sigmoid(m[:, o + F : o + 2 * F] + vf * r.xS[fc, rows, :] + bf)
            r.cS[fc, rows, :] = m[:, o : o + F]
            r.rS[fc, rows, :] = m[:, o + 2 * F : o + 3 * F] + br
        return carry

    if pieces is None:
        lax.fori_loop(0, dm.tok // TM, functools.partial(step, 0), 0)
    else:
        for g, part in pieces:
            step(g * dm.local, part, 0)


def at_time(dm, g, t):
    return pl.ds(pl.multiple_of(g * dm.local + t * dm.runs, dm.runs), dm.runs)


def run_index(dm):
    return lax.rem(lax.broadcasted_iota(jnp.int32, (dm.runs, F), 0), dm.stretch)


def turn(v, by):
    return pltpu.roll(v, by % v.shape[0], 0)


def pack(dm, parts, end):
    row = lax.broadcasted_iota(jnp.int32, (dm.runs, F), 0)
    out = jnp.zeros((dm.runs, F), F32)
    for g in range(dm.nb):
        for j in range(dm.sb):
            to = g * dm.sb + j
            out = jnp.where(row == to, turn(parts[g], to - (j * dm.stretch + end)), out)
    return out


def unpack(dm, packed, g, end):
    row = lax.broadcasted_iota(jnp.int32, (dm.runs, F), 0)
    out = jnp.zeros((dm.runs, F), F32)
    for j in range(dm.sb):
        to = j * dm.stretch + end
        out = jnp.where(row == to, turn(packed, to - (g * dm.sb + j)), out)
    return out


def enter(dm, a, v, first, back):
    start = dm.stretch - 1 if back else 0
    index = run_index(dm)
    state = first
    for _ in range(dm.stretch - 1):
        state = jnp.where(index == start, first, turn(a * state + v, -1 if back else 1))
    return state


def scan_totals(dm, r, n, fc):
    groups = range(dm.nb)

    def step(t, carry):
        new = []
        for g in groups:
            a, v = carry[g]
            at = at_time(dm, g, t)
            f, cand = r.fS[fc, at, :], r.cS[fc, at, :]
            new.append((a * f, cand + f * (v - cand)))
        return tuple(new)

    one, zero = jnp.ones((dm.runs, F), F32), jnp.zeros((dm.runs, F), F32)
    got = lax.fori_loop(0, dm.length, step, tuple((one, zero) for _ in groups), unroll=4)
    index = run_index(dm)
    for_a, for_v = [], []
    for g in groups:
        a, v = got[g]
        r.runA[fc, g] = a
        r.runV[fc, g] = v
        product = a
        for _ in range(dm.stretch - 1):
            product = jnp.where(index == 0, a, a * turn(product, 1))
        for_a.append(product)
        for_v.append(a * enter(dm, a, v, zero, False) + v)
    a, v = pack(dm, for_a, dm.stretch - 1), pack(dm, for_v, dm.stretch - 1)
    r.totS[fc, 0] = a
    r.totS[fc, 1] = v
    r.tot[fc, n.s, 0] = a
    r.tot[fc, n.s, 1] = v
    for p in n.seq_peers:
        remote(r.totS.at[fc], r.tot.at[fc, n.s], r.t_s.at[fc, p], r.t_r.at[fc, n.s], (n.b, p)).start()


def scan_finish(dm, r, n, fc, base):
    for p in n.seq_peers:
        arrived(r.tot.at[fc, p], r.t_r.at[fc, p], (n.b, p))
    vr = vrow(dm, r, n, base + 3, fc)

    def fold(j, c):
        return jnp.where(j < n.s, r.tot[fc, j, 0] * c + r.tot[fc, j, 1], c)

    packed = lax.fori_loop(0, dm.ns, fold, jnp.zeros((dm.runs, F), F32))
    entering = []
    for g in range(dm.nb):
        e = enter(dm, r.runA[fc, g], r.runV[fc, g], unpack(dm, packed, g, 0), False)
        r.incS[fc, g] = e
        entering.append(e)

    def step(t, carry):
        new = []
        for g in range(dm.nb):
            prev = carry[g]
            at = at_time(dm, g, t)
            f, cand, x = r.fS[fc, at, :], r.cS[fc, at, :], r.xS[fc, at, :]
            reset = sigmoid(r.rS[fc, at, :] + vr * prev)
            c = cand + f * (prev - cand)
            r.cellS[fc, at, :] = c
            r.rS[fc, at, :] = reset
            r.hS[fc, at, :] = x + reset * (c - x)
            new.append(c)
        return tuple(new)

    lax.fori_loop(0, dm.length, step, tuple(entering), unroll=2)


def totals_sent(dm, r, n):
    for fc in range(dm.nf):
        for p in n.seq_peers:
            sent(r.totS.at[fc], r.t_s.at[fc, p], (n.b, p))


def back_totals(dm, r, n, fc, base):
    vr = vrow(dm, r, n, base + 3, fc)
    zero = jnp.zeros((dm.runs, F), F32)

    def step(i, carry):
        new = []
        for g in range(dm.nb):
            at = at_time(dm, g, dm.length - 1 - i)
            reset, dh = r.rS[fc, at, :], r.dhS[fc, at, :]
            direct = dh * reset
            dreset = (r.cellS[fc, at, :] - r.xS[fc, at, :]) * direct * (1.0 - reset)
            r.rS[fc, at, :] = direct
            r.drS[fc, at, :] = dreset
            new.append(r.fS[fc, at, :] * (direct + carry[g]) + dreset * vr)
        return tuple(new)

    got = lax.fori_loop(0, dm.length, step, tuple(zero for _ in range(dm.nb)), unroll=2)
    parts = []
    for g in range(dm.nb):
        a, v = r.runA[fc, g], got[g]
        r.backV[fc, g] = v
        parts.append(a * enter(dm, a, v, zero, True) + v)
    v = pack(dm, parts, 0)
    r.bkS[fc] = v
    r.bk[fc, n.s] = v
    for p in n.seq_peers:
        remote(r.bkS.at[fc], r.bk.at[fc, n.s], r.k_s.at[fc, p], r.k_r.at[fc, n.s], (n.b, p)).start()


def back_finish(dm, r, n, fc, base):
    for p in n.seq_peers:
        arrived(r.bk.at[fc, p], r.k_r.at[fc, p], (n.b, p))
    vf, vr = vrow(dm, r, n, base + 1, fc), vrow(dm, r, n, base + 3, fc)

    def fold(i, c):
        j = dm.ns - 1 - i
        return jnp.where(j > n.s, r.tot[fc, j, 0] * c + r.bk[fc, j], c)

    zero = jnp.zeros((dm.runs, F), F32)
    packed = lax.fori_loop(0, dm.ns, fold, zero)
    carries = [
        enter(dm, r.runA[fc, g], r.backV[fc, g], unpack(dm, packed, g, dm.stretch - 1), True) for g in range(dm.nb)
    ]

    def one(at, prev, carry, sums):
        s1, s2, s3, s4 = sums
        f, cand, x = r.fS[fc, at, :], r.cS[fc, at, :], r.xS[fc, at, :]
        direct, dreset = r.rS[fc, at, :], r.drS[fc, at, :]
        dcell = direct + carry
        dcand = dcell * (1.0 - f)
        dforget = dcand * f * (prev - cand)
        r.cS[fc, at, :] = dcand
        r.fS[fc, at, :] = dforget
        r.rS[fc, at, :] = r.dhS[fc, at, :] - direct + dforget * vf
        return f * dcell + dreset * vr, (s1 + dforget * x, s2 + dforget, s3 + dreset * prev, s4 + dreset)

    def step(i, state):
        t = dm.length - 1 - i
        carry, sums = state
        new = []
        for g in range(dm.nb):
            c, sums = one(at_time(dm, g, t), r.cellS[fc, at_time(dm, g, t - 1), :], carry[g], sums)
            new.append(c)
        return tuple(new), sums

    carry, sums = lax.fori_loop(0, dm.length - 1, step, (tuple(carries), (zero, zero, zero, zero)), unroll=3)
    for g in range(dm.nb):
        _, sums = one(at_time(dm, g, 0), r.incS[fc, g], carry[g], sums)
    for k in range(4):
        r.vsum_out[fc, k] = sums[k]
    for g, part in enumerate((r.cS, r.fS, r.drS)):
        r.dmixed[fc, g] = part[fc].astype(BF16)


def back_sent(dm, r, n):
    for fc in range(dm.nf):
        for p in n.seq_peers:
            sent(r.bkS.at[fc], r.k_s.at[fc, p], (n.b, p))


def back_outputs(dm, r, fc):
    return [
        local_copy(r.dmixed.at[fc], r.dmixed_out.at[fc], r.out_sem.at[fc, 0]),
        local_copy(r.rS.at[fc], r.dtail_out.at[fc], r.out_sem.at[fc, 1]),
    ]


class Gather:
    def __init__(self, dm, n, r, l, w):
        self.dm, self.n, self.r, self.l, self.w = dm, n, r, l, w

    def strip(self, fc, pos):
        R = self.dm.rows
        return self.w.at[fc, :, :, pl.ds(pl.multiple_of(pos * R, R), R)]

    def piece(self, fc, b, gates=slice(0, 3)):
        n, R = self.n, self.dm.rows
        return self.w.at[fc, gates, b, pl.ds(pl.multiple_of(n.s * R, R), R)]

    def source(self, fc, p, gate):
        dm = self.dm
        return self.r.w_in.at[self.l, :, pl.ds(at128(gate * dm.d + p * dm.q + fc * F), F)]

    def own(self, fc):
        r, l, b = self.r, self.l, self.n.b
        return [local_copy(self.source(fc, b, g), self.piece(fc, b, g), r.own_sem.at[l, fc, g]) for g in range(3)]

    def pre(self, fc):
        n, r, l = self.n, self.r, self.l
        for p in n.batch_peers:
            for g in range(3):
                remote(
                    self.source(fc, p, g), self.piece(fc, n.b, g), r.pre_s.at[l, fc, p], r.pre_r.at[l, fc, n.b], (p, n.s)
                ).start()

    def hop(self, fc, src, to):
        n, r, l, dm = self.n, self.r, self.l, self.dm
        at = self.strip(fc, src * dm.inner + n.y)
        side = 1 if to > 0 else 0
        return remote(at, at, r.z_s.at[l, fc, src, side], r.z_r.at[l, fc, src], (n.b, (n.z + to) * dm.inner + n.y))

    def to_inner(self, fc, src):
        n, r, l, dm = self.n, self.r, self.l, self.dm
        at = self.strip(fc, src * dm.inner + n.y)
        return [
            remote(at, at, r.y_s.at[l, fc, src, p], r.y_r.at[l, fc, src, n.y], (n.b, n.z * dm.inner + p))
            for p in n.inner_peers
        ]

    def begun(self, fc):
        for p in self.n.batch_peers:
            arrived(self.piece(fc, p), self.r.pre_r.at[self.l, fc, p], (p, self.n.s))

    def start(self, fc, inner=True):
        n, dm = self.n, self.dm
        pl.when(n.z < dm.outer - 1)(lambda: self.hop(fc, n.z, 1).start())
        pl.when(n.z > 0)(lambda: self.hop(fc, n.z, -1).start())
        if inner:
            for c in self.to_inner(fc, n.z):
                c.start()

    def step(self, fc, h, inner=True):
        n, r, l, dm = self.n, self.r, self.l, self.dm
        for way in (-1, 1):
            src = n.z + way * h
            has = (src >= 0) if way < 0 else (src < dm.outer)
            on = (n.z < dm.outer - 1) if way < 0 else (n.z > 0)

            def take(src=src, on=on, way=way):
                at = self.strip(fc, src * dm.inner + n.y)
                arrived(at, r.z_r.at[l, fc, src], (n.b, n.s))
                pl.when(on)(lambda: self.hop(fc, src, -way).start())
                if inner:
                    for c in self.to_inner(fc, src):
                        c.start()

            pl.when(has)(take)

    def complete(self, fc):
        n, r, l, dm = self.n, self.r, self.l, self.dm
        for o in range(dm.outer):
            for p in n.inner_peers:
                arrived(self.strip(fc, o * dm.inner + p), r.y_r.at[l, fc, o, p], (n.b, n.s))

    def drain_inner(self, fc):
        for o in range(self.dm.outer):
            for p in self.n.inner_peers:
                sent(self.strip(fc, self.n.s), self.r.y_s.at[self.l, fc, o, p], (self.n.b, self.n.s))

    def drain_pre(self, fc):
        for p in self.n.batch_peers:
            sent(self.piece(fc, p), self.r.pre_s.at[self.l, fc, p], (p, self.n.s))

    def drain_outer(self, fc):
        n, r, l, dm = self.n, self.r, self.l, self.dm
        for o in range(dm.outer):
            right = jnp.logical_and(o <= n.z, n.z < dm.outer - 1)
            left = jnp.logical_and(o >= n.z, n.z > 0)
            for ok, side in ((right, 1), (left, 0)):
                pl.when(ok)(lambda o=o, side=side: sent(self.strip(fc, n.s), r.z_s.at[l, fc, o, side], (n.b, n.s)))


def kernel_one(dm, r):
    n = Net(dm)
    nb, ns, nf, inner, outer, R = dm.nb, dm.ns, dm.nf, dm.inner, dm.outer, dm.rows
    b, s, z, y = n.b, n.s, n.z, n.y
    w0, w1 = Gather(dm, n, r, 0, r.wq0), Gather(dm, n, r, 1, r.wq1_out)
    NX, NA = 4, dm.early
    XR = dm.local // NX

    own_w = [w0.own(fc) for fc in range(nf)]
    own_x = local_copy(r.x_in, r.xg.at[b], r.loc.at[2 * nf])
    r.need("vec_in")
    n.ready()
    for fc in range(nf):
        w0.pre(fc)
        if fc == 0:
            r.vecg[b, s] = r.vec_in[...]
            for p in n.batch_peers:
                remote(r.vec_in, r.vecg.at[b, s], r.vp_s.at[p], r.vp_r.at[b], (p, s)).start()
    remote(r.x_in, r.xg.at[b], r.xc_s, r.xc_r, (n.sib, s)).start()

    def x_send(k):
        rows = pl.ds(k * XR, XR)
        return remote(r.x_in.at[rows], r.xg.at[b, rows], r.xx_s.at[k], r.xx_r.at[k], (n.across, s))

    def x_relay(k):
        at = r.xg.at[n.across, pl.ds(k * XR, XR)]
        return remote(at, at, r.xl_s.at[k], r.xl_r.at[k], (n.sib, s))

    def relay(k):
        arrived(r.xg.at[n.across, pl.ds(k * XR, XR)], r.xx_r.at[k], (n.across, s))
        x_relay(k).start()

    def w0_start(fc):
        for c in own_w[fc]:
            c.wait()
        w0.begun(fc)
        w0.start(fc)

    w0_start(0)
    for k in range(NX):
        x_send(k).start()
    for p in n.batch_peers:
        arrived(r.vecg.at[p, s], r.vp_r.at[p], (p, s))
    for p in n.outer_peers:
        remote(r.vecg.at[:, s], r.vecg.at[:, s], r.vz_s.at[p], r.vz_r.at[z], (b, p * inner + y)).start()
    w0.step(0, 1)
    for p in n.outer_peers:
        arrived(r.vecg.at[:, p * inner + y], r.vz_r.at[p], (b, s))
    for o in range(outer):
        for p in n.inner_peers:
            at = r.vecg.at[:, o * inner + y]
            remote(at, at, r.vy_s.at[o, p], r.vy_r.at[o, y], (b, z * inner + p)).start()
    w0.step(0, 2)
    w0_start(1)
    w0.step(0, 3)
    for o in range(outer):
        for p in n.inner_peers:
            arrived(r.vecg.at[:, o * inner + p], r.vy_r.at[o, p], (b, s))
    per = F // R
    for k in range(dm.d // F):
        bb, s0 = (k * per) // ns, (k * per) % ns
        total = r.vecg[bb, s0]
        for j in range(1, per):
            total = total + r.vecg[bb, s0 + j]
        r.vec[:, k * F : (k + 1) * F] = total
    own_x.wait()

    TILE = 32

    def norm_block(bb, lo=0, count=dm.local):
        def step(i, carry):
            rows = pl.ds(pl.multiple_of(lo + i * TILE, TILE), TILE)
            x = r.xg[bb, rows, :].astype(F32)
            mu, rstd, normed = norm_rows(x, r.vec[0:1, :])
            every = pl.ds(pl.multiple_of(bb * dm.local + lo + i * TILE, TILE), TILE)
            r.normed[every, :] = normed
            r.mu_out[every, :] = jnp.broadcast_to(mu, (TILE, F))
            r.rstd_out[every, :] = jnp.broadcast_to(rstd, (TILE, F))
            for fc in range(nf):
                r.xS[fc, every, :] = r.xg[bb, rows, pl.ds(at128(b * dm.q + fc * F), F)].astype(F32)
            return carry

        lax.fori_loop(0, count // TILE, step, 0, unroll=2)

    def diag_norm(k):
        arrived(r.xg.at[n.diag, pl.ds(k * XR, XR)], r.xl_r.at[k], (n.sib, s))
        norm_block(n.diag, k * XR, XR)

    def across_norm(k):
        norm_block(n.across, k * XR, XR)

    def prod(fc, *pieces):
        products(dm, r, n, r.wq0, (fc,), 0, pieces)

    near = [(g, part) for g in (b, n.sib) for part in range(2)]
    w0.step(1, 1)
    norm_block(b)
    w0.step(1, 2)
    w0_start(2)
    arrived(r.xg.at[n.sib], r.xc_r, (n.sib, s))
    norm_block(n.sib)
    w0.step(1, 3)
    w0.step(2, 1)
    relay(0)
    w0.complete(0)
    prod(0, *near)
    w0.step(2, 2)
    w0_start(3)
    across_norm(0)
    relay(1)
    across_norm(1)
    w0.step(2, 3)
    w0.step(3, 1)
    prod(0, (n.across, 0))
    diag_norm(0)
    w0.step(3, 2)
    diag_norm(1)
    w0.complete(1)
    prod(1, *near)
    w0.step(3, 3)
    relay(2)
    across_norm(2)
    prod(0, (n.diag, 0))
    prod(1, (n.across, 0), (n.diag, 0))
    diag_norm(2)
    second = [c for fc in range(nf) for c in w1.own(fc)]
    relay(3)
    for fc in range(nf):
        w1.pre(fc)
    across_norm(3)
    prod(0, (n.across, 1))
    diag_norm(3)
    prod(0, (n.diag, 1))
    scan_totals(dm, r, n, 0)
    prod(1, (n.across, 1), (n.diag, 1))
    scan_totals(dm, r, n, 1)
    normed_copy = local_copy(r.normed, r.normed_out, r.loc.at[0])
    r.store("mu_out")
    r.store("rstd_out")

    pend = []

    def p2(fc):
        scan_finish(dm, r, n, fc, 0)
        r.hb[fc] = r.hS[fc].astype(BF16)
        remote(r.hb.at[fc], r.x1g_out.at[b, fc], r.h_s.at[fc], r.h_r.at[fc], (n.across, s)).start()
        remote(r.hb.at[fc], r.x1g_out.at[b, fc], r.hc_s.at[fc], r.hc_r.at[fc], (n.sib, s)).start()
        pend.append(local_copy(r.hb.at[fc], r.x1g_out.at[b, fc], r.out_sem.at[fc, 0]))
        pairs = [(r.fS, r.f_out), (r.cS, r.c_out), (r.rS, r.r_out), (r.cellS, r.cell_out), (r.hS, r.x1_out), (r.xS, r.xo_out)]
        for k, (src, dst) in enumerate(pairs):
            pend.append(local_copy(src.at[fc], dst.at[fc], r.out_sem.at[fc, k + 1]))

    def h_relay(fc):
        at = r.x1g_out.at[n.across, fc]
        arrived(at, r.h_r.at[fc], (n.across, s))
        remote(at, at, r.hl_s.at[fc], r.hl_r.at[fc], (n.sib, s)).start()

    for c in second:
        c.wait()
    w1.begun(0)
    w1.start(0, 0 < NA)
    w0.complete(2)
    products(dm, r, n, r.wq0, (2,), 0, None)
    scan_totals(dm, r, n, 2)
    w1.step(0, 1, 0 < NA)
    p2(0)
    w1.step(0, 2, 0 < NA)
    w1.begun(1)
    w1.start(1, 1 < NA)
    p2(1)
    w0.complete(3)
    products(dm, r, n, r.wq0, (3,), 0, None)
    wq_copy = local_copy(r.wq0, r.wq0_out, r.loc.at[2])
    scan_totals(dm, r, n, 3)
    w1.step(0, 3, 0 < NA)
    p2(2)
    w1.step(1, 1, 1 < NA)
    h_relay(0)
    p2(3)
    r.inc_out[...] = r.incS[...]
    r.runA_out[...] = r.runA[...]
    r.tot_out[...] = r.tot[...]
    r.vec_out[...] = r.vec[...]
    for k in ("inc_out", "runA_out", "tot_out", "vec_out"):
        r.store(k)
    w1.step(1, 2, 1 < NA)
    w1.begun(2)
    w1.start(2, 2 < NA)
    w1.step(1, 3, 1 < NA)
    h_relay(1)
    w1.step(2, 1, 2 < NA)
    w1.step(2, 2, 2 < NA)
    w1.step(2, 3, 2 < NA)
    h_relay(2)
    w1.begun(3)
    h_relay(3)
    for fc in range(nf):
        if fc < NA:
            w1.complete(fc)
        arrived(r.x1g_out.at[n.sib, fc], r.hc_r.at[fc], (n.sib, s))
        arrived(r.x1g_out.at[n.diag, fc], r.hl_r.at[fc], (n.sib, s))
    for c in pend:
        c.wait()
    normed_copy.wait()
    wq_copy.wait()
    for p in n.batch_peers:
        sent(r.vec_in, r.vp_s.at[p], (p, s))
    for p in n.outer_peers:
        sent(r.vecg.at[:, s], r.vz_s.at[p], (b, s))
    for p in n.inner_peers:
        for o in range(outer):
            sent(r.vecg.at[:, s], r.vy_s.at[o, p], (b, s))
    sent(r.x_in, r.xc_s, (n.sib, s))
    for k in range(NX):
        x_send(k).wait_send()
        x_relay(k).wait_send()
    totals_sent(dm, r, n)
    for fc in range(nf):
        w0.drain_pre(fc)
        w1.drain_pre(fc)
        w0.drain_outer(fc)
        w0.drain_inner(fc)
        if fc < NA:
            w1.drain_inner(fc)
        if fc < nf - 1:
            w1.drain_outer(fc)
        for sem in (r.h_s, r.hc_s, r.hl_s):
            sent(r.hb.at[fc], sem.at[fc], (b, s))


def scan_scratch(dm):
    nf, ns = dm.nf, dm.ns
    return dict(
        totS=V((nf, 2, dm.runs, F), F32),
        t_s=DMA((nf, ns)), t_r=DMA((nf, ns)),
    )


def call_one(dm, x, w, vec):
    nb, ns, nf, inner, outer, R = dm.nb, dm.ns, dm.nf, dm.inner, dm.outer, dm.rows
    D, q, tok, L = dm.d, dm.q, dm.tok, dm.layers
    wshape = (nf, 3, nb, ns * R, F)
    chunk, cV = ((nf, tok, F), F32, HBM), V((nf, tok, F), F32)
    ins = dict(x_in=(x, HBM), w_in=(w, HBM), vec_in=(vec, INV))
    outs = dict(
        normed_out=((tok, D), BF16, HBM), wq0_out=(wshape, BF16, HBM), wq1_out=(wshape, BF16, HBM),
        x1g_out=((nb, nf, tok, F), BF16, HBM),
        x1_out=chunk, xo_out=chunk, f_out=chunk, c_out=chunk, r_out=chunk, cell_out=chunk,
        inc_out=((nf, nb, dm.runs, F), F32, INV), runA_out=((nf, nb, dm.runs, F), F32, INV), tot_out=((nf, ns, 2, dm.runs, F), F32, INV),
        vec_out=((16, D), F32, INV), mu_out=((tok, F), F32, INV), rstd_out=((tok, F), F32, INV),
    )
    scratch = dict(
        xg=V((nb, dm.local, D), BF16), normed=V((tok, D), BF16), wq0=V(wshape, BF16),
        vecg=V((nb, ns, 16, F), F32), vec=V((16, D), F32),
        xS=cV, fS=cV, cS=cV, rS=cV, cellS=cV, hS=cV, hb=V((nf, tok, F), BF16),
        incS=V((nf, nb, dm.runs, F), F32), tot=V((nf, ns, 2, dm.runs, F), F32),
        pre_s=DMA((L, nf, nb)), pre_r=DMA((L, nf, nb)), z_s=DMA((L, nf, outer, 2)), z_r=DMA((L, nf, outer)),
        y_s=DMA((L, nf, outer, inner)), y_r=DMA((L, nf, outer, inner)),
        vp_s=DMA((nb,)), vp_r=DMA((nb,)), vz_s=DMA((outer,)), vz_r=DMA((outer,)),
        vy_s=DMA((outer, inner)), vy_r=DMA((outer, inner)),
        xx_s=DMA((4,)), xx_r=DMA((4,)), xc_s=DMA, xc_r=DMA, xl_s=DMA((4,)), xl_r=DMA((4,)),
        h_s=DMA((nf,)), h_r=DMA((nf,)), hc_s=DMA((nf,)), hc_r=DMA((nf,)), hl_s=DMA((nf,)), hl_r=DMA((nf,)),
        loc=DMA((2 * nf + 1,)), own_sem=DMA((L, nf, 3)), out_sem=DMA((nf, 7)),
        runA=V((nf, nb, dm.runs, F), F32), runV=V((nf, nb, dm.runs, F), F32),
        **scan_scratch(dm),
    )
    return launch(dm, "forward_one", 0, kernel_one, ins, outs, scratch)


def kernel_two(dm, r):
    n = Net(dm)
    nb, nf = dm.nb, dm.nf
    b, s = n.b, n.s
    w1 = Gather(dm, n, r, 1, r.wq)
    NA = dm.early
    x_copy = local_copy(r.x1_in, r.xS, r.loc.at[0])
    w_copy = []
    for fc in range(NA):
        w_copy.append(local_copy(r.w_in.at[fc], r.wq.at[fc], r.w_sem.at[fc, 0]))
    w_late, y_sends = [], {fc: [] for fc in range(NA, nf)}
    last = nf - 1
    for fc in range(NA, last):
        for o in range(dm.outer):
            rows = pl.ds(pl.multiple_of((o * dm.inner + n.y) * dm.rows, dm.rows), dm.rows)
            at = (fc, slice(None), slice(None), rows)
            for p in n.inner_peers:
                y_sends[fc].append(
                    remote(r.w_in.at[at], r.wq.at[at], r.y_s.at[1, fc, o, p], r.y_r.at[1, fc, o, n.y], (b, n.z * dm.inner + p))
                )
            w_late.append(local_copy(r.w_in.at[at], r.wq.at[at], r.w_sem.at[fc, o]))

    rows = pl.ds(pl.multiple_of(s * dm.rows, dm.rows), dm.rows)
    own = local_copy(r.w_in.at[last, :, :, rows], r.wq.at[last, :, :, rows], r.w_sem.at[last, 0])

    def cot_send(p):
        cols = pl.ds(at128(p * dm.q), dm.q)
        at = r.cot.at[pl.ds(pl.multiple_of(b * dm.local, dm.local), dm.local)]
        return remote(r.cot_in.at[:, cols], at, r.c_s.at[p], r.c_r.at[b], (p, s))

    cot_copy = local_copy(
        r.cot_in.at[:, pl.ds(at128(b * dm.q), dm.q)], r.cot.at[pl.ds(pl.multiple_of(b * dm.local, dm.local), dm.local)], r.loc.at[1]
    )
    TT, TILE = 256, 32

    def fetch(k):
        return pltpu.make_async_copy(r.x1g_in.at[:, :, pl.ds(k * TT, TT)], r.xt.at[k % 2], r.xt_sem.at[k % 2])

    fetch(0).start()
    r.need("vec")
    n.ready()
    for c in y_sends[NA]:
        c.start()
    own.wait()
    w1.start(last, False)
    for p in n.batch_peers:
        cot_send(p).start()
    for k in range(dm.tok // TT):
        if (k + 1) * TT < dm.tok:
            fetch(k + 1).start()
        fetch(k).wait()

        def step(i, carry, k=k):
            rows = pl.ds(pl.multiple_of(i * TILE, TILE), TILE)
            x = jnp.concatenate([r.xt[k % 2, q, fc, rows, :] for q in range(nb) for fc in range(nf)], axis=1).astype(F32)
            mu, rstd, normed = norm_rows(x, r.vec[5:6, :])
            every = pl.ds(pl.multiple_of(k * TT + i * TILE, TILE), TILE)
            r.normed[every, :] = normed
            r.mu_out[every, :] = jnp.broadcast_to(mu, (TILE, F))
            r.rstd_out[every, :] = jnp.broadcast_to(rstd, (TILE, F))
            return carry

        lax.fori_loop(0, TT // TILE, step, 0, unroll=2)
        if k in (2, 4, 6):
            w1.step(last, k // 2, False)
    normed_copy = local_copy(r.normed, r.normed_out, r.xt_sem.at[0])
    r.store("mu_out")
    r.store("rstd_out")
    for c in [x_copy, cot_copy] + w_copy:
        c.wait()

    def p1(fcs):
        products(dm, r, n, r.wq, fcs, 5, None)
        for fc in fcs:
            scan_totals(dm, r, n, fc)

    pend = []

    def p2(fc):
        scan_finish(dm, r, n, fc, 5)
        r.hb[fc] = r.hS[fc].astype(BF16)
        pend.append(local_copy(r.hb.at[fc], r.h_out.at[fc], r.out_sem.at[fc, 2]))
        r.dhS[fc] = r.cot[:, fc * F : (fc + 1) * F].astype(F32)
        back_totals(dm, r, n, fc, 5)

    def p3(fc):
        back_finish(dm, r, n, fc, 5)
        pend.extend(back_outputs(dm, r, fc))

    p1((0, 1))
    for o in range(dm.outer):
        for c in w1.to_inner(last, o):
            c.start()
    for p in n.batch_peers:
        arrived(r.cot.at[pl.ds(pl.multiple_of(p * dm.local, dm.local), dm.local)], r.c_r.at[p], (p, s))
    p2(0)
    p2(1)
    for c in w_late:
        c.wait()
    for fc in range(NA, nf):
        w1.complete(fc)
        p1((fc,))
    pend.append(local_copy(r.wq, r.wq_out, r.loc.at[0]))
    for fc in range(NA, nf):
        p2(fc)
    for fc in range(nf):
        p3(fc)
    r.store("vsum_out")
    for c in pend:
        c.wait()
    normed_copy.wait()
    for p in n.batch_peers:
        cot_send(p).wait_send()
    for fc in range(NA, nf):
        w1.drain_inner(fc)
    w1.drain_outer(last)
    totals_sent(dm, r, n)
    back_sent(dm, r, n)


def call_two(dm, one, cot):
    nb, ns, nf = dm.nb, dm.ns, dm.nf
    tok = dm.tok
    cV = V((nf, tok, F), F32)
    ins = dict(
        w_in=(one.wq1_out, HBM), x1_in=(one.x1_out, HBM), cot_in=(cot, HBM),
        x1g_in=(one.x1g_out, HBM), vec=(one.vec_out, INV),
    )
    outs = dict(
        wq_out=((nf, 3, nb, ns * dm.rows, F), BF16, HBM),
        normed_out=((tok, dm.d), BF16, HBM), h_out=((nf, tok, F), BF16, HBM),
        dmixed_out=((nf, 3, tok, F), BF16, HBM), dtail_out=((nf, tok, F), F32, HBM),
        vsum_out=((nf, 4, dm.runs, F), F32, INV), mu_out=((tok, F), F32, INV), rstd_out=((tok, F), F32, INV),
    )
    scratch = dict(
        wq=V((nf, 3, nb, ns * dm.rows, F), BF16), cot=V((tok, dm.q), BF16), xt=V((2, nb, nf, 256, F), BF16),
        normed=V((tok, dm.d), BF16), dmixed=V((nf, 3, tok, F), BF16),
        xS=cV, fS=cV, cS=cV, rS=cV, cellS=cV, drS=cV, hS=cV, hb=V((nf, tok, F), BF16),
        incS=V((nf, nb, dm.runs, F), F32), tot=V((nf, ns, 2, dm.runs, F), F32),
        bk=V((nf, ns, dm.runs, F), F32), bkS=V((nf, dm.runs, F), F32), backV=V((nf, nb, dm.runs, F), F32),
        runA=V((nf, nb, dm.runs, F), F32), runV=V((nf, nb, dm.runs, F), F32),
        k_s=DMA((nf, ns)), k_r=DMA((nf, ns)),
        c_s=DMA((nb,)), c_r=DMA((nb,)), w_sem=DMA((nf, dm.outer)),
        y_s=DMA((2, nf, dm.outer, dm.inner)), y_r=DMA((2, nf, dm.outer, dm.inner)),
        z_s=DMA((2, nf, dm.outer, 2)), z_r=DMA((2, nf, dm.outer)),
        loc=DMA((2,)), xt_sem=DMA((2,)), out_sem=DMA((nf, 3)),
        **scan_scratch(dm),
    )
    alias = dict(scratch)

    def kernel(dm, r):
        r.dhS = r.hS
        kernel_two(dm, r)

    return launch(dm, "layer_two", 1, kernel, ins, outs, alias)


def kernel_three(dm, r):
    n = Net(dm)
    nf = dm.nf
    loads = []
    for fc in range(nf):
        pairs = [(r.f_in.at[fc], r.fS), (r.c_in.at[fc], r.cS), (r.r_in.at[fc], r.rS), (r.cell_in.at[fc], r.cellS),
                 (r.xo_in.at[fc], r.xS), (r.dh_in.at[:, pl.ds(fc * F, F)], r.dhS)]
        loads.append([local_copy(src, dst.at[fc], r.loc.at[fc, k]) for k, (src, dst) in enumerate(pairs)])
    rs = Scatter(dm, n, r, dm.on_time)
    late = range(dm.on_time, rs.count)
    b, s = n.b, n.s

    def block_send(fc, p):
        cols = pl.ds(at128(b * dm.q + fc * F), F)
        src = r.h_in.at[fc, pl.ds(pl.multiple_of(p * dm.local, dm.local), dm.local)]
        return remote(src, r.block_out.at[:, cols], r.o_s.at[fc, p], r.o_r.at[fc, b], (p, s))

    pend = []
    for fc in range(nf):
        cols = pl.ds(at128(b * dm.q + fc * F), F)
        src = r.h_in.at[fc, pl.ds(pl.multiple_of(b * dm.local, dm.local), dm.local)]
        pend.append(local_copy(src, r.block_out.at[:, cols], r.out_sem.at[fc, 2]))
    r.need("wg")
    n.ready()
    rs.start(late[0])
    for fc in range(nf):
        for p in n.batch_peers:
            block_send(fc, p).start()
    r.need("vec", "incS", "runA", "tot")
    for fc in range(nf):
        for c in loads[fc]:
            c.wait()
        back_totals(dm, r, n, fc, 0)
    for ch in late[1:]:
        rs.start(ch)
    rs.mid(late[0])
    for fc in range(nf):
        back_finish(dm, r, n, fc, 0)
        pend.extend(back_outputs(dm, r, fc))
        if 0 < fc < len(late):
            rs.mid(late[fc])
            rs.last(late[fc - 1])
    rs.last(late[-1])
    r.store("vsum_out")
    r.need("fr_early")
    rs.assemble(r.fr_early)
    r.store("wg_out")
    for c in pend:
        c.wait()
    back_sent(dm, r, n)
    for fc in range(nf):
        for p in n.batch_peers:
            block_send(fc, p).wait_send()
            arrived(r.block_out.at[:, pl.ds(at128(p * dm.q + fc * F), F)], r.o_r.at[fc, p], (p, s))
    rs.drain(late)


def call_three(dm, one, two, g1):
    nb, ns, nf, tok = dm.nb, dm.ns, dm.nf, dm.tok
    cV = V((nf, tok, F), F32)
    ins = dict(
        f_in=(one.f_out, HBM), c_in=(one.c_out, HBM), r_in=(one.r_out, HBM), cell_in=(one.cell_out, HBM),
        xo_in=(one.xo_out, HBM), dh_in=(g1.dx_out, HBM), vec=(one.vec_out, INV), incS=(one.inc_out, INV),
        runA=(one.runA_out, INV), tot=(one.tot_out, INV), wg=(g1.late_out, INV), fr_early=(g1.fr_out, INV),
        h_in=(two.h_out, HBM),
    )
    outs = dict(
        block_out=((dm.local, dm.d), BF16, HBM),
        dmixed_out=((nf, 3, tok, F), BF16, HBM), dtail_out=((nf, tok, F), F32, HBM), vsum_out=((nf, 4, dm.runs, F), F32, INV),
        wg_out=((dm.rows, 3 * dm.d), F32, INV),
    )
    scratch = dict(
        dmixed=V((nf, 3, tok, F), BF16), xS=cV, fS=cV, cS=cV, rS=cV, cellS=cV, drS=cV, dhS=cV,
        bk=V((nf, ns, dm.runs, F), F32), bkS=V((nf, dm.runs, F), F32), backV=V((nf, nb, dm.runs, F), F32),
        k_s=DMA((nf, ns)), k_r=DMA((nf, ns)), loc=DMA((nf, 6)), out_sem=DMA((nf, 3)), o_s=DMA((nf, nb)), o_r=DMA((nf, nb)),
        fr=V((nb, 3, dm.rows, dm.q), BF16), **scatter_scratch(dm, 3 * nb - dm.on_time),
    )
    return launch(dm, "layer_one_back", 2, kernel_three, ins, outs, scratch)


class Scatter:
    def __init__(self, dm, n, r, lo):
        self.dm, self.n, self.r, self.lo = dm, n, r, lo
        self.H = 3
        self.count = dm.nb * self.H

    def strip(self, ch, pos):
        R = self.dm.rows
        return self.r.wg.at[ch - self.lo, pl.ds(pl.multiple_of(pos * R, R), R)]

    def y_copy(self, ch, j, o):
        n, r, I, k = self.n, self.r, self.dm.inner, ch - self.lo
        p = lax.rem(n.y + j, I)
        return remote(
            self.strip(ch, o * I + p), r.yr.at[k, I - j - 1, o], r.ry_s.at[k, j - 1, o], r.ry_r.at[k, I - j - 1, o], (n.b, n.z * I + p)
        )

    def z_copy(self, ch, j):
        n, r, O, k = self.n, self.r, self.dm.outer, ch - self.lo
        p = lax.rem(n.z + j, O)
        return remote(
            r.zs.at[k, p], r.zr.at[k, O - j - 1], r.rz_s.at[k, j - 1], r.rz_r.at[k, O - j - 1], (n.b, p * self.dm.inner + n.y)
        )

    def f_copy(self, ch):
        n, r, k = self.n, self.r, ch - self.lo
        return remote(r.fs.at[k], r.fr.at[n.b, ch % self.H], r.rf_s.at[k], r.rf_r.at[n.b, ch % self.H], (ch // self.H, n.s))

    def start(self, ch):
        for j in range(1, self.dm.inner):
            for o in range(self.dm.outer):
                self.y_copy(ch, j, o).start()

    def mid(self, ch):
        n, r, dm, k = self.n, self.r, self.dm, ch - self.lo
        for j in range(1, dm.inner):
            for o in range(dm.outer):
                arrived(r.yr.at[k, j - 1, o], r.ry_r.at[k, j - 1, o], (n.b, n.s))
        for jz in range(dm.outer):
            o = lax.rem(n.z + jz + 1, dm.outer)
            pos = pl.ds(pl.multiple_of((o * dm.inner + n.y) * dm.rows, dm.rows), dm.rows)
            total = r.wg[k, pos, :].astype(F32)
            for j in range(1, dm.inner):
                total = total + r.yr[k, j - 1, o].astype(F32)
            r.zs[k, o] = total.astype(BF16)
            if jz + 1 < dm.outer:
                self.z_copy(ch, jz + 1).start()

    def last(self, ch):
        n, r, dm, k = self.n, self.r, self.dm, ch - self.lo
        for j in range(1, dm.outer):
            arrived(r.zr.at[k, j - 1], r.rz_r.at[k, j - 1], (n.b, n.s))
        total = r.zs[k, n.z].astype(F32)
        for j in range(1, dm.outer):
            total = total + r.zr[k, j - 1].astype(F32)
        r.fs[k] = total.astype(BF16)
        pl.when(n.b != ch // self.H)(lambda: self.f_copy(ch).start())

        @pl.when(n.b == ch // self.H)
        def _():
            r.fr[n.b, ch % self.H] = r.fs[k]

    def receive(self, chunks):
        n, r = self.n, self.r
        for ch in chunks:

            @pl.when(n.b == ch // self.H)
            def _(ch=ch):
                for p in n.batch_peers:
                    arrived(r.fr.at[p, ch % self.H], r.rf_r.at[p, ch % self.H], (p, n.s))

    def assemble(self, early=None):
        n, r, dm = self.n, self.r, self.dm
        self.receive(range(self.lo, self.count))
        for h in range(self.H):
            here = n.b * self.H + h >= self.lo
            for k in range(dm.nb):
                to = h * dm.d + k * dm.q

                @pl.when(here)
                def _(h=h, k=k, to=to):
                    r.wg_out[:, to : to + dm.q] = r.fr[k, h].astype(F32)

                if early is not None:

                    @pl.when(jnp.logical_not(here))
                    def _(h=h, k=k, to=to):
                        r.wg_out[:, to : to + dm.q] = early[k, h].astype(F32)

    def drain(self, chunks):
        for ch in chunks:
            for j in range(1, self.dm.inner):
                for o in range(self.dm.outer):
                    self.y_copy(ch, j, o).wait_send()
            for j in range(1, self.dm.outer):
                self.z_copy(ch, j).wait_send()
            pl.when(self.n.b != ch // self.H)(lambda ch=ch: self.f_copy(ch).wait_send())


def scatter_scratch(dm, count):
    inner, outer, R, q = dm.inner, dm.outer, dm.rows, dm.q
    return dict(
        yr=V((count, inner - 1, outer, R, q), BF16), zs=V((count, outer, R, q), BF16), zr=V((count, outer - 1, R, q), BF16),
        fs=V((count, R, q), BF16),
        ry_s=DMA((count, inner - 1, outer)), ry_r=DMA((count, inner - 1, outer)),
        rz_s=DMA((count, outer - 1)), rz_r=DMA((count, outer - 1)), rf_s=DMA((count,)), rf_r=DMA((dm.nb, 3)),
    )


def kernel_grads(first, dm, r):
    n = Net(dm)
    nb, nf, q, tok = dm.nb, dm.nf, dm.q, dm.tok
    b, s = n.b, n.s
    base = 0 if first else 5
    NT = nb
    TR = tok // NT
    PER = TR // F
    rs = Scatter(dm, n, r, 0)
    H, NCH = rs.H, rs.count
    mine = range(NCH if first else dm.on_time)
    dm_load = local_copy(r.dm_in, r.dmS, r.loc.at[0])
    n_load = [local_copy(r.normed_in.at[:, pl.ds(k * q, q)], r.nS.at[:, pl.ds(k * q, q)], r.n_sem.at[k]) for k in range(nb)]
    w_load = local_copy(r.w_in, r.wS, r.loc.at[1])
    half = nb // 2
    order = [j + half * k for j in range(half) for k in range(2)]

    def fetch(k):
        rows, slot = pl.ds(order[k] * TR, TR), k % 2
        return [
            pltpu.make_async_copy(r.x_in.at[:, rows], r.xt.at[slot], r.tile_sem.at[slot, 0]),
            pltpu.make_async_copy(r.dtail_in.at[:, rows], r.dt.at[slot], r.tile_sem.at[slot, 1]),
            pltpu.make_async_copy(r.mu_in.at[rows], r.mt.at[slot], r.tile_sem.at[slot, 2]),
            pltpu.make_async_copy(r.rstd_in.at[rows], r.rt.at[slot], r.tile_sem.at[slot, 3]),
        ]

    def part(quarter, c):
        left = jnp.concatenate([r.dmS[fc, g, c * TR : (c + 1) * TR, :] for fc in range(nf) for g in range(3)], axis=1)
        right = jnp.concatenate([r.wS[fc, g, quarter] for fc in range(nf) for g in range(3)], axis=1)
        return lax.dot_general(left, right, (((1,), (1,)), ((), ())), preferred_element_type=F32)

    def to_sib(buf, got, c, i):
        return remote(buf.at[c], got.at[c], r.p_s.at[i, c], r.p_r.at[i, c], (n.sib, s))

    def to_across(c):
        return remote(r.pb.at[c], r.prb.at[c], r.p_s.at[1, c], r.p_r.at[1, c], (n.across, s))

    def sums_of(k, v, quarter, fresh=False):
        c = order[k]
        cols = pl.ds(at128(quarter * q), q)
        t1 = v * r.vec[base : base + 1, cols]
        t2 = v * r.nS[c * TR : (c + 1) * TR, cols].astype(F32)
        for j, t in enumerate((t1, t2)):
            total = t[:, :F]
            for fc in range(1, nf):
                total = total + t[:, fc * F : (fc + 1) * F]
            r.rows[j] = total if fresh else r.rows[j] + total

    def stage(k, between=None):
        c = order[k]
        v = part(n.diag, c)
        r.pa[c] = v.astype(BF16)
        to_sib(r.pa, r.pra, c, 0).start()
        sums_of(k, v, n.diag, True)
        v = part(b, c)
        r.acc[c * TR : (c + 1) * TR, :] = v
        sums_of(k, v, b)
        if between is not None:
            between()
        to_sib(r.pa, r.pra, c, 0).wait_send()
        v = part(n.sib, c)
        r.pa[c] = v.astype(BF16)
        to_sib(r.pa, r.prc, c, 2).start()
        sums_of(k, v, n.sib)
        v = part(n.across, c)
        sums_of(k, v, n.across)
        for i in range(PER):
            for j in range(2):
                r.st[b, k, j, i : i + 1, :] = jnp.sum(r.rows[j, i * F : (i + 1) * F, :].T, axis=0, keepdims=True)
        for p in n.batch_peers:
            stats_copy(k, p).start()
        arrived(r.pra.at[c], r.p_r.at[0, c], (n.sib, s))
        r.pb[c] = (v + r.pra[c].astype(F32)).astype(BF16)
        to_across(c).start()

    def wgrad(ch, begin=None):
        bb, h = ch // H, ch % H
        right = jnp.concatenate([r.dmS[fc, h] for fc in range(nf)], axis=1)
        r.wg[ch] = lax.dot_general(
            r.nS[:, bb * q : (bb + 1) * q], right, (((0,), (0,)), ((), ())), preferred_element_type=F32
        ).astype(BF16)
        if begin is not None:
            begin()
        if ch in mine:
            rs.start(ch)

    def mid(ch):
        if ch in mine:
            rs.mid(ch)

    def last(ch):
        if ch in mine:
            rs.last(ch)

    def gain(fc):
        return vrow(dm, r, n, base, fc)

    def stats_copy(k, p):
        return remote(r.st.at[b, k], r.st.at[b, k], r.st_s.at[k, p], r.st_r.at[k, b], (p, s))

    pend = []

    def final(k):
        c, slot = order[k], k % 2
        for p in n.batch_peers:
            arrived(r.st.at[p, k], r.st_r.at[k, p], (p, s))
        arrived(r.prc.at[c], r.p_r.at[2, c], (n.sib, s))
        arrived(r.prb.at[c], r.p_r.at[1, c], (n.across, s))
        for copy in fetch(k):
            copy.wait()
        if first:
            to_across(c).wait_send()

        def step(i, sums):
            near = pl.ds(pl.multiple_of(i * F, F), F)
            rows = pl.ds(pl.multiple_of(c * TR + i * F, F), F)
            mu, rstd = r.mt[slot, near, :], r.rt[slot, near, :]
            means = []
            for j in range(2):
                total = r.st[0, k, j, pl.ds(i, 1), :]
                for m in range(1, nb):
                    total = total + r.st[m, k, j, pl.ds(i, 1), :]
                means.append(jnp.broadcast_to(total * (1.0 / dm.d), (F, F)).T)
            new = []
            for fc in range(nf):
                cols = slice(fc * F, (fc + 1) * F)
                dn = r.acc[rows, cols] + r.prc[c, near, cols].astype(F32) + r.prb[c, near, cols].astype(F32)
                xhat = (r.xt[slot, fc, near, :] - mu) * rstd
                new.append(sums[fc] + jnp.sum((dn * xhat).reshape(F // 8, 8, F), axis=0))
                out = r.dt[slot, fc, near, :] + rstd * (dn * gain(fc) - means[0] - xhat * means[1])
                if first:
                    r.pb[c, near, cols] = out.astype(BF16)
                else:
                    r.acc[rows, cols] = out
            return tuple(new)

        sums = lax.fori_loop(0, PER, step, tuple(jnp.zeros((8, F), F32) for _ in range(nf)))
        for fc in range(nf):
            r.gsum[fc] = sums[fc] if k == 0 else r.gsum[fc] + sums[fc]
        if k + 2 < NT:
            for copy in fetch(k + 2):
                copy.start()
        if first:
            pl.when(b != c)(lambda: to_owner(c).start())
        else:
            rows = pl.ds(c * TR, TR)
            pend.append(local_copy(r.acc.at[rows], r.dx_out.at[rows], r.loc.at[3 + c]))

    def to_owner(c):
        return remote(r.pb.at[c], r.fin.at[b], r.g_s.at[c], r.g_r.at[b], (c, s))

    dm_load.wait()
    n_load[0].wait()
    wgrad(0, n.ready)
    wgrad(1)
    wgrad(2)
    r.need("vec")
    for c in n_load[1:] + [w_load]:
        c.wait()
    stage(0, lambda: mid(0))
    for k in range(2):
        for copy in fetch(k):
            copy.start()
    wgrad(3)
    stage(1, lambda: mid(1))
    wgrad(4)
    mid(2)
    stage(2)
    wgrad(5)
    stage(3, lambda: mid(3))
    wgrad(6)
    mid(4)
    for ch in range(3):
        last(ch)
    final(0)
    wgrad(7)
    mid(5)
    last(3)
    final(1)
    wgrad(8)
    last(4)
    mid(6)
    wgrad(9)
    last(5)
    mid(7)
    final(2)
    wgrad(10)
    last(6)
    mid(8)
    wgrad(11)
    last(7)
    final(3)
    mid(9)
    if not first:
        r.late[...] = r.wg[dm.on_time :]
        pend.append(local_copy(r.late, r.late_out, r.loc.at[0]))
    if first:
        vector_start(dm, r, n)
    else:
        r.store("gsum")
    last(8)
    mid(10)
    last(9)
    mid(11)
    last(10)
    if first:

        r.fin[b] = r.pb[b]
        for k in range(nb):

            @pl.when(k != b)
            def _(k=k):
                arrived(r.fin.at[k], r.g_r.at[k], (b, s))

            r.acc[k * TR : (k + 1) * TR, :] = r.fin[k].astype(F32)
            pend.append(local_copy(r.acc.at[pl.ds(k * TR, TR)], r.dx_out.at[:, pl.ds(k * q, q)], r.loc.at[3 + k]))
    if first:
        vector_finish(dm, r, n)
    last(11)
    if first:
        rs.assemble()
        r.store("wg_out")
    else:
        rs.receive(mine)
        pend.append(local_copy(r.fr, r.fr_out, r.loc.at[1]))
    for c in pend:
        c.wait()
    for k in range(NT):
        c = order[k]
        to_sib(r.pa, r.prc, c, 2).wait_send()
        if first:
            pl.when(b != c)(lambda c=c: to_owner(c).wait_send())
        else:
            to_across(c).wait_send()
        for p in n.batch_peers:
            stats_copy(k, p).wait_send()
    rs.drain(mine)


def vector_start(dm, r, n):
    r.need("vsum0", "vsum1", "gsum1")
    r.vg[n.s] = jnp.zeros((16, dm.q), F32)
    for l, (vs, gs) in enumerate(((r.vsum0, r.gsum), (r.vsum1, r.gsum1))):
        for fc in range(dm.nf):
            cols = slice(fc * F, (fc + 1) * F)
            r.vg[n.s, 5 * l : 5 * l + 1, cols] = jnp.sum(gs[fc], axis=0, keepdims=True)
            for k in range(4):
                r.vg[n.s, 5 * l + 1 + k : 5 * l + 2 + k, cols] = jnp.sum(vs[fc, k], axis=0, keepdims=True)
    for p in n.seq_peers:
        remote(r.vg.at[n.s], r.vg.at[n.s], r.v_s.at[p], r.v_r.at[n.s], (n.b, p)).start()


def vector_finish(dm, r, n):
    for p in n.seq_peers:
        arrived(r.vg.at[p], r.v_r.at[p], (n.b, p))
    total = r.vg[0]
    for j in range(1, dm.ns):
        total = total + r.vg[j]
    r.vg_out[...] = total
    r.store("vg_out")
    for p in n.seq_peers:
        sent(r.vg.at[n.s], r.v_s.at[p], (n.b, p))


def call_grads(dm, first, w, normed, x, mu, rstd, vec, scans, more):
    nb, ns, nf, R, q, tok = dm.nb, dm.ns, dm.nf, dm.rows, dm.q, dm.tok
    TR, H = tok // nb, 3
    NCH = nb * H
    late = NCH - dm.on_time
    ins = dict(
        dm_in=(scans.dmixed_out, HBM), w_in=(w, HBM), normed_in=(normed, HBM), x_in=(x, HBM),
        dtail_in=(scans.dtail_out, HBM), mu_in=(mu, HBM), rstd_in=(rstd, HBM), vec=(vec, INV),
    )
    bV = V((nb, TR, q), BF16)
    scratch = dict(
        dmS=V((nf, 3, tok, F), BF16), wS=V((nf, 3, nb, ns * R, F), BF16), nS=V((tok, dm.d), BF16),
        acc=V((tok, q), F32), pa=bV, pra=bV, pb=bV, prb=bV, prc=bV,
        wg=V((NCH, ns * R, q), BF16), fr=V((nb, H, R, q), BF16), **scatter_scratch(dm, NCH if first else dm.on_time),
        xt=V((2, nf, TR, F), F32), dt=V((2, nf, TR, F), F32), mt=V((2, TR, F), F32), rt=V((2, TR, F), F32),
        st=V((nb, nb, 2, TR // F, F), F32), rows=V((2, TR, F), F32),
        loc=DMA((3 + nb,)), n_sem=DMA((nb,)), tile_sem=DMA((2, 4)), p_s=DMA((3, nb)), p_r=DMA((3, nb)),
        st_s=DMA((nb, nb)), st_r=DMA((nb, nb)),
    )
    if first:
        outs = dict(wg_out=((R, 3 * dm.d), F32, INV), dx_out=((dm.local, dm.d), F32, HBM), vg_out=((16, q), F32, INV))
        ins.update({k: (v, INV) for k, v in more.items()})
        scratch.update(
            dict(fin=bV, g_s=DMA((nb,)), g_r=DMA((nb,)), vg=V((ns, 16, q), F32), v_s=DMA((ns,)), v_r=DMA((ns,)),
             gsum=V((nf, 8, F), F32))
        )
    else:
        outs = dict(
            dx_out=((tok, q), F32, HBM), gsum=((nf, 8, F), F32, INV), fr_out=((nb, H, R, q), BF16, HBM),
            late_out=((late, ns * R, q), BF16, HBM),
        )
        scratch["late"] = V((late, ns * R, q), BF16)
    return launch(dm, "grads_one" if first else "grads_two", 3 if first else 4, functools.partial(kernel_grads, first), ins, outs, scratch)


def prepare(dm, block_input, weight, vectors, cotangent):
    D, nf, nb, R = dm.d, dm.nf, dm.nb, dm.rows
    x, cot = [v.reshape(dm.runs, dm.length, D).swapaxes(0, 1).reshape(dm.local, D) for v in (block_input, cotangent)]
    s = lax.axis_index("seq")
    v = jnp.pad(vectors.reshape(dm.layers * 5, R), ((0, 16 - dm.layers * 5), (0, 0)))
    lane = lax.broadcasted_iota(jnp.int32, (16, F), 1) // R
    v = jnp.where(lane == lax.rem(s, F // R), jnp.tile(v, (1, F // R)), 0.0)
    return x, weight, v, cot


def natural(dm, v, shape):
    return v.reshape(dm.length, dm.runs, dm.d).swapaxes(0, 1).reshape(shape)


def tuned_body(nb, ns, block_input, weight, vectors, cotangent):
    dm = Dims(nb, ns, block_input.shape, weight.shape)
    x, w, vec, cot = prepare(dm, block_input, weight, vectors, cotangent)
    one = call_one(dm, x, w, vec)
    two = call_two(dm, one, cot)
    g1 = call_grads(dm, False, two.wq_out, two.normed_out, one.x1_out, two.mu_out, two.rstd_out, one.vec_out, two, {})
    three = call_three(dm, one, two, g1)
    more = dict(vsum0=three.vsum_out, vsum1=two.vsum_out, gsum1=g1.gsum)
    g0 = call_grads(dm, True, one.wq0_out, one.normed_out, one.xo_out, one.mu_out, one.rstd_out, one.vec_out, three, more)
    weight_grad = jnp.stack([g0.wg_out, three.wg_out], axis=0)
    s = lax.axis_index("seq")
    mine = lax.dynamic_slice_in_dim(g0.vg_out, s * dm.rows, dm.rows, axis=1)[: dm.layers * 5]
    vector_grad = mine.reshape(dm.layers, 5, dm.rows)
    return (
        natural(dm, three.block_out, block_input.shape), natural(dm, g0.dx_out, block_input.shape), weight_grad, vector_grad,
    )


def prefix(value, axis, join, neutral, backward):
    count, mine = (lax.axis_size(axis), lax.axis_index(axis))
    pieces = jax.tree.map(lambda part: lax.all_gather(part, axis), value)
    if backward:
        pieces = jax.tree.map(lambda part: part[::-1], pieces)
        mine = count - 1 - mine
    subtotal = jax.tree.map(
        lambda part, zero: jnp.full_like(part, 0) + jnp.asarray(zero, part.dtype), value, neutral
    )

    def step(position, subtotal):
        longer = join(subtotal, jax.tree.map(lambda part: part[position], pieces))
        return jax.tree.map(lambda new, old: jnp.where(position < mine, new, old), longer, subtotal)

    return lax.fori_loop(0, count - 1, step, subtotal)


def compose(earlier, later):
    return (later[0] * earlier[0], later[0] * earlier[1] + later[1])


def rebuild_forward(stream, full, vec):
    norm_scale, vforget, bforget = (vec[0], vec[1], vec[2])
    sequence_batch, time_steps, hidden_width = stream.shape
    center = jnp.mean(stream, axis=-1, keepdims=True)
    shifted_input = stream - center
    inverse_deviation = lax.rsqrt(
        jnp.mean(shifted_input * shifted_input, axis=-1, keepdims=True) + epsilon
    )
    centered_input = shifted_input * inverse_deviation
    normed_input = (
        (centered_input * norm_scale)
        .astype(jnp.bfloat16)
        .reshape(sequence_batch * time_steps, hidden_width)
    )
    mixed = jnp.dot(normed_input, full, preferred_element_type=jnp.float32).reshape(
        sequence_batch, time_steps, 3 * hidden_width
    )
    candidate_value = mixed[..., :hidden_width]
    reset_input = mixed[..., 2 * hidden_width :]
    forget_gate = jax.nn.sigmoid(
        mixed[..., hidden_width : 2 * hidden_width] + vforget * stream + bforget
    )
    gate_values, norm_bias = lax.associative_scan(
        compose, (forget_gate, (1.0 - forget_gate) * candidate_value), axis=1
    )
    return (
        centered_input,
        inverse_deviation,
        normed_input,
        candidate_value,
        reset_input,
        forget_gate,
        gate_values,
        norm_bias,
    )


def finish(vec, reset_input, gate_values, norm_bias, incoming):
    vreset, breset = (vec[3], vec[4])
    cells = gate_values * incoming[:, None, :] + norm_bias
    previous = jnp.concatenate([incoming[:, None, :], cells[:, :-1]], axis=1)
    reset = jax.nn.sigmoid(reset_input + vreset * previous + breset)
    return (cells, previous, reset)


def general_body(block_input, weight, vectors, cotangent):
    sequence_batch, time_steps, hidden_width = block_input.shape
    layers = weight.shape[0]
    params = lax.all_gather(vectors, ("batch", "seq"), axis=2, tiled=True)
    stream = block_input.astype(jnp.float32)
    ones = jnp.ones((sequence_batch, hidden_width), jnp.float32)
    zeros = jnp.zeros((sequence_batch, hidden_width), jnp.float32)
    inputs = []
    entering = []
    for layer in range(layers):
        full = lax.all_gather(weight[layer], ("batch", "seq"), axis=0, tiled=True)
        vec = params[layer]
        pieces = rebuild_forward(stream, full, vec)
        gate_values, norm_bias = (pieces[6], pieces[7])
        arrived = prefix(
            (gate_values[:, -1], norm_bias[:, -1]), "seq", compose, (ones, zeros), False
        )
        incoming = arrived[1]
        cells, previous, reset = finish(vec, pieces[4], gate_values, norm_bias, incoming)
        inputs.append(stream)
        entering.append(incoming)
        stream = reset * cells + (1.0 - reset) * stream
    block_output = stream.astype(jnp.bfloat16)
    grad_out = cotangent.astype(jnp.float32)
    weight_grads = [None] * layers
    vector_terms = [None] * layers
    rows = weight.shape[1]
    for layer in reversed(range(layers)):
        full = lax.all_gather(weight[layer], ("batch", "seq"), axis=0, tiled=True)
        vec = params[layer]
        norm_scale, vforget, vreset = (vec[0], vec[1], vec[3])
        stream = inputs[layer]
        (
            centered_input,
            inverse_deviation,
            normed_input,
            candidate_value,
            reset_input,
            forget_gate,
            gate_values,
            norm_bias,
        ) = rebuild_forward(stream, full, vec)
        cells, previous, reset = finish(vec, reset_input, gate_values, norm_bias, entering[layer])
        dreset = grad_out * (cells - stream) * reset * (1.0 - reset)
        direct = grad_out * reset
        inject = forget_gate * direct + dreset * vreset
        back_gates, back_offsets = lax.associative_scan(
            compose, (jnp.flip(forget_gate, 1), jnp.flip(inject, 1)), axis=1
        )
        back_gates = jnp.flip(back_gates, 1)
        back_offsets = jnp.flip(back_offsets, 1)
        arrived = prefix(
            (back_gates[:, 0], back_offsets[:, 0]), "seq", compose, (ones, zeros), True
        )
        later = arrived[1]
        carried = back_gates * later[:, None, :] + back_offsets
        following = jnp.concatenate([carried[:, 1:], later[:, None, :]], axis=1)
        dcell = direct + following
        dcandidate = dcell * (1.0 - forget_gate)
        dforget = dcell * (previous - candidate_value) * forget_gate * (1.0 - forget_gate)
        dmixed = jnp.concatenate([dcandidate, dforget, dreset], axis=-1).astype(jnp.bfloat16)
        dmixed = dmixed.reshape(sequence_batch * time_steps, 3 * hidden_width)

        def weight_term(start, count, normed_input=normed_input, dmixed=dmixed):
            return lax.dot_general(
                normed_input, dmixed, (((0,), (0,)), ((), ())), preferred_element_type=jnp.float32
            )

        weight_grads[layer] = lax.psum_scatter(
            weight_term(jnp.int32(0), rows * lax.axis_size(("batch", "seq"))),
            ("batch", "seq"),
            scatter_dimension=0,
            tiled=True,
        )
        normed_gradient = lax.dot_general(
            dmixed, full, (((1,), (1,)), ((), ())), preferred_element_type=jnp.float32
        )
        normed_gradient = normed_gradient.reshape(sequence_batch, time_steps, hidden_width)
        vector_terms[layer] = jnp.stack(
            [
                jnp.sum(normed_gradient * centered_input, axis=(0, 1)),
                jnp.sum(dforget * stream, axis=(0, 1)),
                jnp.sum(dforget, axis=(0, 1)),
                jnp.sum(dreset * previous, axis=(0, 1)),
                jnp.sum(dreset, axis=(0, 1)),
            ],
            axis=0,
        )
        centered_gradient = normed_gradient * norm_scale
        through_norm = inverse_deviation * (
            centered_gradient
            - jnp.mean(centered_gradient, axis=-1, keepdims=True)
            - centered_input * jnp.mean(centered_gradient * centered_input, axis=-1, keepdims=True)
        )
        grad_out = grad_out * (1.0 - reset) + dforget * vforget + through_norm
    weight_grad = jnp.stack(weight_grads, axis=0)
    vector_grad = lax.psum_scatter(
        jnp.stack(vector_terms, axis=0), ("batch", "seq"), scatter_dimension=2, tiled=True
    )
    return (block_output, grad_out, weight_grad, vector_grad)


def solution(mesh):
    nb, ns = mesh.shape["batch"], mesh.shape["seq"]
    body = functools.partial(tuned_body, nb, ns) if (nb, ns) == (4, 8) else general_body
    placed = (
        P("batch", "seq", None),
        P(None, ("batch", "seq"), None),
        P(None, None, ("batch", "seq")),
        P("batch", "seq", None),
    )
    return jax.shard_map(
        body,
        mesh=mesh,
        in_specs=placed,
        out_specs=(
            P("batch", "seq", None),
            P("batch", "seq", None),
            P(None, ("batch", "seq"), None),
            P(None, None, ("batch", "seq")),
        ),
        check_vma=False,
    )
```
